32 devices in a mesh: gx: 4 (over y, core), gy: 8 (over z, x).
Axes of the slice: x: 2, y: 2, z: 4, core: 2. Of those that a mesh axis runs over, the one named last changes fastest.
Arguments:
- coefficients: float32 [13, 56, 8192], P(None, None, ('gx', 'gy')), may hold values from -6 to 6
- jacobian: float32 [3, 3, 8192], P(None, None, ('gx', 'gy')), may hold values from -1 to 1
- face_normals: float32 [4, 3, 8192], P(None, None, ('gx', 'gy')), may hold values from -3 to 3
- wave_speed: float32 [8192], P(('gx', 'gy')), may hold values from 0.3 to 1.5
- star_mats: float32 [3, 13, 13], replicated, may hold values from -1.75 to 1.75
- deriv_mats: float32 [3, 56, 56], replicated, may hold values from -0.75 to 0.75
- stiff_mats: float32 [3, 56, 56], replicated, may hold values from -0.75 to 0.75
- source_mat: float32 [13, 13], replicated, may hold values from -4 to 4
- trace_mats: float32 [4, 21, 56], replicated, may hold values from -0.75 to 0.75
- lift_mats: float32 [4, 56, 21], replicated, may hold values from -1.25 to 1.25
- face_partner: int32 [4, 8192], P(None, ('gx', 'gy')), may hold values from -1 to 1535, as said below
- send_faces: int32 [8, 2048], P(None, ('gx', 'gy')), may hold values from 0 to 1023, as said below
- sea_face: int32 [8192], P(('gx', 'gy')), may hold values from 0 to 1023
- sea_row: int32 [8192, 1], P(('gx', 'gy')), may hold values from 0 to 7; in each aligned block of 256 rows (0 to 255, 256 to 511, ...) at most 64 rows name the same one
- sea_base: int32 [8192, 2], P(('gx', 'gy')), may hold values from 0 to 252
- interp_mat: float32 [16, 21], replicated, may hold values from -1.25 to 1.25
- water_depth: float32 [1024, 2048], P('gx', 'gy'), may hold values from 0.6 to 1.4
- momentum: float32 [2, 1024, 2048], P(None, 'gx', 'gy'), may hold values from -0.5 to 0.5
- bottom: float32 [1024, 2048], P('gx', 'gy'), may hold values from -0.3 to 0.3
Outputs:
- solid_final: float32 [13, 56, 8192], P(None, None, ('gx', 'gy'))
- ocean_final: float32 [3, 1024, 2048], P(None, 'gx', 'gy')
- bed_final: float32 [1024, 2048], P('gx', 'gy')
The draws below stay inside these ranges and needn't reach their ends.
Inputs may be any that keep to these rules, and one draw needn't show every extreme that they name: `face_partner`: for each face of a device's elements: -1 on the domain's outer boundary, a code below 1024 naming a face of the same device, or 1024 + k * 64 + s for the face paired with the neighbouring device at offset k in slot s. Pairings are symmetric; a device shares exactly 64 faces with each neighbour that exists on the device grid. `send_faces`: entry (k, s) of a device is the code f * 256 + e of its face paired in slot s with the neighbouring device at offset k; the 512 codes of a device are distinct. `sea_row`: among the rows of one device no tile row is named more than 64 times.
All inputs are finite; a program needn't handle non-finite values.
Results may differ from the reference program's by a relative error of at most 0.0001.
Values sent between devices are 32-bit elements; how exact they have to be, the bound alone decides.
No kernel may reach another device: no remote copies, remote signals or barrier semaphores. Data moves between devices by JAX's collectives and lax.ppermute only.
A program may use at most 64 MiB of HBM per device.

```python
import math
import jax
import jax.numpy as jnp
import numpy as np
from jax import lax

FIELDS = 13
BASIS = 56
FACE_BASIS = 21
POINTS = 16
ORD = 3
STEPS_DG = 2
STEPS_OCEAN = 2
CAP = 64
E_DEV = 256
SEA = 256
TILE_X = 256
TILE_Y = 256
S_FACE = 64
E_TOTAL = 8192
NX_OCEAN = 1024
NY_OCEAN = 2048
N_GX = 4
N_GY = 8
DEVICES = 32


offset_x = [-1, -1, -1, 0, 0, 1, 1, 1]


offset_y = [-1, 0, 1, -1, 1, -1, 0, 1]


def mesh_tables(key):
    face_count = 4 * E_DEV
    shift_x = jnp.array(offset_x, jnp.int32)
    shift_y = jnp.array(offset_y, jnp.int32)

    def one_device(device):
        subkey = jax.random.fold_in(key, device)
        rank_order = jax.random.permutation(subkey, face_count).astype(jnp.int32)
        anchor = jax.random.randint(jax.random.fold_in(subkey, 1), (), 0, 8 * S_FACE)
        rank_order = (rank_order + (face_count - 1 - rank_order[anchor])) % face_count
        places = jnp.arange(face_count, dtype=jnp.int32)
        direction = jnp.minimum(places // S_FACE, 7)
        grid_row = device // N_GY + shift_x[direction]
        grid_column = device % N_GY + shift_y[direction]
        inside = (grid_row >= 0) & (grid_row < N_GX) & (grid_column >= 0) & (grid_column < N_GY)
        paired = rank_order[jnp.bitwise_xor(places, 1)]
        values = jnp.where(places < 8 * S_FACE, jnp.where(inside, face_count + places, -1), paired)
        face_codes = jnp.zeros((face_count,), jnp.int32).at[rank_order].set(values)
        return (face_codes.reshape(4, E_DEV), rank_order[:8 * S_FACE].reshape(8, S_FACE))
    face_codes, send_lists = jax.vmap(one_device)(jnp.arange(DEVICES, dtype=jnp.int32))
    partner_table = face_codes.transpose(1, 0, 2).reshape(4, DEVICES * E_DEV)
    send_table = send_lists.transpose(1, 0, 2).reshape(8, DEVICES * S_FACE)
    return (partner_table, send_table)


def draw_face_partner(key, part):
    return mesh_tables(jax.random.fold_in(key, 7))[0]


def draw_send_faces(key, part):
    return mesh_tables(jax.random.fold_in(key, 7))[1]


def with_ends(entries, stream_key, smallest, largest):
    extent = entries.shape
    index_at = [jax.random.randint(jax.random.fold_in(stream_key, axis), (), 0, extent[axis]) for axis in range(len(extent))]
    entries = entries.at[tuple(index_at)].set(smallest)
    longest = extent.index(max(extent))
    index_at[longest] = (index_at[longest] + 1) % extent[longest]
    return entries.at[tuple(index_at)].set(largest)


def levels(own_key, extent, cuts, low, largest):
    level = 1.0
    for axis_at, blocks in cuts:
        draws = jax.random.uniform(jax.random.fold_in(jax.random.fold_in(own_key, 6), axis_at), (blocks,), jnp.float32, low / len(cuts), largest / len(cuts))
        level = level * jnp.repeat(jnp.exp(draws), extent[axis_at] // blocks).reshape((-1,) + (1,) * (len(extent) - 1 - axis_at))
    return level


def deal_out(rng, own, number, rows, count, top, limit, lean):
    ranking = jax.random.permutation(rng, count)
    crowded, usual = portions_of(count, rows * top, limit, lean, True), portions_of(count, rows * top, limit, lean, False)
    places = jnp.arange(count)

    def named(sizes, turn):
        used = int((sizes > 0).sum())
        fixed = max(1, used // 4)
        passed = fixed + (places - fixed + turn * (used - fixed)) % max(1, count - fixed)
        return jnp.zeros((count,), jnp.int32).at[ranking[jnp.where(places < fixed, places, passed)]].set(jnp.asarray(sizes, jnp.int32))

    sizes = jnp.where(number % 4 == 0, named(crowded, number // 4), named(usual, number - number // 4 - 1))
    mixed = jax.random.permutation(jax.random.fold_in(own, 3), count)
    donor, taker = mixed[0:count // 2 * 2:2], mixed[1:count // 2 * 2:2]
    slack = jnp.minimum(sizes[donor] - 1, limit - sizes[taker]) // 2
    slack = jnp.where((donor == ranking[0]) | (taker == ranking[0]) | (sizes[taker] == 0), 0, jnp.maximum(slack, 0))
    passed = jax.random.randint(jax.random.fold_in(own, 4), (count // 2,), 0, 1 << 20) % (slack + 1)
    sizes = sizes.at[donor].add(-passed).at[taker].add(passed)
    items = jnp.searchsorted(jnp.cumsum(sizes), jnp.arange(rows * top), side="right").astype(jnp.int32)
    table = items.reshape(top, rows).T
    table = table[jax.random.permutation(jax.random.fold_in(own, 1), rows)]
    turn = jax.random.randint(jax.random.fold_in(own, 2), (rows, 1), 0, top)
    return jnp.take_along_axis(table, (jnp.arange(top)[None, :] + turn) % top, axis=1)


def portions_of(count, total, limit, slope, full):
    loads = [(1 << 20) // math.isqrt(rank ** slope) + 1 for rank in range(1, count + 1)]
    largest = limit if full else min(limit, max(-(-total // count), total * loads[0] // sum(loads)))
    least = 1 if total - largest >= count - 1 else 0
    counts, rest = [largest] + [least] * (count - 1), total - largest - least * (count - 1)
    while rest > 0:
        movable = [i for i in range(1, count) if counts[i] < largest] or [i for i in range(1, count) if counts[i] < limit]
        pool, left = sum([loads[i] for i in movable]), rest
        for i in movable:
            extra = min(limit - counts[i], max(1, left * loads[i] // pool), rest)
            counts[i] = counts[i] + extra
            rest = rest - extra
    return np.array(counts)


def bell_draw(key, dims, scale, bound, split=(), kind=jnp.bfloat16):
    drawn = jax.random.normal(key, dims, jnp.float32) * scale
    if len(split) > 0:
        drawn = levels(key, dims, split, -0.22, 0.18) * drawn
    return jnp.clip(drawn, min=-bound, max=bound).astype(kind)


def setup_inputs(seed: int = 0) -> dict:
    keys = jax.random.split(jax.random.key(seed), 20)
    coefficients = bell_draw(keys[0], (FIELDS, BASIS, E_TOTAL), 1.0, 6.0, ((2, 32),), jnp.float32)
    jacobian = jnp.clip(jax.random.uniform(keys[1], (3, 3, E_TOTAL), jnp.float32, -1.0, 1.0) * levels(keys[1], (3, 3, E_TOTAL), ((2, 32),), -0.4, 0.0), -1.0, 1.0)
    face_normals = bell_draw(keys[2], (4, 3, E_TOTAL), 0.5, 3.0, ((2, 32),), jnp.float32)
    wave_speed = jnp.clip(jnp.exp(math.log(1.5) - 1.60943787 * jax.random.uniform(keys[3], (E_TOTAL,), jnp.float32) ** levels(keys[3], (E_TOTAL,), ((0, 32),), -0.2, 0.2)), 0.3, 1.5)
    star_mats = bell_draw(keys[4], (3, FIELDS, FIELDS), FIELDS ** -0.5, 1.75, (), jnp.float32)
    deriv_mats = bell_draw(keys[5], (3, BASIS, BASIS), BASIS ** -0.5, 0.75, (), jnp.float32)
    stiff_mats = bell_draw(keys[6], (3, BASIS, BASIS), BASIS ** -0.5, 0.75, (), jnp.float32)
    source_mat = bell_draw(keys[7], (FIELDS, FIELDS), 0.8, 4.0, (), jnp.float32)
    trace_mats = bell_draw(keys[8], (4, FACE_BASIS, BASIS), BASIS ** -0.5, 0.75, (), jnp.float32)
    lift_mats = bell_draw(keys[9], (4, BASIS, FACE_BASIS), FACE_BASIS ** -0.5, 1.25, (), jnp.float32)
    face_partner = draw_face_partner(jax.random.fold_in(keys[19], 71), 0)
    send_faces = draw_send_faces(jax.random.fold_in(keys[19], 71), 0)
    sea_face = with_ends(jax.random.randint(keys[12], (SEA * DEVICES,), 0, 4 * E_DEV), jax.random.fold_in(keys[12], 1), 0, (4 * E_DEV) - 1).astype(jnp.int32)
    sea_row_keys = jax.random.split(jax.random.fold_in(keys[13], 1), (SEA * DEVICES) // SEA)
    sea_row_turns = jax.random.permutation(jax.random.fold_in(keys[13], 3), (SEA * DEVICES) // SEA)
    sea_row = jax.vmap(lambda own, number: deal_out(jax.random.fold_in(keys[13], 2), own, number, SEA, N_GY, 1, CAP, 2))(sea_row_keys, sea_row_turns).reshape((SEA * DEVICES, 1))
    sea_base = with_ends(jax.random.randint(keys[14], (SEA * DEVICES, 2), 0, min(TILE_X, TILE_Y) - 3), jax.random.fold_in(keys[14], 1), 0, (min(TILE_X, TILE_Y) - 3) - 1).astype(jnp.int32)
    interp_mat = bell_draw(keys[15], (POINTS, FACE_BASIS), FACE_BASIS ** -0.5, 1.25, (), jnp.float32)
    water_depth = jnp.clip(0.6 + 0.79999995 * jax.random.uniform(keys[16], (NX_OCEAN, NY_OCEAN), jnp.float32) ** levels(keys[16], (NX_OCEAN, NY_OCEAN), ((0, 4), (1, 8)), -0.2, 0.2), 0.6, 1.4)
    momentum = bell_draw(keys[17], (2, NX_OCEAN, NY_OCEAN), 0.1, 0.5, ((1, 4), (2, 8)), jnp.float32)
    bottom = jnp.clip(jax.random.uniform(keys[18], (NX_OCEAN, NY_OCEAN), jnp.float32, -0.3, 0.3) * levels(keys[18], (NX_OCEAN, NY_OCEAN), ((0, 4), (1, 8)), -0.4, 0.0), -0.3, 0.3)
    return dict(coefficients=coefficients, jacobian=jacobian, face_normals=face_normals, wave_speed=wave_speed, star_mats=star_mats, deriv_mats=deriv_mats, stiff_mats=stiff_mats, source_mat=source_mat, trace_mats=trace_mats, lift_mats=lift_mats, face_partner=face_partner, send_faces=send_faces, sea_face=sea_face, sea_row=sea_row, sea_base=sea_base, interp_mat=interp_mat, water_depth=water_depth, momentum=momentum, bottom=bottom)


highest = lax.Precision.HIGHEST
step_solid = 0.4
step_ocean = 0.2
depth_floor = 0.5
vertical_field = 6
patch_side = 4
offset_x = [-1, -1, -1, 0, 0, 1, 1, 1]
offset_y = [-1, 0, 1, -1, 1, -1, 0, 1]

def derivative(coeffs, jacobian, star_mats, deriv_mats, source_mat):
    spatial = jnp.einsum('dlk,gke->dgle', deriv_mats, coeffs, precision=highest)
    combined = jnp.einsum('dce,dgle->cgle', jacobian, spatial, precision=highest)
    mixed = jnp.einsum('cgh,chle->gle', star_mats, combined, precision=highest)
    return -mixed - jnp.einsum('gh,hle->gle', source_mat, coeffs, precision=highest)

def volume_term(integral, jacobian, star_mats, stiff_mats):
    spatial = jnp.einsum('dlk,gke->dgle', stiff_mats, integral, precision=highest)
    combined = jnp.einsum('dce,dgle->cgle', jacobian, spatial, precision=highest)
    return jnp.einsum('cgh,chle->gle', star_mats, combined, precision=highest)

def time_integral(coeffs, jacobian, star_mats, deriv_mats, source_mat):
    integral = step_solid * coeffs
    current = coeffs
    factor = step_solid
    for order in range(1, ORD):
        current = derivative(current, jacobian, star_mats, deriv_mats, source_mat)
        factor = factor * step_solid / (order + 1)
        integral = integral + factor * current
    return integral

def face_traces(integral, trace_mats):
    return jnp.einsum('fml,gle->gmfe', trace_mats, integral, precision=highest)

def face_update(coeffs, integral, jacobian, normals, speed, inner, outer, star_mats, stiff_mats, lift_mats):
    sum_term = inner + outer
    jump_term = inner - outer
    rotated = jnp.einsum('cgh,hmfe->cgmfe', star_mats, sum_term, precision=highest)
    numeric_flux = 0.5 * jnp.einsum('fce,cgmfe->gmfe', normals, rotated, precision=highest) + 0.5 * speed * jump_term
    lifted = jnp.einsum('flm,gmfe->gle', lift_mats, numeric_flux, precision=highest)
    return coeffs + volume_term(integral, jacobian, star_mats, stiff_mats) - lifted

def partner_columns(face_partner, send_faces):
    devices = N_GX * N_GY
    elements_all = devices * E_DEV
    shift_x = jnp.array(offset_x, jnp.int32)
    shift_y = jnp.array(offset_y, jnp.int32)
    face_codes = face_partner.reshape(4, devices, E_DEV)
    device_ids = jnp.arange(devices, dtype=jnp.int32)[None, :, None]
    local_column = face_codes // E_DEV * elements_all + device_ids * E_DEV + face_codes % E_DEV
    relative = jnp.maximum(face_codes - 4 * E_DEV, 0)
    direction = jnp.minimum(relative // S_FACE, 7)
    slot_index = relative % S_FACE
    neighbour = (device_ids // N_GY + shift_x[direction]) * N_GY + device_ids % N_GY + shift_y[direction]
    neighbour = jnp.clip(neighbour, 0, devices - 1)
    send_lists = send_faces.reshape(8, devices, S_FACE)
    their_code = send_lists[7 - direction, neighbour, slot_index]
    remote_column = their_code // E_DEV * elements_all + neighbour * E_DEV + their_code % E_DEV
    columns = jnp.where(face_codes < 0, 4 * elements_all, jnp.where(face_codes < 4 * E_DEV, local_column, remote_column))
    return columns.transpose(1, 0, 2)

def solid_step(coeffs, jacobian, face_normals, wave_speed, columns, star_mats, deriv_mats, stiff_mats, source_mat, trace_mats, lift_mats):
    devices = N_GX * N_GY
    width = FIELDS * FACE_BASIS
    blocks = coeffs.reshape(FIELDS, BASIS, devices, E_DEV).transpose(2, 0, 1, 3)
    jac_blocks = jacobian.reshape(3, 3, devices, E_DEV).transpose(2, 0, 1, 3)
    normal_blocks = face_normals.reshape(4, 3, devices, E_DEV).transpose(2, 0, 1, 3)
    speed_blocks = wave_speed.reshape(devices, E_DEV)

    def integrate(pair):
        integral = time_integral(pair[0], pair[1], star_mats, deriv_mats, source_mat)
        return (integral, face_traces(integral, trace_mats))
    integrals, traces = lax.map(integrate, (blocks, jac_blocks))
    table = traces.transpose(1, 2, 3, 0, 4).reshape(width, 4 * devices * E_DEV)
    table = jnp.concatenate([table, jnp.zeros((width, 1), table.dtype)], axis=1)

    def update(pack):
        block, integral, jac_block, normal_block, speed_block, column_block, inner = pack
        outer = table[:, column_block.reshape(-1)].reshape(FIELDS, FACE_BASIS, 4, E_DEV)
        return face_update(block, integral, jac_block, normal_block, speed_block, inner, outer, star_mats, stiff_mats, lift_mats)
    new_blocks = lax.map(update, (blocks, integrals, jac_blocks, normal_blocks, speed_blocks, columns, traces))
    return new_blocks.transpose(1, 2, 0, 3).reshape(FIELDS, BASIS, devices * E_DEV)

def seafloor_forcing(coeffs, sea_face, sea_row, sea_base, trace_mats, interp_mat):
    devices = N_GX * N_GY
    elements_all = devices * E_DEV
    vertical = coeffs[vertical_field]
    sea_traces = jnp.einsum('fml,le->mfe', trace_mats, vertical, precision=highest).reshape(FACE_BASIS, 4 * elements_all)
    owner = jnp.arange(SEA * devices, dtype=jnp.int32) // SEA
    column = sea_face // E_DEV * elements_all + owner * E_DEV + sea_face % E_DEV
    rates = jnp.dot(interp_mat, sea_traces[:, column], precision=highest)
    points = jnp.arange(POINTS, dtype=jnp.int32)
    cell_x = (owner // N_GY * TILE_X + sea_base[:, 0])[None, :] + (points // patch_side)[:, None]
    cell_y = (sea_row[:, 0] * TILE_Y + sea_base[:, 1])[None, :] + (points % patch_side)[:, None]
    return jnp.zeros((TILE_X * N_GX, TILE_Y * N_GY), rates.dtype).at[cell_x, cell_y].add(rates)

def ocean_update(padded):
    height, mom_x, mom_y, bed = (padded[0], padded[1], padded[2], padded[3])
    safe = jnp.maximum(height, depth_floor)
    vel_x = mom_x / safe
    vel_y = mom_y / safe
    celerity = jnp.sqrt(safe)
    speed_x = jnp.abs(vel_x) + celerity
    speed_y = jnp.abs(vel_y) + celerity
    conserved = (height, mom_x, mom_y)
    flux_x = (mom_x, mom_x * vel_x + 0.5 * height * height, mom_y * vel_x)
    flux_y = (mom_y, mom_x * vel_y, mom_y * vel_y + 0.5 * height * height)
    wave_x = jnp.maximum(speed_x[:-1, 1:-1], speed_x[1:, 1:-1])
    wave_y = jnp.maximum(speed_y[1:-1, :-1], speed_y[1:-1, 1:])
    results = []
    for index in range(3):
        state_now = conserved[index]
        face_x = 0.5 * (flux_x[index][:-1, 1:-1] + flux_x[index][1:, 1:-1]) - 0.5 * wave_x * (state_now[1:, 1:-1] - state_now[:-1, 1:-1])
        face_y = 0.5 * (flux_y[index][1:-1, :-1] + flux_y[index][1:-1, 1:]) - 0.5 * wave_y * (state_now[1:-1, 1:] - state_now[1:-1, :-1])
        results.append(state_now[1:-1, 1:-1] - step_ocean * (face_x[1:] - face_x[:-1] + face_y[:, 1:] - face_y[:, :-1]))
    inner_height = height[1:-1, 1:-1]
    slope_x = 0.5 * (bed[2:, 1:-1] - bed[:-2, 1:-1])
    slope_y = 0.5 * (bed[1:-1, 2:] - bed[1:-1, :-2])
    return (results[0], results[1] - step_ocean * inner_height * slope_x, results[2] - step_ocean * inner_height * slope_y)

def reference(coefficients, jacobian, face_normals, wave_speed, star_mats, deriv_mats, stiff_mats, source_mat, trace_mats, lift_mats, face_partner, send_faces, sea_face, sea_row, sea_base, interp_mat, water_depth, momentum, bottom):
    columns = partner_columns(face_partner, send_faces)
    state = coefficients
    for section in range(STEPS_DG):
        state = solid_step(state, jacobian, face_normals, wave_speed, columns, star_mats, deriv_mats, stiff_mats, source_mat, trace_mats, lift_mats)
    forcing = seafloor_forcing(state, sea_face, sea_row, sea_base, trace_mats, interp_mat)
    height = water_depth
    mom_x = momentum[0]
    mom_y = momentum[1]
    bed = bottom
    for section in range(STEPS_OCEAN):
        bed = bed + step_ocean * forcing
        stacked = jnp.stack([height, mom_x, mom_y, bed])
        padded = jnp.pad(stacked, ((0, 0), (1, 1), (1, 1)))
        height, mom_x, mom_y = ocean_update(padded)
    return (state, jnp.stack([height, mom_x, mom_y]), bed)
```

```python
import functools

import jax
import jax.numpy as jnp
from jax import lax
from jax.experimental import pallas as pl
from jax.experimental.pallas import tpu as pltpu
from jax.sharding import PartitionSpec as P

FIELDS = 13
FACE_BASIS = 21
FACE_PAD = 24
POINTS = 16
ORD = 3
STEPS_OCEAN = 2
CAP = 64
TABLE = FIELDS * FACE_PAD
HALF = 160
WIDE = 2 * HALF
OCEAN_ROWS = 16
MARGIN = 16

step_solid = 0.4
step_ocean = 0.2
depth_floor = 0.5
vertical_field = 6
patch_side = 4

F32 = jnp.float32
BF16 = jnp.bfloat16
NT = (((1,), (1,)), ((), ()))
VMEM_LIMIT = 48 * 1024 * 1024


def iota(shape, dim):
    return lax.broadcasted_iota(jnp.int32, shape, dim)


def dot(a, b):
    return jnp.dot(a, b, preferred_element_type=F32)


def exact_dot(a, b):
    return jnp.dot(a, b, preferred_element_type=F32, precision=lax.Precision.HIGHEST)


def parts(x):
    high = x.astype(BF16)
    low = (x - high.astype(F32)).astype(BF16)
    return high, low


def both_parts(x):
    high = x.astype(BF16).astype(F32)
    return jnp.concatenate([high, x - high], axis=0).astype(BF16)


def folded(y):
    half = y.shape[0] // 2
    return y[:half] + y[half:]


def weights(w):
    return both_parts(w), w.astype(BF16)


def weighted(stack, high, x):
    x_high, x_low = parts(x)
    return folded(dot(stack, x_high)) + dot(high, x_low)


def selector(rows, columns, shift):
    return (iota((rows, columns), 1) == iota((rows, columns), 0) + shift).astype(F32)


def star_weights(mats):
    size = FIELDS * 8
    spread = ((iota((FIELDS, 2 * size), 1) % size) // 8 == iota((FIELDS, 2 * size), 0)).astype(F32)
    diagonal = iota((size, 2 * size), 0) % 8 == iota((size, 2 * size), 1) % 8
    first = iota((size, 2 * size), 1) < size
    high, low = [], []
    for mat in mats:
        wide = exact_dot(mat, spread)
        tall = jnp.concatenate(
            [jnp.broadcast_to(wide[g : g + 1], (8, 2 * size)) for g in range(FIELDS)], axis=0
        )
        tall = jnp.where(diagonal, tall, 0.0)
        top = tall.astype(BF16).astype(F32)
        high.append(top)
        low.append(jnp.where(first, tall - top, 0.0))
    return jnp.concatenate(high + low, axis=0).astype(BF16)


def side_by_side(mats):
    rows, columns = mats[0].shape
    total = len(mats) * columns
    return sum(exact_dot(m, selector(columns, total, i * columns)) for i, m in enumerate(mats))


def stacked_traces(trace_ref):
    basis = trace_ref.shape[2]
    place = (
        iota((FACE_PAD, FACE_BASIS), 0) == iota((FACE_PAD, FACE_BASIS), 1)
    ).astype(F32)
    return jnp.concatenate([exact_dot(place, trace_ref[f]) for f in range(4)], axis=0)


def spread_out(source, jac_ref, star, target, extra=None):
    basis = target.shape[1] // 3
    size = FIELDS * 8
    for j in range(basis // 8):
        x = jnp.concatenate(
            [source[g * basis + 8 * j : g * basis + 8 * j + 8, :] for g in range(FIELDS)], axis=0
        )
        y = folded(dot(star, both_parts(x)))
        for d in range(3):
            z = sum(jac_ref[d, c : c + 1, :] * y[c * size : (c + 1) * size] for c in range(3))
            for g in range(FIELDS):
                target[g, d * basis + 8 * j : d * basis + 8 * j + 8, :] = z[8 * g : 8 * g + 8]
        if extra is not None:
            for g in range(FIELDS):
                extra[g * basis + 8 * j : g * basis + 8 * j + 8, :] = y[
                    3 * size + 8 * g : 3 * size + 8 * g + 8
                ]


def derivative(source, target, jac_ref, star, basis_weights, spread_ref, relaxed_ref):
    basis = spread_ref.shape[1] // 3
    spread_out(source, jac_ref, star, spread_ref, relaxed_ref)
    for g in range(FIELDS):
        rows = slice(g * basis, (g + 1) * basis)
        target[rows, :] = -(weighted(*basis_weights, spread_ref[g]) + relaxed_ref[rows, :])


def unequal(place):
    a1 = jnp.where(place[0] % 2 == 0, 1, -1)
    c1 = jnp.where(place[1] % 2 == 0, 1, -1)
    return a1, c1


def column_block(a):
    return jnp.where(a > 0, 6, 1)


def row_block(c):
    return jnp.where(c > 0, 4, 3)


def front(
    place, q_ref, jac_ref, star_ref, source_ref, deriv_ref, trace_ref, send_ref,
    integral_ref, table_ref, p1_ref, p2_ref, q1_ref, q2_ref, spread_ref, relaxed_ref, d1_ref, d2_ref,
):
    basis = deriv_ref.shape[1]
    elements = q_ref.shape[1]
    star = star_weights([star_ref[0], star_ref[1], star_ref[2], source_ref[...]])
    basis_weights = weights(side_by_side([deriv_ref[d] for d in range(3)]))
    derivative(q_ref, d1_ref, jac_ref, star, basis_weights, spread_ref, relaxed_ref)
    derivative(d1_ref, d2_ref, jac_ref, star, basis_weights, spread_ref, relaxed_ref)
    first = step_solid
    second = first * step_solid / 2
    third = second * step_solid / 3
    trace = weights(stacked_traces(trace_ref))
    for g in range(FIELDS):
        rows = slice(g * basis, (g + 1) * basis)
        whole = first * q_ref[rows, :] + second * d1_ref[rows, :] + third * d2_ref[rows, :]
        integral_ref[rows, :] = whole
        faces = weighted(*trace, whole)
        for f in range(4):
            table_ref[g * FACE_PAD : (g + 1) * FACE_PAD, f * elements : (f + 1) * elements] = faces[
                f * FACE_PAD : (f + 1) * FACE_PAD
            ]
    a1, c1 = unequal(place)
    picks = [
        (p1_ref, 0, column_block(a1)),
        (p2_ref, 0, column_block(-a1)),
        (p1_ref, HALF, column_block(a1) + c1),
        (p1_ref, 2 * HALF, column_block(a1) - c1),
        (p2_ref, HALF, column_block(-a1) + c1),
        (p2_ref, 2 * HALF, column_block(-a1) - c1),
        (q1_ref, 0, row_block(c1)),
        (q2_ref, 0, row_block(-c1)),
    ]
    stack = table_parts(table_ref)
    left = iota((HALF, 2 * CAP), 1) < CAP
    codes = iota((4 * elements, 2 * CAP), 0)
    for n in range(0, 8, 2):
        wanted = jnp.concatenate(
            [send_ref[pl.ds(picks[n][2], 1), :], send_ref[pl.ds(picks[n + 1][2], 1), :]], axis=1
        )
        got = folded(dot(stack, (codes == wanted).astype(F32).astype(BF16)))
        low, high = got[:HALF], got[HALF:]
        ref, at, _ = picks[n]
        ref[at : at + HALF, :] = jnp.where(left, low, pltpu.roll(high, CAP, 1))
        ref, at, _ = picks[n + 1]
        ref[at : at + HALF, :] = jnp.where(left, pltpu.roll(low, CAP, 1), high)


def table_parts(table_ref):
    pad = jnp.zeros((WIDE - TABLE, table_ref.shape[1]), BF16)
    high, low = parts(table_ref[...])
    both = [high.astype(F32), pad.astype(F32), low.astype(F32), pad.astype(F32)]
    return jnp.concatenate(both, axis=0).astype(BF16)


def middle(
    q_ref, jac_ref, star_ref, stiff_ref, integral_ref, table_ref, partner_ref,
    base_ref, outer_ref, spread_ref,
):
    basis = stiff_ref.shape[1]
    elements = q_ref.shape[1]
    star = star_weights([star_ref[0], star_ref[1], star_ref[2]])
    basis_weights = weights(side_by_side([stiff_ref[d] for d in range(3)]))
    spread_out(integral_ref, jac_ref, star, spread_ref)
    for g in range(FIELDS):
        rows = slice(g * basis, (g + 1) * basis)
        base_ref[rows, :] = q_ref[rows, :] + weighted(*basis_weights, spread_ref[g])
    stack = table_parts(table_ref)
    codes = iota((4 * elements, elements), 0)
    for f in range(4):
        hot = (codes == partner_ref[f : f + 1, :]).astype(F32).astype(BF16)
        outer_ref[:, f * elements : (f + 1) * elements] = folded(dot(stack, hot))[:TABLE]


def back(
    place, base_ref, table_ref, outer_ref, partner_ref, normal_ref, speed_ref, star_ref, lift_ref,
    p1_ref, p2_ref, q1_ref, q2_ref, state_ref, flux_ref,
):
    basis = lift_ref.shape[1]
    elements = base_ref.shape[1]
    a1, c1 = unequal(place)
    blocks = [
        (p1_ref, 0, column_block(a1)),
        (p2_ref, 0, column_block(-a1)),
        (q1_ref, 0, row_block(c1)),
        (q1_ref, HALF, column_block(a1) + c1),
        (q1_ref, 2 * HALF, column_block(-a1) + c1),
        (q2_ref, 0, row_block(-c1)),
        (q2_ref, HALF, column_block(a1) - c1),
        (q2_ref, 2 * HALF, column_block(-a1) - c1),
    ]
    left = iota((HALF, 2 * CAP), 1) < CAP
    tops, bottoms = [], []
    for n in range(0, 8, 2):
        one = blocks[n][0][blocks[n][1] : blocks[n][1] + HALF, :]
        two = blocks[n + 1][0][blocks[n + 1][1] : blocks[n + 1][1] + HALF, :]
        tops.append(jnp.where(left, one, pltpu.roll(two, CAP, 1)))
        bottoms.append(jnp.where(left, pltpu.roll(one, CAP, 1), two))
    remote = jnp.concatenate(
        [jnp.concatenate(tops, axis=1), jnp.concatenate(bottoms, axis=1)], axis=0
    )
    remote = both_parts(remote)
    slot = iota((CAP, elements), 0)
    for f in range(4):
        wanted = partner_ref[f : f + 1, :] - 4 * elements
        hot = jnp.concatenate(
            [(slot + CAP * block[2] == wanted).astype(F32) for block in blocks], axis=0
        ).astype(BF16)
        columns = slice(f * elements, (f + 1) * elements)
        outer_ref[:, columns] += folded(dot(remote, hot))[:TABLE]
    star = star_weights([star_ref[0], star_ref[1], star_ref[2]])
    size = FIELDS * 8
    for part in range(FACE_PAD // 8):
        at = [slice(g * FACE_PAD + 8 * part, g * FACE_PAD + 8 * part + 8) for g in range(FIELDS)]
        for f in range(4):
            columns = slice(f * elements, (f + 1) * elements)
            inner = jnp.concatenate([table_ref[rows, columns] for rows in at], axis=0)
            outer = jnp.concatenate([outer_ref[rows, columns] for rows in at], axis=0)
            y = folded(dot(star, both_parts(inner + outer)))
            flux = 0.5 * speed_ref[...] * (inner - outer)
            for c in range(3):
                flux = flux + 0.5 * normal_ref[f, c : c + 1, :] * y[c * size : (c + 1) * size]
            for g in range(FIELDS):
                flux_ref[g, f * FACE_PAD + 8 * part : f * FACE_PAD + 8 * part + 8, :] = flux[
                    8 * g : 8 * g + 8
                ]
    place_lift = [
        exact_dot(lift_ref[f], selector(FACE_BASIS, 4 * FACE_PAD, f * FACE_PAD)) for f in range(4)
    ]
    lift = weights(sum(place_lift))
    for g in range(FIELDS):
        rows = slice(g * basis, (g + 1) * basis)
        state_ref[rows, :] = base_ref[rows, :] - weighted(*lift, flux_ref[g])


def rates_out(state_ref, trace_ref, interp_ref, sea_face_ref, sea_base_ref, sea_row_ref, out_ref):
    basis = trace_ref.shape[2]
    elements = state_ref.shape[1]
    faces = sea_face_ref.shape[1]
    tiles = out_ref.shape[0]
    vertical = state_ref[vertical_field * basis : (vertical_field + 1) * basis, :]
    sea = weighted(*weights(stacked_traces(trace_ref)), vertical)
    sea = jnp.concatenate([sea[f * FACE_PAD : (f + 1) * FACE_PAD] for f in range(4)], axis=1)
    hot = (iota((4 * elements, faces), 0) == sea_face_ref[...]).astype(F32).astype(BF16)
    coeffs = folded(dot(both_parts(sea), hot))[:FACE_BASIS]
    rates = exact_dot(interp_ref[...], coeffs)
    sent = both_parts(jnp.concatenate([rates, sea_base_ref[...]], axis=0))
    row = sea_row_ref[...]
    hits = (iota((faces, 128), 1) == row).astype(F32)
    before = (iota((faces, faces), 1) < iota((faces, faces), 0)).astype(F32)
    count = dot(before.astype(BF16), hits.astype(BF16))
    slot = jnp.sum(count * hits, axis=1, keepdims=True).astype(jnp.int32)
    lane = iota((faces, 2 * CAP), 1)
    mine = slot == lane % CAP
    left = iota((POINTS // 2, 2 * CAP), 1) < CAP
    left_1 = iota((1, 2 * CAP), 1) < CAP
    for j in range(tiles):
        edges = mine & (row == jnp.where(lane < CAP, j - 1, j + 1))
        inside = mine & (row == j)
        hot = jnp.concatenate([edges.astype(F32), inside.astype(F32)], axis=1).astype(BF16)
        got = folded(dot(sent, hot))
        near, own = got[:, : 2 * CAP], got[:, 2 * CAP :]
        out_ref[j, 0:POINTS, :] = near[:POINTS]
        out_ref[j, 16:24, :] = jnp.where(left, own[0:8], own[8:16])
        out_ref[j, 24:26, :] = near[POINTS : POINTS + 2]
        out_ref[j, 26:27, :] = jnp.where(left_1, own[16:17], own[17:18])
        out_ref[j, 27:32, :] = jnp.zeros((5, 2 * CAP), F32)


def forced(place, got_ref, forcing_ref, s1_ref, s2_ref):
    tiles = got_ref.shape[0]
    tile_x = forcing_ref.shape[0]
    tile_y = forcing_ref.shape[1] - 128
    left8 = iota((8, 2 * CAP), 1) < CAP
    left1 = iota((1, 2 * CAP), 1) < CAP
    tops, bottoms, xs, ys = [], [], [], []
    for s in range(0, tiles, 2):
        one, two = got_ref[s, 16:24, :], got_ref[s + 1, 16:24, :]
        tops.append(jnp.where(left8, one, pltpu.roll(two, CAP, 1)))
        bottoms.append(jnp.where(left8, pltpu.roll(one, CAP, 1), two))
        one, two = got_ref[s, 24:32, :], got_ref[s + 1, 24:32, :]
        xs.append(jnp.where(left8, one, pltpu.roll(two, CAP, 1))[2:3])
        ys.append(jnp.where(left8, pltpu.roll(one, CAP, 1), two)[2:3])
    lower, upper = jnp.concatenate(tops, axis=1), jnp.concatenate(bottoms, axis=1)
    x0, y0 = jnp.concatenate(xs, axis=1), jnp.concatenate(ys, axis=1)
    arrived = x0.shape[1]
    from_x = iota((tile_x, arrived), 0).astype(F32) - x0
    from_y = iota((tile_y, arrived), 0).astype(F32) - y0
    total = jnp.zeros((tile_x, tile_y), F32)
    for pr in range(patch_side):
        source = lower if pr < 2 else upper
        value = jnp.zeros((tile_y, arrived), F32)
        for pc in range(patch_side):
            at = (pr * patch_side + pc) % 8
            value = jnp.where(from_y == pc, source[at : at + 1], value)
        hot = (from_x == pr).astype(F32).astype(BF16)
        for value in parts(value):
            total += lax.dot_general(hot, value, NT, preferred_element_type=F32)
    forcing_ref[:, :tile_y] = total
    near = jnp.concatenate([got_ref[s, 0:POINTS, :] for s in range(tiles)], axis=1)
    x0 = jnp.concatenate([got_ref[s, 24:25, :] for s in range(tiles)], axis=1)
    y0 = jnp.concatenate([got_ref[s, 25:26, :] for s in range(tiles)], axis=1)
    arrived = x0.shape[1]
    from_x = iota((tile_x, arrived), 0).astype(F32) - x0
    rows = iota((8, arrived), 0)
    before = iota((8, arrived), 1) % (2 * CAP) < CAP
    high_y = jnp.where(before & (rows >= 6), (rows + (tile_y - 8)).astype(F32) - y0, -1.0)
    low_y = jnp.where(before | (rows >= 2), -1.0, rows.astype(F32) - y0)
    total = jnp.zeros((tile_x, 128), F32)
    blank = jnp.zeros((128 - 16, arrived), F32)
    for pr in range(patch_side):
        high, low = jnp.zeros((8, arrived), F32), jnp.zeros((8, arrived), F32)
        for pc in range(patch_side):
            at = pr * patch_side + pc
            high = jnp.where(high_y == pc, near[at : at + 1], high)
            low = jnp.where(low_y == pc, near[at : at + 1], low)
        hot = (from_x == pr).astype(F32).astype(BF16)
        for value in parts(jnp.concatenate([low, blank, high], axis=0)):
            total += lax.dot_general(hot, value, NT, preferred_element_type=F32)
    forcing_ref[:, tile_y:] = total
    a1, _ = unequal(place)
    head, tail = forcing_ref[0:8, :], forcing_ref[tile_x - 8 : tile_x, :]
    tail = pltpu.roll(tail, 2, 0)
    s1_ref[...] = jnp.where(a1 > 0, tail, head)
    s2_ref[...] = jnp.where(a1 > 0, head, tail)


def edges_out(place, depth_ref, momentum_ref, bottom_ref, p1_ref, p2_ref, q1_ref, q2_ref):
    arrays = [depth_ref[...], momentum_ref[0], momentum_ref[1], bottom_ref[...]]
    a1, c1 = unequal(place)
    tile_x, tile_y = depth_ref.shape
    row = iota((8, tile_y), 0)
    up = jnp.where(row < 2, row + (tile_y - 2), row - 2)
    down = jnp.where(row < 2, row, row + (tile_y - 4))
    wanted = jnp.where(c1 > 0, up, down)
    hot = ((row < 4) & (wanted == iota((8, tile_y), 1))).astype(F32)
    for i, array in enumerate(arrays):
        head, tail = array[0:2], array[tile_x - 2 : tile_x]
        one = jnp.where(a1 > 0, tail, head)
        two = jnp.where(a1 > 0, head, tail)
        columns = lax.dot_general(
            hot, array, NT, preferred_element_type=F32, precision=lax.Precision.HIGHEST
        )
        for h in range(2):
            at = slice(4 * i + 2 * h, 4 * i + 2 * h + 2)
            lanes = slice(128 * h, 128 * (h + 1))
            p1_ref[at, :] = one[:, lanes]
            p2_ref[at, :] = two[:, lanes]
            q1_ref[at, :] = columns[0:2, lanes]
            q2_ref[at, :] = columns[2:4, lanes]


def widened(place, depth_ref, momentum_ref, bottom_ref, p1_ref, p2_ref, q1_ref, q2_ref, out_ref):
    tile_x, tile_y = depth_ref.shape
    a1, c1 = unequal(place)
    arrays = [depth_ref[...], momentum_ref[0], momentum_ref[1], bottom_ref[...]]
    p1, p2, q1, q2 = p1_ref[...], p2_ref[...], q1_ref[...], q2_ref[...]
    below, above = jnp.where(a1 > 0, p2, p1), jnp.where(a1 > 0, p1, p2)
    before, after = jnp.where(c1 > 0, q2, q1), jnp.where(c1 > 0, q1, q2)
    n = OCEAN_ROWS

    def ends(rows):
        one, two = rows[n : 2 * n], rows[2 * n :]
        return jnp.where(a1 > 0, two, one), jnp.where(a1 > 0, one, two)

    before_below, before_above = ends(before)
    after_below, after_above = ends(after)
    lane = iota((2, 128), 1)
    low, high = lane < 2, lane >= 126
    for i, array in enumerate(arrays):
        first, second = slice(4 * i, 4 * i + 2), slice(4 * i + 2, 4 * i + 4)
        out_ref[i, 0:MARGIN, :] = jnp.zeros((MARGIN, tile_y + 128), F32)
        out_ref[i, MARGIN + tile_x :, :] = jnp.zeros((MARGIN, tile_y + 128), F32)
        out_ref[i, MARGIN : MARGIN + tile_x, :tile_y] = array
        for at, rows, left, right in (
            (MARGIN - 2, below, before_below, after_below),
            (MARGIN + tile_x, above, before_above, after_above),
        ):
            out_ref[i, at : at + 2, 0:128] = rows[first]
            out_ref[i, at : at + 2, 128:256] = rows[second]
            corner = jnp.where(low, right[first], jnp.where(high, left[second], 0.0))
            out_ref[i, at : at + 2, 256:384] = corner
        start = jnp.concatenate([after[first], after[second]], axis=1)
        finish = jnp.concatenate([before[first], before[second]], axis=1)
        columns = jnp.concatenate([start, jnp.zeros((124, tile_x), F32), finish], axis=0)
        out_ref[i, MARGIN : MARGIN + tile_x, tile_y:] = columns.T


def ocean(
    place, wide_ref, forcing_ref, s1_ref, s2_ref, out_ref, bed_ref, state, bed, cell,
):
    tile_x, tile_y = bed_ref.shape
    span = tile_y + 128
    a1, _ = unequal(place)
    below = jnp.where(a1 > 0, s2_ref[...], s1_ref[...])[0:2]
    above = jnp.where(a1 > 0, s1_ref[...], s2_ref[...])[0:2]
    force_lo = step_ocean * below
    force_hi = step_ocean * above
    height = tile_x + 2 * MARGIN
    strip = 16

    def next_of(x):
        return pltpu.roll(x, span - 1, 1)

    def previous_of(x):
        return pltpu.roll(x, 1, 1)

    bed[...] = wide_ref[3]
    bed[MARGIN : MARGIN + tile_x, :] += step_ocean * forcing_ref[...]
    bed[MARGIN - 2 : MARGIN, :] += force_lo
    bed[MARGIN + tile_x : MARGIN + tile_x + 2, :] += force_hi
    lane = iota((strip, span), 1)
    outside = ((lane == span - 1) & (place[1] == 0)) | (
        (lane == tile_y) & (place[1] == place[3] - 1)
    )

    def cells(read, at, rows):
        h, mx, my = (read(k, at, rows) for k in range(3))
        safe = jnp.maximum(h, depth_floor)
        u, v = mx / safe, my / safe
        c = jnp.sqrt(safe)
        half = 0.5 * h * h
        cell[0, at : at + rows, :] = mx * u + half
        cell[1, at : at + rows, :] = my * u
        cell[2, at : at + rows, :] = my * v + half
        cell[3, at : at + rows, :] = jnp.abs(u) + c
        cell[4, at : at + rows, :] = jnp.abs(v) + c

    def update(read, at, rows):
        here, up, down = slice(at, at + rows), slice(at + 1, at + rows + 1), slice(at - 1, at + rows - 1)

        def x_face(i, j):
            wave = 0.5 * jnp.maximum(cell[3, i, :], cell[3, j, :])
            u_i, u_j = [read(k, i) for k in range(3)], [read(k, j) for k in range(3)]
            f_i = (u_i[1], cell[0, i, :], cell[1, i, :])
            f_j = (u_j[1], cell[0, j, :], cell[1, j, :])
            return [0.5 * (f_i[k] + f_j[k]) - wave * (u_j[k] - u_i[k]) for k in range(3)]

        now = [read(k, here) for k in range(3)]
        flux = (now[2], cell[1, here, :], cell[2, here, :])
        speed = cell[4, here, :]
        wave = 0.5 * jnp.maximum(speed, next_of(speed))
        y_face = [
            0.5 * (flux[k] + next_of(flux[k])) - wave * (next_of(now[k]) - now[k]) for k in range(3)
        ]
        upper, lower = x_face(here, up), x_face(down, here)
        new = [
            now[k] - step_ocean * (upper[k] - lower[k] + y_face[k] - previous_of(y_face[k]))
            for k in range(3)
        ]
        b = bed[here, :]
        slope_x = 0.5 * (bed[up, :] - bed[down, :])
        slope_y = 0.5 * (next_of(b) - previous_of(b))
        new[1] = new[1] - step_ocean * now[0] * slope_x
        new[2] = new[2] - step_ocean * now[0] * slope_y
        return new

    for at in range(8, height - 8, 8):
        cells(lambda k, i, n: wide_ref[k, i : i + n, :], at, 8)
    for at in range(8, height - 8, strip):
        rows = min(strip, height - 8 - at)
        new = update(lambda k, i: wide_ref[k, i, :], at, rows)
        out = outside[:rows]
        row = iota((rows, span), 0) + at
        out = out | ((row < MARGIN) & (place[0] == 0))
        out = out | ((row >= MARGIN + tile_x) & (place[0] == place[2] - 1))
        for k in range(3):
            state[k, at : at + rows, :] = jnp.where(out, 0.0, new[k])
    for at in range(8, height - 8, 8):
        cells(lambda k, i, n: state[k, i : i + n, :], at, 8)
    bed[MARGIN : MARGIN + tile_x, :] += step_ocean * forcing_ref[...]
    bed[MARGIN - 2 : MARGIN, :] += force_lo
    bed[MARGIN + tile_x : MARGIN + tile_x + 2, :] += force_hi
    for at in range(MARGIN, MARGIN + tile_x, strip):
        new = update(lambda k, i: state[k, i, :], at, strip)
        for k in range(3):
            out_ref[k, at - MARGIN : at - MARGIN + strip, :] = new[k][:, :tile_y]
    bed_ref[...] = bed[MARGIN : MARGIN + tile_x, :tile_y]


def call(body, out_shape, *args, place=None, scratch=(), aliases=None):
    specs = [pl.BlockSpec(memory_space=pltpu.VMEM) for _ in args]
    if place is not None:
        specs = [pl.BlockSpec(memory_space=pltpu.SMEM)] + specs
        args = (place,) + args
    shapes = [jax.ShapeDtypeStruct(s, F32) for s in out_shape]
    return pl.pallas_call(
        body,
        out_shape=shapes,
        in_specs=specs,
        out_specs=[pl.BlockSpec(memory_space=pltpu.VMEM) for _ in shapes],
        scratch_shapes=[pltpu.VMEM(s, F32) for s in scratch],
        input_output_aliases=aliases or {},
        compiler_params=pltpu.CompilerParams(vmem_limit_bytes=VMEM_LIMIT),
    )(*args)


def swap(block, axis, parity):
    count = lax.axis_size(axis)
    pairs = []
    for i in range(parity, count - 1, 2):
        pairs += [(i, i + 1), (i + 1, i)]
    return lax.ppermute(block, axis, pairs)


def per_device(
    coefficients,
    jacobian,
    face_normals,
    wave_speed,
    star_mats,
    deriv_mats,
    stiff_mats,
    source_mat,
    trace_mats,
    lift_mats,
    face_partner,
    send_faces,
    sea_face,
    sea_row,
    sea_base,
    interp_mat,
    water_depth,
    momentum,
    bottom,
):
    basis, elements = coefficients.shape[1:]
    rows = FIELDS * basis
    tile_x, tile_y = water_depth.shape
    tiles = lax.axis_size("gy")
    place = jnp.stack(
        [lax.axis_index("gx"), lax.axis_index("gy"), lax.axis_size("gx"), tiles]
    ).astype(jnp.int32)
    speed = wave_speed.reshape(1, elements)
    spread = (FIELDS, 3 * basis, elements)
    faces = (TABLE, 4 * elements)
    buffer = (3 * HALF, 128)
    state = coefficients.reshape(rows, elements)
    edge_rows = call(
        edges_out, [(OCEAN_ROWS, 128)] * 4, water_depth, momentum, bottom, place=place
    )
    for section in range(2):
        integral, table, p1, p2, q1, q2 = call(
            front,
            [(rows, elements), faces, buffer, buffer, (HALF, 128), (HALF, 128)],
            state, jacobian, star_mats, source_mat, deriv_mats, trace_mats, send_faces,
            place=place,
            scratch=[spread, (rows, elements), (rows, elements), (rows, elements)],
        )
        own = (q1, q2)
        if section == 0:
            p1 = jnp.concatenate([p1, edge_rows[0]], axis=0)
            p2 = jnp.concatenate([p2, edge_rows[1]], axis=0)
        p1, p2 = swap(p1, "gx", 0), swap(p2, "gx", 1)
        base, outer = call(
            middle,
            [(rows, elements), faces],
            state, jacobian, star_mats, stiff_mats, integral, table, face_partner,
            scratch=[spread],
        )
        sent = []
        for n in range(2):
            at = slice((n + 1) * HALF, (n + 2) * HALF)
            pieces = [own[n], p1[at], p2[at]]
            if section == 0:
                pieces += [edge_rows[2 + n], p1[3 * HALF :], p2[3 * HALF :]]
            sent.append(jnp.concatenate(pieces, axis=0))
        q1, q2 = swap(sent[0], "gy", 0), swap(sent[1], "gy", 1)
        (state,) = call(
            back,
            [(rows, elements)],
            base, table, outer, face_partner, face_normals, speed, star_mats, lift_mats,
            p1, p2, q1, q2,
            place=place,
            scratch=[(FIELDS, 4 * FACE_PAD, elements)],
        )
        if section == 0:
            (wide,) = call(
                widened,
                [(4, tile_x + 2 * MARGIN, tile_y + 128)],
                water_depth, momentum, bottom,
                p1[3 * HALF :], p2[3 * HALF :], q1[3 * HALF :], q2[3 * HALF :],
                place=place,
            )
    corners = jnp.pad(sea_base.T.astype(F32), ((0, 6), (0, 0)))
    (outgoing,) = call(
        rates_out,
        [(tiles, 32, 128)],
        state, trace_mats, interp_mat, sea_face.reshape(1, -1), corners, sea_row,
    )
    incoming = lax.all_to_all(outgoing, "gy", split_axis=0, concat_axis=0, tiled=True)
    forcing, s1, s2 = call(
        forced,
        [(tile_x, tile_y + 128), (8, tile_y + 128), (8, tile_y + 128)],
        incoming,
        place=place,
    )
    s1, s2 = swap(s1, "gx", 0), swap(s2, "gx", 1)
    wide_shape = (tile_x + 2 * MARGIN, tile_y + 128)
    ocean_final, bed_final = call(
        ocean,
        [(3, tile_x, tile_y), (tile_x, tile_y)],
        wide, forcing, s1, s2,
        place=place,
        scratch=[(3,) + wide_shape, wide_shape, (5,) + wide_shape],
    )
    return (state.reshape(coefficients.shape), ocean_final, bed_final)


def solution(mesh):
    in_specs = (
        P(None, None, ("gx", "gy")),
        P(None, None, ("gx", "gy")),
        P(None, None, ("gx", "gy")),
        P(("gx", "gy")),
        P(),
        P(),
        P(),
        P(),
        P(),
        P(),
        P(None, ("gx", "gy")),
        P(None, ("gx", "gy")),
        P(("gx", "gy")),
        P(("gx", "gy"), None),
        P(("gx", "gy"), None),
        P(),
        P("gx", "gy"),
        P(None, "gx", "gy"),
        P("gx", "gy"),
    )
    out_specs = (P(None, None, ("gx", "gy")), P(None, "gx", "gy"), P("gx", "gy"))
    return jax.shard_map(
        per_device, mesh=mesh, in_specs=in_specs, out_specs=out_specs, check_vma=False
    )
```

```python
import jax
import jax.numpy as jnp
from jax import lax
from jax.experimental import pallas as pl
from jax.experimental.pallas import tpu as pltpu
from jax.sharding import PartitionSpec as P

FIELDS = 13
FACE_BASIS = 21
FACE_PAD = 24
POINTS = 16
ORD = 3
STEPS_OCEAN = 2
CAP = 64
TABLE = FIELDS * FACE_PAD
HALF = 160
WIDE = 2 * HALF
OCEAN_ROWS = 16
MARGIN = 16

step_solid = 0.4
step_ocean = 0.2
depth_floor = 0.5
vertical_field = 6
patch_side = 4

F32 = jnp.float32
BF16 = jnp.bfloat16
NT = (((1,), (1,)), ((), ()))
VMEM_LIMIT = 48 * 1024 * 1024
START_LIMIT = 62 * 1024 * 1024


def iota(shape, dim):
    return lax.broadcasted_iota(jnp.int32, shape, dim)


def dot(a, b):
    return jnp.dot(a, b, preferred_element_type=F32)


def exact_dot(a, b):
    return jnp.dot(a, b, preferred_element_type=F32, precision=lax.Precision.HIGHEST)


def parts(x):
    high = x.astype(BF16)
    low = (x - high.astype(F32)).astype(BF16)
    return high, low


def both_parts(x):
    high = x.astype(BF16).astype(F32)
    return jnp.concatenate([high, x - high], axis=0).astype(BF16)


def folded(y):
    half = y.shape[0] // 2
    return y[:half] + y[half:]


def weights(w):
    return both_parts(w), w.astype(BF16)


def weighted(stack, high, x):
    x_high, x_low = parts(x)
    return folded(dot(stack, x_high)) + dot(high, x_low)


def selector(rows, columns, shift):
    return (iota((rows, columns), 1) == iota((rows, columns), 0) + shift).astype(F32)


def star_weights(mats):
    size = FIELDS * 8
    spread = ((iota((FIELDS, 2 * size), 1) % size) // 8 == iota((FIELDS, 2 * size), 0)).astype(F32)
    diagonal = iota((size, 2 * size), 0) % 8 == iota((size, 2 * size), 1) % 8
    first = iota((size, 2 * size), 1) < size
    high, low = [], []
    for mat in mats:
        wide = exact_dot(mat, spread)
        tall = jnp.concatenate(
            [jnp.broadcast_to(wide[g : g + 1], (8, 2 * size)) for g in range(FIELDS)], axis=0
        )
        tall = jnp.where(diagonal, tall, 0.0)
        top = tall.astype(BF16).astype(F32)
        high.append(top)
        low.append(jnp.where(first, tall - top, 0.0))
    return jnp.concatenate(high + low, axis=0).astype(BF16)


def side_by_side(mats):
    rows, columns = mats[0].shape
    total = len(mats) * columns
    return sum(exact_dot(m, selector(columns, total, i * columns)) for i, m in enumerate(mats))


def stacked_traces(trace_ref):
    place = (
        iota((FACE_PAD, FACE_BASIS), 0) == iota((FACE_PAD, FACE_BASIS), 1)
    ).astype(F32)
    return jnp.concatenate([exact_dot(place, trace_ref[:, f, :]) for f in range(4)], axis=0)


def spread_out(source, jac_ref, star, target, extra=None):
    basis = target.shape[1] // 3
    size = FIELDS * 8
    for j in range(basis // 8):
        x = jnp.concatenate(
            [source[g * basis + 8 * j : g * basis + 8 * j + 8, :] for g in range(FIELDS)], axis=0
        )
        y = folded(dot(star, both_parts(x)))
        for d in range(3):
            z = sum(jac_ref[d, c : c + 1, :] * y[c * size : (c + 1) * size] for c in range(3))
            for g in range(FIELDS):
                target[g, d * basis + 8 * j : d * basis + 8 * j + 8, :] = z[8 * g : 8 * g + 8]
        if extra is not None:
            for g in range(FIELDS):
                extra[g * basis + 8 * j : g * basis + 8 * j + 8, :] = y[
                    3 * size + 8 * g : 3 * size + 8 * g + 8
                ]


def derivative(source, target, jac_ref, star, basis_weights, spread_ref, relaxed_ref):
    basis = spread_ref.shape[1] // 3
    spread_out(source, jac_ref, star, spread_ref, relaxed_ref)
    for g in range(FIELDS):
        rows = slice(g * basis, (g + 1) * basis)
        target[rows, :] = -(weighted(*basis_weights, spread_ref[g]) + relaxed_ref[rows, :])


def unequal(place):
    a1 = jnp.where(place[0] % 2 == 0, 1, -1)
    c1 = jnp.where(place[1] % 2 == 0, 1, -1)
    return a1, c1


def column_block(a):
    return jnp.where(a > 0, 6, 1)


def row_block(c):
    return jnp.where(c > 0, 4, 3)


def front(
    place, q_ref, jac_ref, star_ref, source_ref, deriv_ref, trace_ref, send_ref,
    integral_ref, table_ref, p1_ref, p2_ref, q1_ref, q2_ref, spread_ref, relaxed_ref, d1_ref, d2_ref,
):
    basis = deriv_ref.shape[1]
    elements = q_ref.shape[1]
    star = star_weights([star_ref[0], star_ref[1], star_ref[2], source_ref[...]])
    basis_weights = weights(side_by_side([deriv_ref[d] for d in range(3)]))
    derivative(q_ref, d1_ref, jac_ref, star, basis_weights, spread_ref, relaxed_ref)
    derivative(d1_ref, d2_ref, jac_ref, star, basis_weights, spread_ref, relaxed_ref)
    first = step_solid
    second = first * step_solid / 2
    third = second * step_solid / 3
    trace = weights(stacked_traces(trace_ref))
    for g in range(FIELDS):
        rows = slice(g * basis, (g + 1) * basis)
        whole = first * q_ref[rows, :] + second * d1_ref[rows, :] + third * d2_ref[rows, :]
        integral_ref[rows, :] = whole
        faces = weighted(*trace, whole)
        for f in range(4):
            table_ref[g * FACE_PAD : (g + 1) * FACE_PAD, f * elements : (f + 1) * elements] = faces[
                f * FACE_PAD : (f + 1) * FACE_PAD
            ]
    a1, c1 = unequal(place)
    picks = [
        (p1_ref, 0, column_block(a1)),
        (p2_ref, 0, column_block(-a1)),
        (p1_ref, HALF, column_block(a1) + c1),
        (p1_ref, 2 * HALF, column_block(a1) - c1),
        (p2_ref, HALF, column_block(-a1) + c1),
        (p2_ref, 2 * HALF, column_block(-a1) - c1),
        (q1_ref, 0, row_block(c1)),
        (q2_ref, 0, row_block(-c1)),
    ]
    stack = table_parts(table_ref)
    left = iota((HALF, 2 * CAP), 1) < CAP
    codes = iota((4 * elements, 2 * CAP), 0)
    for n in range(0, 8, 2):
        wanted = jnp.concatenate(
            [send_ref[pl.ds(picks[n][2], 1), :], send_ref[pl.ds(picks[n + 1][2], 1), :]], axis=1
        )
        got = folded(dot(stack, (codes == wanted).astype(F32).astype(BF16)))
        low, high = got[:HALF], got[HALF:]
        ref, at, _ = picks[n]
        ref[at : at + HALF, :] = jnp.where(left, low, pltpu.roll(high, CAP, 1))
        ref, at, _ = picks[n + 1]
        ref[at : at + HALF, :] = jnp.where(left, pltpu.roll(low, CAP, 1), high)


def start(place, *refs):
    sources, water, refs = refs[:7], refs[7:10], refs[10:]
    outs, refs = refs[:6], refs[6:]
    held, (sems, heads, tails, *scratch) = refs[:7], refs[7:]
    depth, momentum, bottom = water
    last = depth.shape[0] - 8
    pairs = [(sources[i], held[i]) for i in range(7)]
    for rows, target in ((pl.ds(0, 8), heads), (pl.ds(last, 8), tails)):
        pairs += [
            (depth.at[rows], target.at[0]),
            (momentum.at[0, rows], target.at[1]),
            (momentum.at[1, rows], target.at[2]),
            (bottom.at[rows], target.at[3]),
        ]
    copies = [pltpu.make_async_copy(a, b, sems.at[i]) for i, (a, b) in enumerate(pairs)]
    for copy in copies:
        copy.start()
    for copy in copies:
        copy.wait()
    edge_rows(place, heads, tails, *outs[2:4])
    front(place, *held, *outs, *scratch)


def table_parts(table_ref):
    pad = jnp.zeros((WIDE - TABLE, table_ref.shape[1]), BF16)
    high, low = parts(table_ref[...])
    both = [high.astype(F32), pad.astype(F32), low.astype(F32), pad.astype(F32)]
    return jnp.concatenate(both, axis=0).astype(BF16)


def volume(q_ref, jac_ref, star_ref, stiff_ref, integral_ref, base_ref, spread_ref):
    basis = stiff_ref.shape[1]
    star = star_weights([star_ref[0], star_ref[1], star_ref[2]])
    basis_weights = weights(side_by_side([stiff_ref[d] for d in range(3)]))
    spread_out(integral_ref, jac_ref, star, spread_ref)
    for g in range(FIELDS):
        rows = slice(g * basis, (g + 1) * basis)
        base_ref[rows, :] = q_ref[rows, :] + weighted(*basis_weights, spread_ref[g])


def forward(p1_ref, p2_ref, *refs):
    outs = refs[-2:]
    for n, out in enumerate(outs):
        at = slice((n + 1) * HALF, (n + 2) * HALF)
        out[0:HALF, :] = refs[n][...]
        out[HALF : 2 * HALF, :] = p1_ref[at, :]
        out[2 * HALF : 3 * HALF, :] = p2_ref[at, :]
        if len(refs) > 4:
            at = 3 * HALF
            for piece in (refs[2 + n][...], p1_ref[3 * HALF :, :], p2_ref[3 * HALF :, :]):
                out[at : at + OCEAN_ROWS, :] = piece
                at += OCEAN_ROWS


def local_faces(table_ref, partner_ref, outer_ref):
    elements = partner_ref.shape[1]
    stack = table_parts(table_ref)
    codes = iota((4 * elements, elements), 0)
    for f in range(4):
        hot = (codes == partner_ref[f : f + 1, :]).astype(F32).astype(BF16)
        outer_ref[:, f * elements : (f + 1) * elements] = folded(dot(stack, hot))[:TABLE]


def back(
    place, base_ref, table_ref, outer_ref, partner_ref, normal_ref, speed_ref, star_ref, lift_ref,
    p1_ref, p2_ref, q1_ref, q2_ref, state_ref, flux_ref,
):
    basis = lift_ref.shape[2]
    elements = base_ref.shape[1]
    a1, c1 = unequal(place)
    blocks = [
        (p1_ref, 0, column_block(a1)),
        (p2_ref, 0, column_block(-a1)),
        (q1_ref, 0, row_block(c1)),
        (q1_ref, HALF, column_block(a1) + c1),
        (q1_ref, 2 * HALF, column_block(-a1) + c1),
        (q2_ref, 0, row_block(-c1)),
        (q2_ref, HALF, column_block(a1) - c1),
        (q2_ref, 2 * HALF, column_block(-a1) - c1),
    ]
    left = iota((HALF, 2 * CAP), 1) < CAP
    tops, bottoms = [], []
    for n in range(0, 8, 2):
        one = blocks[n][0][blocks[n][1] : blocks[n][1] + HALF, :]
        two = blocks[n + 1][0][blocks[n + 1][1] : blocks[n + 1][1] + HALF, :]
        tops.append(jnp.where(left, one, pltpu.roll(two, CAP, 1)))
        bottoms.append(jnp.where(left, pltpu.roll(one, CAP, 1), two))
    remote = jnp.concatenate(
        [jnp.concatenate(tops, axis=1), jnp.concatenate(bottoms, axis=1)], axis=0
    )
    remote = both_parts(remote)
    slot = iota((CAP, elements), 0)
    for f in range(4):
        wanted = partner_ref[f : f + 1, :] - 4 * elements
        hot = jnp.concatenate(
            [(slot + CAP * block[2] == wanted).astype(F32) for block in blocks], axis=0
        ).astype(BF16)
        columns = slice(f * elements, (f + 1) * elements)
        outer_ref[:, columns] += folded(dot(remote, hot))[:TABLE]
    star = star_weights([star_ref[0], star_ref[1], star_ref[2]])
    size = FIELDS * 8
    for part in range(FACE_PAD // 8):
        at = [slice(g * FACE_PAD + 8 * part, g * FACE_PAD + 8 * part + 8) for g in range(FIELDS)]
        for f in range(4):
            columns = slice(f * elements, (f + 1) * elements)
            inner = jnp.concatenate([table_ref[rows, columns] for rows in at], axis=0)
            outer = jnp.concatenate([outer_ref[rows, columns] for rows in at], axis=0)
            y = folded(dot(star, both_parts(inner + outer)))
            flux = 0.5 * speed_ref[...] * (inner - outer)
            for c in range(3):
                flux = flux + 0.5 * normal_ref[c, f : f + 1, :] * y[c * size : (c + 1) * size]
            for g in range(FIELDS):
                flux_ref[g, f * FACE_PAD + 8 * part : f * FACE_PAD + 8 * part + 8, :] = flux[
                    8 * g : 8 * g + 8
                ]
    lift = weights(
        lax.dot_general(
            selector(basis, basis, 0),
            stacked_traces(lift_ref),
            NT,
            preferred_element_type=F32,
            precision=lax.Precision.HIGHEST,
        )
    )
    for g in range(FIELDS):
        rows = slice(g * basis, (g + 1) * basis)
        state_ref[rows, :] = base_ref[rows, :] - weighted(*lift, flux_ref[g])


def rates_out(state_ref, trace_ref, interp_ref, sea_face_ref, sea_base_ref, sea_row_ref, out_ref):
    basis = trace_ref.shape[2]
    elements = state_ref.shape[1]
    faces = sea_face_ref.shape[1]
    tiles = out_ref.shape[0]
    vertical = state_ref[vertical_field * basis : (vertical_field + 1) * basis, :]
    sea = weighted(*weights(stacked_traces(trace_ref)), vertical)
    sea = jnp.concatenate([sea[f * FACE_PAD : (f + 1) * FACE_PAD] for f in range(4)], axis=1)
    hot = (iota((4 * elements, faces), 0) == sea_face_ref[...]).astype(F32).astype(BF16)
    coeffs = folded(dot(both_parts(sea), hot))[:FACE_BASIS]
    rates = exact_dot(interp_ref[...], coeffs)
    corners = jnp.where(
        iota((8, faces), 0) == 0, sea_base_ref[0:1, :], sea_base_ref[1:2, :]
    ).astype(F32)
    sent = both_parts(jnp.concatenate([rates, corners], axis=0))
    row = sea_row_ref[...]
    hits = (iota((tiles, faces), 0) == row).astype(F32)
    before = (iota((faces, faces), 0) < iota((faces, faces), 1)).astype(F32)
    count = dot(hits.astype(BF16), before.astype(BF16))
    slot = jnp.sum(count * hits, axis=0, keepdims=True).astype(jnp.int32)
    lane = iota((2 * CAP, faces), 0)
    mine = slot == lane % CAP
    left = iota((POINTS // 2, 2 * CAP), 1) < CAP
    left_1 = iota((1, 2 * CAP), 1) < CAP
    for j in range(tiles):
        edges = mine & (row == jnp.where(lane < CAP, j - 1, j + 1))
        inside = mine & (row == j)
        hot = jnp.concatenate([edges.astype(F32), inside.astype(F32)], axis=0).astype(BF16)
        got = folded(lax.dot_general(sent, hot, NT, preferred_element_type=F32))
        near, own = got[:, : 2 * CAP], got[:, 2 * CAP :]
        out_ref[j, 0:POINTS, :] = near[:POINTS]
        out_ref[j, 16:24, :] = jnp.where(left, own[0:8], own[8:16])
        out_ref[j, 24:26, :] = near[POINTS : POINTS + 2]
        out_ref[j, 26:27, :] = jnp.where(left_1, own[16:17], own[17:18])
        out_ref[j, 27:32, :] = jnp.zeros((5, 2 * CAP), F32)


def finish(*refs):
    solid, sea, (state_ref, out_ref, flux_ref) = refs[:13], refs[13:18], refs[18:]
    back(*solid, state_ref, flux_ref)
    rates_out(state_ref, *sea, out_ref)


def forced(place, got_ref, forcing_ref, s1_ref, s2_ref):
    tiles = got_ref.shape[0]
    tile_x = forcing_ref.shape[0]
    tile_y = forcing_ref.shape[1] - 128
    left8 = iota((8, 2 * CAP), 1) < CAP
    left1 = iota((1, 2 * CAP), 1) < CAP
    tops, bottoms, xs, ys = [], [], [], []
    for s in range(0, tiles, 2):
        one, two = got_ref[s, 16:24, :], got_ref[s + 1, 16:24, :]
        tops.append(jnp.where(left8, one, pltpu.roll(two, CAP, 1)))
        bottoms.append(jnp.where(left8, pltpu.roll(one, CAP, 1), two))
        one, two = got_ref[s, 24:32, :], got_ref[s + 1, 24:32, :]
        xs.append(jnp.where(left8, one, pltpu.roll(two, CAP, 1))[2:3])
        ys.append(jnp.where(left8, pltpu.roll(one, CAP, 1), two)[2:3])
    lower, upper = jnp.concatenate(tops, axis=1), jnp.concatenate(bottoms, axis=1)
    x0, y0 = jnp.concatenate(xs, axis=1), jnp.concatenate(ys, axis=1)
    arrived = x0.shape[1]
    from_x = iota((tile_x, arrived), 0).astype(F32) - x0
    from_y = iota((tile_y, arrived), 0).astype(F32) - y0
    total = jnp.zeros((tile_x, tile_y), F32)
    for pr in range(patch_side):
        source = lower if pr < 2 else upper
        value = jnp.zeros((tile_y, arrived), F32)
        for pc in range(patch_side):
            at = (pr * patch_side + pc) % 8
            value = jnp.where(from_y == pc, source[at : at + 1], value)
        hot = (from_x == pr).astype(F32).astype(BF16)
        for value in parts(value):
            total += lax.dot_general(hot, value, NT, preferred_element_type=F32)
    forcing_ref[:, :tile_y] = total
    near = jnp.concatenate([got_ref[s, 0:POINTS, :] for s in range(tiles)], axis=1)
    x0 = jnp.concatenate([got_ref[s, 24:25, :] for s in range(tiles)], axis=1)
    y0 = jnp.concatenate([got_ref[s, 25:26, :] for s in range(tiles)], axis=1)
    arrived = x0.shape[1]
    from_x = iota((tile_x, arrived), 0).astype(F32) - x0
    rows = iota((8, arrived), 0)
    before = iota((8, arrived), 1) % (2 * CAP) < CAP
    high_y = jnp.where(before & (rows >= 6), (rows + (tile_y - 8)).astype(F32) - y0, -1.0)
    low_y = jnp.where(before | (rows >= 2), -1.0, rows.astype(F32) - y0)
    total = jnp.zeros((tile_x, 128), F32)
    blank = jnp.zeros((128 - 16, arrived), F32)
    for pr in range(patch_side):
        high, low = jnp.zeros((8, arrived), F32), jnp.zeros((8, arrived), F32)
        for pc in range(patch_side):
            at = pr * patch_side + pc
            high = jnp.where(high_y == pc, near[at : at + 1], high)
            low = jnp.where(low_y == pc, near[at : at + 1], low)
        hot = (from_x == pr).astype(F32).astype(BF16)
        for value in parts(jnp.concatenate([low, blank, high], axis=0)):
            total += lax.dot_general(hot, value, NT, preferred_element_type=F32)
    forcing_ref[:, tile_y:] = total
    a1, _ = unequal(place)
    head, tail = forcing_ref[0:8, :], forcing_ref[tile_x - 8 : tile_x, :]
    tail = pltpu.roll(tail, 2, 0)
    s1_ref[...] = jnp.where(a1 > 0, tail, head)
    s2_ref[...] = jnp.where(a1 > 0, head, tail)


def edge_rows(place, heads, tails, p1_ref, p2_ref):
    a1, _ = unequal(place)
    for i in range(4):
        head, tail = heads[i, 0:2, :], tails[i, 6:8, :]
        one = jnp.where(a1 > 0, tail, head)
        two = jnp.where(a1 > 0, head, tail)
        for h in range(2):
            at = slice(3 * HALF + 4 * i + 2 * h, 3 * HALF + 4 * i + 2 * h + 2)
            lanes = slice(128 * h, 128 * (h + 1))
            p1_ref[at, :] = one[:, lanes]
            p2_ref[at, :] = two[:, lanes]


def edge_columns(place, depth_ref, momentum_ref, bottom_ref, one_ref, two_ref):
    arrays = [depth_ref[...], momentum_ref[0], momentum_ref[1], bottom_ref[...]]
    _, c1 = unequal(place)
    tile_y = depth_ref.shape[1]
    row = iota((8, tile_y), 0)
    up = jnp.where(row < 2, row + (tile_y - 2), row - 2)
    down = jnp.where(row < 2, row, row + (tile_y - 4))
    wanted = jnp.where(c1 > 0, up, down)
    hot = ((row < 4) & (wanted == iota((8, tile_y), 1))).astype(F32)
    for i, array in enumerate(arrays):
        columns = lax.dot_general(
            hot, array, NT, preferred_element_type=F32, precision=lax.Precision.HIGHEST
        )
        for h in range(2):
            at = slice(4 * i + 2 * h, 4 * i + 2 * h + 2)
            lanes = slice(128 * h, 128 * (h + 1))
            one_ref[at, :] = columns[0:2, lanes]
            two_ref[at, :] = columns[2:4, lanes]


def volume_and_columns(place, *refs):
    solid, water, (base_ref, one_ref, two_ref, spread_ref) = refs[:5], refs[5:8], refs[8:]
    volume(*solid, base_ref, spread_ref)
    edge_columns(place, *water, one_ref, two_ref)


def widened(place, depth_ref, momentum_ref, bottom_ref, p1_ref, p2_ref, q1_ref, q2_ref, out_ref):
    tile_x, tile_y = depth_ref.shape
    a1, c1 = unequal(place)
    arrays = [depth_ref[...], momentum_ref[0], momentum_ref[1], bottom_ref[...]]
    at = 3 * HALF
    p1, p2, q1, q2 = p1_ref[at:, :], p2_ref[at:, :], q1_ref[at:, :], q2_ref[at:, :]
    below, above = jnp.where(a1 > 0, p2, p1), jnp.where(a1 > 0, p1, p2)
    before, after = jnp.where(c1 > 0, q2, q1), jnp.where(c1 > 0, q1, q2)
    n = OCEAN_ROWS

    def ends(rows):
        one, two = rows[n : 2 * n], rows[2 * n :]
        return jnp.where(a1 > 0, two, one), jnp.where(a1 > 0, one, two)

    before_below, before_above = ends(before)
    after_below, after_above = ends(after)
    lane = iota((2, 128), 1)
    low, high = lane < 2, lane >= 126
    for i, array in enumerate(arrays):
        first, second = slice(4 * i, 4 * i + 2), slice(4 * i + 2, 4 * i + 4)
        out_ref[i, 0:MARGIN, :] = jnp.zeros((MARGIN, tile_y + 128), F32)
        out_ref[i, MARGIN + tile_x :, :] = jnp.zeros((MARGIN, tile_y + 128), F32)
        out_ref[i, MARGIN : MARGIN + tile_x, :tile_y] = array
        for at, rows, left, right in (
            (MARGIN - 2, below, before_below, after_below),
            (MARGIN + tile_x, above, before_above, after_above),
        ):
            out_ref[i, at : at + 2, 0:128] = rows[first]
            out_ref[i, at : at + 2, 128:256] = rows[second]
            corner = jnp.where(low, right[first], jnp.where(high, left[second], 0.0))
            out_ref[i, at : at + 2, 256:384] = corner
        start = jnp.concatenate([after[first], after[second]], axis=1)
        finish = jnp.concatenate([before[first], before[second]], axis=1)
        columns = jnp.concatenate([start, jnp.zeros((124, tile_x), F32), finish], axis=0)
        out_ref[i, MARGIN : MARGIN + tile_x, tile_y:] = columns.T


STRIP = 16


def next_of(x):
    return pltpu.roll(x, x.shape[1] - 1, 1)


def previous_of(x):
    return pltpu.roll(x, 1, 1)


def cells(state, cell):
    for at in range(8, cell.shape[1] - 8, 8):
        here = slice(at, at + 8)
        h, mx, my = state[0, here, :], state[1, here, :], state[2, here, :]
        safe = jnp.maximum(h, depth_floor)
        root = lax.rsqrt(safe)
        inverse = root * root
        c = safe * root
        u, v = mx * inverse, my * inverse
        half = 0.5 * h * h
        cell[0, here, :] = mx * u + half
        cell[1, here, :] = my * u
        cell[2, here, :] = my * v + half
        cell[3, here, :] = 0.5 * (jnp.abs(u) + c)
        cell[4, here, :] = 0.5 * (jnp.abs(v) + c)


def moved(state, cell, at, rows):
    here, up, down = slice(at, at + rows), slice(at + 1, at + rows + 1), slice(at - 1, at + rows - 1)

    def x_face(i, j):
        wave = jnp.maximum(cell[3, i, :], cell[3, j, :])
        u_i, u_j = [state[k, i, :] for k in range(3)], [state[k, j, :] for k in range(3)]
        f_i = (u_i[1], cell[0, i, :], cell[1, i, :])
        f_j = (u_j[1], cell[0, j, :], cell[1, j, :])
        return [0.5 * (f_i[k] + f_j[k]) - wave * (u_j[k] - u_i[k]) for k in range(3)]

    now = [state[k, here, :] for k in range(3)]
    flux = (now[2], cell[1, here, :], cell[2, here, :])
    speed = cell[4, here, :]
    wave = jnp.maximum(speed, next_of(speed))
    y_face = [
        0.5 * (flux[k] + next_of(flux[k])) - wave * (next_of(now[k]) - now[k]) for k in range(3)
    ]
    upper, lower = x_face(here, up), x_face(down, here)
    return [
        now[k] - step_ocean * (upper[k] - lower[k] + y_face[k] - previous_of(y_face[k]))
        for k in range(3)
    ]


def sloped(height, bed, at, rows):
    b = bed[at : at + rows, :]
    slope_x = 0.5 * (bed[at + 1 : at + rows + 1, :] - bed[at - 1 : at + rows - 1, :])
    slope_y = 0.5 * (next_of(b) - previous_of(b))
    scale = step_ocean * height
    return scale * slope_x, scale * slope_y


def ocean_first(
    place, depth_ref, momentum_ref, bottom_ref, p1_ref, p2_ref, q1_ref, q2_ref, wide, state, cell
):
    tile_x, tile_y = depth_ref.shape
    widened(place, depth_ref, momentum_ref, bottom_ref, p1_ref, p2_ref, q1_ref, q2_ref, wide)
    cells(wide, cell)
    height, span = wide.shape[1:]
    lane = iota((STRIP, span), 1)
    outside = ((lane == span - 1) & (place[1] == 0)) | (
        (lane == tile_y) & (place[1] == place[3] - 1)
    )
    state[:, 0:8, :] = jnp.zeros((3, 8, span), F32)
    state[:, height - 8 :, :] = jnp.zeros((3, 8, span), F32)
    for at in range(8, height - 8, STRIP):
        new = moved(wide, cell, at, STRIP)
        row = iota((STRIP, span), 0) + at
        out = outside | ((row < MARGIN) & (place[0] == 0))
        out = out | ((row >= MARGIN + tile_x) & (place[0] == place[2] - 1))
        for k in range(3):
            state[k, at : at + STRIP, :] = jnp.where(out, 0.0, new[k])


def ocean_last(place, wide, first, forcing_ref, s1_ref, s2_ref, out_ref, bed_ref, state, bed, cell):
    tile_x, tile_y = bed_ref.shape
    height = wide.shape[1]
    a1, _ = unequal(place)
    force_lo = step_ocean * jnp.where(a1 > 0, s2_ref[...], s1_ref[...])[0:2]
    force_hi = step_ocean * jnp.where(a1 > 0, s1_ref[...], s2_ref[...])[0:2]
    inner = slice(MARGIN, MARGIN + tile_x)

    def raised(source):
        bed[inner, :] = source[inner, :] + step_ocean * forcing_ref[...]
        bed[MARGIN - 2 : MARGIN, :] = source[MARGIN - 2 : MARGIN, :] + force_lo
        above = slice(MARGIN + tile_x, MARGIN + tile_x + 2)
        bed[above, :] = source[above, :] + force_hi

    bed[0:MARGIN, :] = wide[3, 0:MARGIN, :]
    bed[MARGIN + tile_x :, :] = wide[3, MARGIN + tile_x :, :]
    raised(wide.at[3])
    for at in range(8, height - 8, STRIP):
        here = slice(at, at + STRIP)
        change_x, change_y = sloped(wide[0, here, :], bed, at, STRIP)
        state[0, here, :] = first[0, here, :]
        state[1, here, :] = first[1, here, :] - change_x
        state[2, here, :] = first[2, here, :] - change_y
    cells(state, cell)
    raised(bed)
    for at in range(MARGIN, MARGIN + tile_x, STRIP):
        new = moved(state, cell, at, STRIP)
        change_x, change_y = sloped(state[0, at : at + STRIP, :], bed, at, STRIP)
        new[1] -= change_x
        new[2] -= change_y
        for k in range(3):
            out_ref[k, at - MARGIN : at - MARGIN + STRIP, :] = new[k][:, :tile_y]
    bed_ref[...] = bed[inner, :tile_y]


def call(body, out_shape, *args, place=None, scratch=(), held=0, copies=0, limit=VMEM_LIMIT):
    space = pltpu.HBM if held else pltpu.VMEM
    specs = [pl.BlockSpec(memory_space=space) for _ in args]
    scratch = [pltpu.VMEM(s, F32) for s in scratch]
    if held:
        sems = pltpu.SemaphoreType.DMA((copies,))
        scratch = [pltpu.VMEM(x.shape, x.dtype) for x in args[:held]] + [sems] + scratch
    if place is not None:
        sizes, inner = place, body

        def body(*refs):
            here = (lax.axis_index("gx"), lax.axis_index("gy"))
            inner(here + sizes, *refs)

    shapes = [jax.ShapeDtypeStruct(s, F32) for s in out_shape]
    return pl.pallas_call(
        body,
        out_shape=shapes,
        in_specs=specs,
        out_specs=[pl.BlockSpec(memory_space=pltpu.VMEM) for _ in shapes],
        scratch_shapes=scratch,
        compiler_params=pltpu.CompilerParams(vmem_limit_bytes=limit),
    )(*args)


def swap(block, axis, parity):
    count = lax.axis_size(axis)
    pairs = []
    for i in range(parity, count - 1, 2):
        pairs += [(i, i + 1), (i + 1, i)]
    return lax.ppermute(block, axis, pairs)


def per_device(
    coefficients,
    jacobian,
    face_normals,
    wave_speed,
    star_mats,
    deriv_mats,
    stiff_mats,
    source_mat,
    trace_mats,
    lift_mats,
    face_partner,
    send_faces,
    sea_face,
    sea_row,
    sea_base,
    interp_mat,
    water_depth,
    momentum,
    bottom,
):
    basis, elements = coefficients.shape[1:]
    rows = FIELDS * basis
    tile_x, tile_y = water_depth.shape
    tiles = lax.axis_size("gy")
    place = (lax.axis_size("gx"), tiles)
    speed = wave_speed.reshape(1, elements)
    traces = trace_mats.transpose(1, 0, 2)
    normals = face_normals.transpose(1, 0, 2)
    lifts = lift_mats.transpose(2, 0, 1)
    spread = (FIELDS, 3 * basis, elements)
    faces = (TABLE, 4 * elements)
    solid = (rows, elements)
    wide_shape = (tile_x + 2 * MARGIN, tile_y + 128)
    state = coefficients.reshape(solid)
    for section in range(2):
        fixed = (state, jacobian, star_mats, source_mat, deriv_mats, traces, send_faces)
        scratch = [spread, solid, solid, solid]
        if section == 0:
            extra = OCEAN_ROWS
            buffers = [(3 * HALF + extra, 128)] * 2 + [(HALF, 128)] * 2
            integral, table, p1, p2, own1, own2 = call(
                start, [solid, faces] + buffers, *fixed, water_depth, momentum, bottom,
                place=place, scratch=[(4, 8, tile_y)] * 2 + scratch, held=len(fixed), copies=len(fixed) + 8,
                limit=START_LIMIT,
            )
        else:
            extra = 0
            buffers = [(3 * HALF, 128)] * 2 + [(HALF, 128)] * 2
            integral, table, p1, p2, own1, own2 = call(
                front, [solid, faces] + buffers, *fixed, place=place, scratch=scratch
            )
        p2, p1 = swap(p2, "gx", 1), swap(p1, "gx", 0)
        inside = (state, jacobian, star_mats, stiff_mats, integral)
        own = (own1, own2)
        if section == 0:
            base, *columns = call(
                volume_and_columns, [solid] + [(OCEAN_ROWS, 128)] * 2,
                *inside, water_depth, momentum, bottom,
                place=place, scratch=[spread],
            )
            own += tuple(columns)
        else:
            (base,) = call(volume, [solid], *inside, scratch=[spread])
        p1, p2, base = lax.optimization_barrier((p1, p2, base))
        q1, q2 = call(forward, [(3 * HALF + 3 * extra, 128)] * 2, p1, p2, *own)
        q2, q1 = swap(q2, "gy", 1), swap(q1, "gy", 0)
        (outer,) = call(local_faces, [faces], table, face_partner)
        if section == 1:
            wide, first = call(
                ocean_first,
                [(4,) + wide_shape, (3,) + wide_shape],
                water_depth, momentum, bottom, *halos,
                place=place, scratch=[(5,) + wide_shape],
            )
            q1, q2, outer, wide, first = lax.optimization_barrier((q1, q2, outer, wide, first))
        else:
            q1, q2, outer = lax.optimization_barrier((q1, q2, outer))
        last = (
            base, table, outer, face_partner, normals, speed, star_mats, lifts, p1, p2, q1, q2,
        )
        flux = [(FIELDS, 4 * FACE_PAD, elements)]
        if section == 0:
            (state,) = call(back, [solid], *last, place=place, scratch=flux)
            halos = (p1, p2, q1, q2)
        else:
            state, outgoing = call(
                finish,
                [solid, (tiles, 32, 128)],
                *last, traces, interp_mat, sea_face.reshape(1, -1), sea_base.T, sea_row.T,
                place=place, scratch=flux,
            )
    incoming = lax.all_to_all(outgoing, "gy", split_axis=0, concat_axis=0, tiled=True)
    forcing, s1, s2 = call(
        forced,
        [(tile_x, tile_y + 128), (8, tile_y + 128), (8, tile_y + 128)],
        incoming,
        place=place,
    )
    s2, s1 = swap(s2, "gx", 1), swap(s1, "gx", 0)
    ocean_final, bed_final = call(
        ocean_last,
        [(3, tile_x, tile_y), (tile_x, tile_y)],
        wide, first, forcing, s1, s2,
        place=place,
        scratch=[(3,) + wide_shape, wide_shape, (5,) + wide_shape],
    )
    return (state.reshape(coefficients.shape), ocean_final, bed_final)


def solution(mesh):
    in_specs = (
        P(None, None, ("gx", "gy")),
        P(None, None, ("gx", "gy")),
        P(None, None, ("gx", "gy")),
        P(("gx", "gy")),
        P(),
        P(),
        P(),
        P(),
        P(),
        P(),
        P(None, ("gx", "gy")),
        P(None, ("gx", "gy")),
        P(("gx", "gy")),
        P(("gx", "gy"), None),
        P(("gx", "gy"), None),
        P(),
        P("gx", "gy"),
        P(None, "gx", "gy"),
        P("gx", "gy"),
    )
    out_specs = (P(None, None, ("gx", "gy")), P(None, "gx", "gy"), P("gx", "gy"))
    return jax.shard_map(
        per_device, mesh=mesh, in_specs=in_specs, out_specs=out_specs, check_vma=False
    )
```

```python
import jax
import jax.numpy as jnp
from jax import lax
from jax.experimental import pallas as pl
from jax.experimental.pallas import tpu as pltpu
from jax.sharding import PartitionSpec as P

FIELDS = 13
FACE_BASIS = 21
FACE_PAD = 24
POINTS = 16
ORD = 3
STEPS_OCEAN = 2
CAP = 64
TABLE = FIELDS * FACE_PAD
WIDE = 320
HALF = 144
OCEAN_ROWS = 16
MARGIN = 16

step_solid = 0.4
step_ocean = 0.2
depth_floor = 0.5
vertical_field = 6
patch_side = 4

F32 = jnp.float32
BF16 = jnp.bfloat16
NT = (((1,), (1,)), ((), ()))
VMEM_LIMIT = 48 * 1024 * 1024
START_LIMIT = 62 * 1024 * 1024


def iota(shape, dim):
    return lax.broadcasted_iota(jnp.int32, shape, dim)


def dot(a, b):
    return jnp.dot(a, b, preferred_element_type=F32)


def exact_dot(a, b):
    return jnp.dot(a, b, preferred_element_type=F32, precision=lax.Precision.HIGHEST)


def parts(x):
    high = x.astype(BF16)
    low = (x - high.astype(F32)).astype(BF16)
    return high, low


def both_parts(x):
    high = x.astype(BF16).astype(F32)
    return jnp.concatenate([high, x - high], axis=0).astype(BF16)


def folded(y):
    half = y.shape[0] // 2
    return y[:half] + y[half:]


def weights(w):
    return both_parts(w), w.astype(BF16)


def weighted(stack, high, x):
    x_high, x_low = parts(x)
    return folded(dot(stack, x_high)) + dot(high, x_low)


def selector(rows, columns, shift):
    return (iota((rows, columns), 1) == iota((rows, columns), 0) + shift).astype(F32)


def star_weights(mats):
    size = FIELDS * 8
    spread = ((iota((FIELDS, 2 * size), 1) % size) // 8 == iota((FIELDS, 2 * size), 0)).astype(F32)
    diagonal = iota((size, 2 * size), 0) % 8 == iota((size, 2 * size), 1) % 8
    first = iota((size, 2 * size), 1) < size
    high, low = [], []
    for mat in mats:
        wide = exact_dot(mat, spread)
        tall = jnp.concatenate(
            [jnp.broadcast_to(wide[g : g + 1], (8, 2 * size)) for g in range(FIELDS)], axis=0
        )
        tall = jnp.where(diagonal, tall, 0.0)
        top = tall.astype(BF16).astype(F32)
        high.append(top)
        low.append(jnp.where(first, tall - top, 0.0))
    return jnp.concatenate(high + low, axis=0).astype(BF16)


def side_by_side(mats):
    rows, columns = mats[0].shape
    total = len(mats) * columns
    return sum(exact_dot(m, selector(columns, total, i * columns)) for i, m in enumerate(mats))


def stacked_traces(trace_ref):
    place = (
        iota((FACE_PAD, FACE_BASIS), 0) == iota((FACE_PAD, FACE_BASIS), 1)
    ).astype(F32)
    return jnp.concatenate([exact_dot(place, trace_ref[:, f, :]) for f in range(4)], axis=0)


def spread_out(source, jac_ref, star, target, extra=None):
    basis = target.shape[1] // 3
    size = FIELDS * 8
    for j in range(basis // 8):
        x = jnp.concatenate(
            [source[g * basis + 8 * j : g * basis + 8 * j + 8, :] for g in range(FIELDS)], axis=0
        )
        y = folded(dot(star, both_parts(x)))
        for d in range(3):
            z = sum(jac_ref[d, c : c + 1, :] * y[c * size : (c + 1) * size] for c in range(3))
            for g in range(FIELDS):
                target[g, d * basis + 8 * j : d * basis + 8 * j + 8, :] = z[8 * g : 8 * g + 8]
        if extra is not None:
            for g in range(FIELDS):
                extra[g * basis + 8 * j : g * basis + 8 * j + 8, :] = y[
                    3 * size + 8 * g : 3 * size + 8 * g + 8
                ]


def derivative(source, target, jac_ref, star, basis_weights, spread_ref, relaxed_ref):
    basis = spread_ref.shape[1] // 3
    spread_out(source, jac_ref, star, spread_ref, relaxed_ref)
    for g in range(FIELDS):
        rows = slice(g * basis, (g + 1) * basis)
        target[rows, :] = -(weighted(*basis_weights, spread_ref[g]) + relaxed_ref[rows, :])


def unequal(place):
    a1 = jnp.where(place[0] % 2 == 0, 1, -1)
    c1 = jnp.where(place[1] % 2 == 0, 1, -1)
    return a1, c1


def column_block(a):
    return jnp.where(a > 0, 6, 1)


def row_block(c):
    return jnp.where(c > 0, 4, 3)


def front(
    place, q_ref, jac_ref, star_ref, source_ref, deriv_ref, trace_ref, send_ref,
    integral_ref, table_ref, p1_ref, p2_ref, own1_ref, own2_ref,
    spread_ref, relaxed_ref, d1_ref, d2_ref, packed_ref, ready=lambda *numbers: None, made=lambda *numbers: None,
):
    elements = q_ref.shape[1]
    ready(2, 3)
    star = star_weights([star_ref[0], star_ref[1], star_ref[2], source_ref[...]])
    ready(4, 5)
    basis = deriv_ref.shape[1]
    basis_weights = weights(side_by_side([deriv_ref[d] for d in range(3)]))
    trace = weights(stacked_traces(trace_ref))
    ready(0, 1)
    derivative(q_ref, d1_ref, jac_ref, star, basis_weights, spread_ref, relaxed_ref)
    derivative(d1_ref, d2_ref, jac_ref, star, basis_weights, spread_ref, relaxed_ref)
    first = step_solid
    second = first * step_solid / 2
    third = second * step_solid / 3
    for g in range(FIELDS):
        rows = slice(g * basis, (g + 1) * basis)
        whole = first * q_ref[rows, :] + second * d1_ref[rows, :] + third * d2_ref[rows, :]
        integral_ref[rows, :] = whole
        faces = weighted(*trace, whole)
        for f in range(4):
            table_ref[g * FACE_PAD : (g + 1) * FACE_PAD, f * elements : (f + 1) * elements] = faces[
                f * FACE_PAD : (f + 1) * FACE_PAD
            ]
    made(0, 1)
    ready(6)
    a1, c1 = unequal(place)
    picks = [
        (p1_ref, 0, column_block(a1)),
        (p2_ref, 0, column_block(-a1)),
        (p1_ref, HALF, column_block(a1) + c1),
        (p1_ref, 2 * HALF, column_block(a1) - c1),
        (p2_ref, HALF, column_block(-a1) + c1),
        (p2_ref, 2 * HALF, column_block(-a1) - c1),
        (own1_ref, 0, row_block(c1)),
        (own2_ref, 0, row_block(-c1)),
    ]
    stack = table_parts(table_ref)
    left = iota((HALF, 2 * CAP), 1) < CAP
    codes = iota((4 * elements, 4 * CAP), 0)
    packed_ref[FIELDS * FACE_BASIS :, :] = jnp.zeros((2 * HALF - FIELDS * FACE_BASIS, 4 * CAP), F32)
    for n in range(0, 8, 4):
        wanted = jnp.concatenate([send_ref[pl.ds(pick[2], 1), :] for pick in picks[n : n + 4]], axis=1)
        got = folded(dot(stack, (codes == wanted).astype(F32).astype(BF16)))
        pack(got, packed_ref)
        for pair in range(2):
            lanes = slice(pair * 2 * CAP, (pair + 1) * 2 * CAP)
            low, high = packed_ref[0:HALF, lanes], packed_ref[HALF:, lanes]
            ref, at, _ = picks[n + 2 * pair]
            ref[at : at + HALF, :] = jnp.where(left, low, pltpu.roll(high, CAP, 1))
            ref, at, _ = picks[n + 2 * pair + 1]
            ref[at : at + HALF, :] = jnp.where(left, pltpu.roll(low, CAP, 1), high)


def pack(table, packed_ref):
    rest = FACE_BASIS - 16
    for g in range(FIELDS):
        packed_ref[16 * g : 16 * (g + 1), :] = table[FACE_PAD * g : FACE_PAD * g + 16]
        at = 16 * FIELDS + rest * g
        packed_ref[at : at + rest, :] = table[FACE_PAD * g + 16 : FACE_PAD * g + FACE_BASIS]


def unpack(packed_ref, table_ref):
    rest = FACE_BASIS - 16
    for g in range(FIELDS):
        table_ref[FACE_PAD * g : FACE_PAD * g + 16, :] = packed_ref[16 * g : 16 * (g + 1), :]
        at = 16 * FIELDS + rest * g
        last = FACE_PAD * g + 16
        table_ref[last : last + 8, :] = jnp.zeros((8, table_ref.shape[1]), F32)
        table_ref[last : last + rest, :] = packed_ref[at : at + rest, :]


def start(place, *refs):
    sources, water, refs = refs[:7], refs[7:10], refs[10:]
    targets, refs = refs[:6], refs[6:]
    held, (sems, heads, tails), refs = refs[:7], refs[7:10], refs[10:]
    outs, scratch = refs[:6], refs[6:]
    depth, momentum, bottom = water
    last = depth.shape[0] - 8
    pairs = [(sources[i], held[i]) for i in range(7)]
    for rows, target in ((pl.ds(0, 8), heads), (pl.ds(last, 8), tails)):
        pairs += [
            (depth.at[rows], target.at[0]),
            (momentum.at[0, rows], target.at[1]),
            (momentum.at[1, rows], target.at[2]),
            (bottom.at[rows], target.at[3]),
        ]
    first_out = len(pairs)
    pairs += list(zip(outs, targets))
    copies = [pltpu.make_async_copy(a, b, sems.at[i]) for i, (a, b) in enumerate(pairs)]
    for copy in copies[:first_out]:
        copy.start()

    def ready(*numbers):
        for i in numbers:
            copies[i].wait()

    def made(*numbers):
        for i in numbers:
            copies[first_out + i].start()

    front(place, *held, *outs, *scratch, ready=ready, made=made)
    ready(*range(7, first_out))
    edge_rows(place, heads, tails, *outs[2:4])
    made(2, 3, 4, 5)
    ready(*range(first_out, len(copies)))


def table_parts(table_ref):
    pad = jnp.zeros((WIDE - TABLE, table_ref.shape[1]), BF16)
    high, low = parts(table_ref[...])
    both = [high.astype(F32), pad.astype(F32), low.astype(F32), pad.astype(F32)]
    return jnp.concatenate(both, axis=0).astype(BF16)


def volume(q_ref, jac_ref, star_ref, stiff_ref, integral_ref, base_ref, spread_ref):
    basis = stiff_ref.shape[1]
    star = star_weights([star_ref[0], star_ref[1], star_ref[2]])
    basis_weights = weights(side_by_side([stiff_ref[d] for d in range(3)]))
    spread_out(integral_ref, jac_ref, star, spread_ref)
    for g in range(FIELDS):
        rows = slice(g * basis, (g + 1) * basis)
        base_ref[rows, :] = q_ref[rows, :] + weighted(*basis_weights, spread_ref[g])


def forward(place, p1_ref, p2_ref, *refs):
    outs = refs[-2:]
    _, c1 = unequal(place)
    for n, out in enumerate(outs):
        at = slice((n + 1) * HALF, (n + 2) * HALF)
        out[0:HALF, :] = p1_ref[at, :]
        out[HALF : 2 * HALF, :] = p2_ref[at, :]
        out[2 * HALF : 3 * HALF, :] = refs[n][...]
        if len(refs) > 4:
            at = 3 * HALF + OCEAN_ROWS
            out[3 * HALF : at, :] = refs[2 + n][...]
            for p_ref in (p1_ref, p2_ref):
                rows = p_ref[3 * HALF :, :]
                for i in range(4):
                    low, high = rows[4 * i : 4 * i + 2], rows[4 * i + 2 : 4 * i + 4]
                    ends = (high, low) if n == 0 else (low, high)
                    out[at : at + 2, :] = jnp.where(c1 > 0, *ends)
                    at += 2


def local_faces(table_ref, partner_ref, outer_ref):
    elements = partner_ref.shape[1]
    stack = table_parts(table_ref)
    codes = iota((4 * elements, elements), 0)
    for f in range(4):
        hot = (codes == partner_ref[f : f + 1, :]).astype(F32).astype(BF16)
        outer_ref[:, f * elements : (f + 1) * elements] = folded(dot(stack, hot))[:TABLE]


def remote_faces(place, outer_ref, partner_ref, table_refs, packed_ref, table_ref):
    p1_ref, p2_ref, q1_ref, q2_ref = table_refs
    elements = partner_ref.shape[1]
    a1, c1 = unequal(place)
    blocks = [
        (p1_ref, 0, column_block(a1)),
        (p2_ref, 0, column_block(-a1)),
        (q1_ref, 2 * HALF, row_block(c1)),
        (q2_ref, 2 * HALF, row_block(-c1)),
        (q1_ref, 0, column_block(a1) + c1),
        (q1_ref, HALF, column_block(-a1) + c1),
        (q2_ref, 0, column_block(a1) - c1),
        (q2_ref, HALF, column_block(-a1) - c1),
    ]
    left = iota((HALF, 2 * CAP), 1) < CAP
    for n in range(0, 8, 2):
        one = blocks[n][0][blocks[n][1] : blocks[n][1] + HALF, :]
        two = blocks[n + 1][0][blocks[n + 1][1] : blocks[n + 1][1] + HALF, :]
        lanes = slice(n * CAP, (n + 2) * CAP)
        packed_ref[0:HALF, lanes] = jnp.where(left, one, pltpu.roll(two, CAP, 1))
        packed_ref[HALF:, lanes] = jnp.where(left, pltpu.roll(one, CAP, 1), two)
    unpack(packed_ref, table_ref)
    remote = table_parts(table_ref)
    slot = iota((CAP, elements), 0)
    for f in range(4):
        wanted = partner_ref[f : f + 1, :] - 4 * elements
        hot = jnp.concatenate(
            [(slot + CAP * block[2] == wanted).astype(F32) for block in blocks], axis=0
        ).astype(BF16)
        columns = slice(f * elements, (f + 1) * elements)
        outer_ref[:, columns] += folded(dot(remote, hot))[:TABLE]


def lift_weights(lift_ref):
    basis = lift_ref.shape[2]
    return weights(
        lax.dot_general(
            selector(basis, basis, 0),
            stacked_traces(lift_ref),
            NT,
            preferred_element_type=F32,
            precision=lax.Precision.HIGHEST,
        )
    )


def lifted(base_ref, table_ref, outer_ref, normal_ref, speed_ref, star_ref, lift_ref, state_ref, flux_ref):
    basis = lift_ref.shape[2]
    elements = base_ref.shape[1]
    star = star_weights([star_ref[0], star_ref[1], star_ref[2]])
    size = FIELDS * 8
    for part in range(FACE_PAD // 8):
        at = [slice(g * FACE_PAD + 8 * part, g * FACE_PAD + 8 * part + 8) for g in range(FIELDS)]
        for f in range(4):
            columns = slice(f * elements, (f + 1) * elements)
            inner = jnp.concatenate([table_ref[rows, columns] for rows in at], axis=0)
            outer = jnp.concatenate([outer_ref[rows, columns] for rows in at], axis=0)
            y = folded(dot(star, both_parts(inner + outer)))
            flux = 0.5 * speed_ref[...] * (inner - outer)
            for c in range(3):
                flux = flux + 0.5 * normal_ref[c, f : f + 1, :] * y[c * size : (c + 1) * size]
            for g in range(FIELDS):
                flux_ref[g, f * FACE_PAD + 8 * part : f * FACE_PAD + 8 * part + 8, :] = flux[
                    8 * g : 8 * g + 8
                ]
    lift = lift_weights(lift_ref)
    for g in range(FIELDS):
        rows = slice(g * basis, (g + 1) * basis)
        state_ref[rows, :] = base_ref[rows, :] - weighted(*lift, flux_ref[g])


def back(
    place, base_ref, table_ref, outer_ref, partner_ref, normal_ref, speed_ref, star_ref, lift_ref,
    p1_ref, p2_ref, q1_ref, q2_ref,
    state_ref, flux_ref, packed_ref, remote_ref,
):
    arrived = (p1_ref, p2_ref, q1_ref, q2_ref)
    remote_faces(place, outer_ref, partner_ref, arrived, packed_ref, remote_ref)
    lifted(base_ref, table_ref, outer_ref, normal_ref, speed_ref, star_ref, lift_ref, state_ref, flux_ref)


def rates_out(vertical, trace_ref, interp_ref, sea_face_ref, sea_base_ref, sea_row_ref, out_ref):
    elements = vertical.shape[1]
    faces = sea_face_ref.shape[1]
    tiles = out_ref.shape[0]
    sea = weighted(*weights(stacked_traces(trace_ref)), vertical)
    sea = jnp.concatenate([sea[f * FACE_PAD : (f + 1) * FACE_PAD] for f in range(4)], axis=1)
    hot = (iota((4 * elements, faces), 0) == sea_face_ref[...]).astype(F32).astype(BF16)
    coeffs = folded(dot(both_parts(sea), hot))[:FACE_BASIS]
    rates = exact_dot(interp_ref[...], coeffs)
    corners = jnp.where(
        iota((8, faces), 0) == 0, sea_base_ref[0:1, :], sea_base_ref[1:2, :]
    ).astype(F32)
    sent = both_parts(jnp.concatenate([rates, corners], axis=0))
    row = sea_row_ref[...]
    hits = (iota((tiles, faces), 0) == row).astype(F32)
    before = (iota((faces, faces), 0) < iota((faces, faces), 1)).astype(F32)
    count = dot(hits.astype(BF16), before.astype(BF16))
    slot = jnp.sum(count * hits, axis=0, keepdims=True).astype(jnp.int32)
    lane = iota((2 * CAP, faces), 0)
    mine = slot == lane % CAP
    left = iota((POINTS // 2, 2 * CAP), 1) < CAP
    left_1 = iota((1, 2 * CAP), 1) < CAP
    for j in range(tiles):
        edges = mine & (row == jnp.where(lane < CAP, j - 1, j + 1))
        inside = mine & (row == j)
        hot = jnp.concatenate([edges.astype(F32), inside.astype(F32)], axis=0).astype(BF16)
        got = folded(lax.dot_general(sent, hot, NT, preferred_element_type=F32))
        near, own = got[:, : 2 * CAP], got[:, 2 * CAP :]
        out_ref[j, 0:POINTS, :] = near[:POINTS]
        out_ref[j, 16:24, :] = jnp.where(left, own[0:8], own[8:16])
        out_ref[j, 24:26, :] = near[POINTS : POINTS + 2]
        out_ref[j, 26:27, :] = jnp.where(left_1, own[16:17], own[17:18])
        out_ref[j, 27:32, :] = jnp.zeros((5, 2 * CAP), F32)


def finish(*refs):
    solid, sea, (state_ref, out_ref, *scratch) = refs[:13], refs[13:18], refs[18:]
    back(*solid, state_ref, *scratch)
    basis = sea[0].shape[2]
    vertical = state_ref[vertical_field * basis : (vertical_field + 1) * basis, :]
    rates_out(vertical, *sea, out_ref)


def forced(place, got_ref, forcing_ref, s1_ref, s2_ref):
    tiles = got_ref.shape[0]
    tile_x = forcing_ref.shape[0]
    tile_y = forcing_ref.shape[1] - 128
    left8 = iota((8, 2 * CAP), 1) < CAP
    left1 = iota((1, 2 * CAP), 1) < CAP
    tops, bottoms, xs, ys = [], [], [], []
    for s in range(0, tiles, 2):
        one, two = got_ref[s, 16:24, :], got_ref[s + 1, 16:24, :]
        tops.append(jnp.where(left8, one, pltpu.roll(two, CAP, 1)))
        bottoms.append(jnp.where(left8, pltpu.roll(one, CAP, 1), two))
        one, two = got_ref[s, 24:32, :], got_ref[s + 1, 24:32, :]
        xs.append(jnp.where(left8, one, pltpu.roll(two, CAP, 1))[2:3])
        ys.append(jnp.where(left8, pltpu.roll(one, CAP, 1), two)[2:3])
    lower, upper = jnp.concatenate(tops, axis=1), jnp.concatenate(bottoms, axis=1)
    x0, y0 = jnp.concatenate(xs, axis=1), jnp.concatenate(ys, axis=1)
    arrived = x0.shape[1]
    from_x = iota((tile_x, arrived), 0).astype(F32) - x0
    from_y = iota((tile_y, arrived), 0).astype(F32) - y0
    total = jnp.zeros((tile_x, tile_y), F32)
    for pr in range(patch_side):
        source = lower if pr < 2 else upper
        value = jnp.zeros((tile_y, arrived), F32)
        for pc in range(patch_side):
            at = (pr * patch_side + pc) % 8
            value = jnp.where(from_y == pc, source[at : at + 1], value)
        hot = (from_x == pr).astype(F32).astype(BF16)
        for value in parts(value):
            total += lax.dot_general(hot, value, NT, preferred_element_type=F32)
    forcing_ref[:, :tile_y] = total
    near = jnp.concatenate([got_ref[s, 0:POINTS, :] for s in range(tiles)], axis=1)
    x0 = jnp.concatenate([got_ref[s, 24:25, :] for s in range(tiles)], axis=1)
    y0 = jnp.concatenate([got_ref[s, 25:26, :] for s in range(tiles)], axis=1)
    arrived = x0.shape[1]
    from_x = iota((tile_x, arrived), 0).astype(F32) - x0
    rows = iota((8, arrived), 0)
    before = iota((8, arrived), 1) % (2 * CAP) < CAP
    high_y = jnp.where(before & (rows >= 6), (rows + (tile_y - 8)).astype(F32) - y0, -1.0)
    low_y = jnp.where(before | (rows >= 2), -1.0, rows.astype(F32) - y0)
    total = jnp.zeros((tile_x, 128), F32)
    blank = jnp.zeros((128 - 16, arrived), F32)
    for pr in range(patch_side):
        high, low = jnp.zeros((8, arrived), F32), jnp.zeros((8, arrived), F32)
        for pc in range(patch_side):
            at = pr * patch_side + pc
            high = jnp.where(high_y == pc, near[at : at + 1], high)
            low = jnp.where(low_y == pc, near[at : at + 1], low)
        hot = (from_x == pr).astype(F32).astype(BF16)
        for value in parts(jnp.concatenate([low, blank, high], axis=0)):
            total += lax.dot_general(hot, value, NT, preferred_element_type=F32)
    forcing_ref[:, tile_y:] = total
    a1, _ = unequal(place)
    head, tail = forcing_ref[0:8, :], forcing_ref[tile_x - 8 : tile_x, :]
    tail = pltpu.roll(tail, 2, 0)
    s1_ref[...] = jnp.where(a1 > 0, tail, head)
    s2_ref[...] = jnp.where(a1 > 0, head, tail)


def edge_rows(place, heads, tails, p1_ref, p2_ref):
    a1, _ = unequal(place)
    for i in range(4):
        head, tail = heads[i, 0:2, :], tails[i, 6:8, :]
        one = jnp.where(a1 > 0, tail, head)
        two = jnp.where(a1 > 0, head, tail)
        for h in range(2):
            at = slice(3 * HALF + 4 * i + 2 * h, 3 * HALF + 4 * i + 2 * h + 2)
            lanes = slice(128 * h, 128 * (h + 1))
            p1_ref[at, :] = one[:, lanes]
            p2_ref[at, :] = two[:, lanes]


def edge_columns(place, depth_ref, momentum_ref, bottom_ref, one_ref, two_ref):
    arrays = [depth_ref[...], momentum_ref[0], momentum_ref[1], bottom_ref[...]]
    _, c1 = unequal(place)
    tile_y = depth_ref.shape[1]
    row = iota((8, tile_y), 0)
    up = jnp.where(row < 2, row + (tile_y - 2), row - 2)
    down = jnp.where(row < 2, row, row + (tile_y - 4))
    wanted = jnp.where(c1 > 0, up, down)
    hot = ((row < 4) & (wanted == iota((8, tile_y), 1))).astype(F32)
    for i, array in enumerate(arrays):
        columns = lax.dot_general(
            hot, array, NT, preferred_element_type=F32, precision=lax.Precision.HIGHEST
        )
        for h in range(2):
            at = slice(4 * i + 2 * h, 4 * i + 2 * h + 2)
            lanes = slice(128 * h, 128 * (h + 1))
            one_ref[at, :] = columns[0:2, lanes]
            two_ref[at, :] = columns[2:4, lanes]


def volume_and_columns(place, *refs):
    solid, water, (base_ref, one_ref, two_ref, spread_ref) = refs[:5], refs[5:8], refs[8:]
    volume(*solid, base_ref, spread_ref)
    edge_columns(place, *water, one_ref, two_ref)


def widened(place, depth_ref, momentum_ref, bottom_ref, p1_ref, p2_ref, q1_ref, q2_ref, out_ref):
    tile_x, tile_y = depth_ref.shape
    a1, c1 = unequal(place)
    arrays = [depth_ref[...], momentum_ref[0], momentum_ref[1], bottom_ref[...]]
    p1, p2 = p1_ref[3 * HALF :, :], p2_ref[3 * HALF :, :]
    q1, q2 = q1_ref[3 * HALF :, :], q2_ref[3 * HALF :, :]
    is_below, is_above = place[0] > 0, place[0] < place[2] - 1
    below = jnp.where(is_below, jnp.where(a1 > 0, p2, p1), 0.0)
    above = jnp.where(is_above, jnp.where(a1 > 0, p1, p2), 0.0)
    before = jnp.where(place[1] > 0, jnp.where(c1 > 0, q2, q1), 0.0)
    after = jnp.where(place[1] < place[3] - 1, jnp.where(c1 > 0, q1, q2), 0.0)
    n = OCEAN_ROWS

    def ends(rows):
        one, two = rows[n : n + 8], rows[n + 8 :]
        return (
            jnp.where(is_below, jnp.where(a1 > 0, two, one), 0.0),
            jnp.where(is_above, jnp.where(a1 > 0, one, two), 0.0),
        )

    before_below, before_above = ends(before)
    after_below, after_above = ends(after)
    lane = iota((2, 128), 1)
    low, high = lane < 2, lane >= 126
    for i, array in enumerate(arrays):
        first, second = slice(4 * i, 4 * i + 2), slice(4 * i + 2, 4 * i + 4)
        out_ref[i, 0:MARGIN, :] = jnp.zeros((MARGIN, tile_y + 128), F32)
        out_ref[i, MARGIN + tile_x :, :] = jnp.zeros((MARGIN, tile_y + 128), F32)
        out_ref[i, MARGIN : MARGIN + tile_x, :tile_y] = array
        for at, rows, left, right in (
            (MARGIN - 2, below, before_below, after_below),
            (MARGIN + tile_x, above, before_above, after_above),
        ):
            out_ref[i, at : at + 2, 0:128] = rows[first]
            out_ref[i, at : at + 2, 128:256] = rows[second]
            end = slice(2 * i, 2 * i + 2)
            corner = jnp.where(low, right[end], jnp.where(high, left[end], 0.0))
            out_ref[i, at : at + 2, 256:384] = corner
        start = jnp.concatenate([after[first], after[second]], axis=1)
        finish = jnp.concatenate([before[first], before[second]], axis=1)
        columns = jnp.concatenate([start, jnp.zeros((124, tile_x), F32), finish], axis=0)
        out_ref[i, MARGIN : MARGIN + tile_x, tile_y:] = columns.T


STRIP = 16


def next_of(x):
    return pltpu.roll(x, x.shape[1] - 1, 1)


def previous_of(x):
    return pltpu.roll(x, 1, 1)


def cells(state, cell):
    for at in range(8, cell.shape[1] - 8, 8):
        here = slice(at, at + 8)
        h, mx, my = state[0, here, :], state[1, here, :], state[2, here, :]
        safe = jnp.maximum(h, depth_floor)
        root = lax.rsqrt(safe)
        inverse = root * root
        c = safe * root
        u, v = mx * inverse, my * inverse
        half = 0.5 * h * h
        cell[0, here, :] = mx * u + half
        cell[1, here, :] = my * u
        cell[2, here, :] = my * v + half
        cell[3, here, :] = 0.5 * (jnp.abs(u) + c)
        cell[4, here, :] = 0.5 * (jnp.abs(v) + c)


def moved(state, cell, at, rows):
    here, up, down = slice(at, at + rows), slice(at + 1, at + rows + 1), slice(at - 1, at + rows - 1)

    def x_face(i, j):
        wave = jnp.maximum(cell[3, i, :], cell[3, j, :])
        u_i, u_j = [state[k, i, :] for k in range(3)], [state[k, j, :] for k in range(3)]
        f_i = (u_i[1], cell[0, i, :], cell[1, i, :])
        f_j = (u_j[1], cell[0, j, :], cell[1, j, :])
        return [0.5 * (f_i[k] + f_j[k]) - wave * (u_j[k] - u_i[k]) for k in range(3)]

    now = [state[k, here, :] for k in range(3)]
    flux = (now[2], cell[1, here, :], cell[2, here, :])
    speed = cell[4, here, :]
    wave = jnp.maximum(speed, next_of(speed))
    y_face = [
        0.5 * (flux[k] + next_of(flux[k])) - wave * (next_of(now[k]) - now[k]) for k in range(3)
    ]
    upper, lower = x_face(here, up), x_face(down, here)
    return [
        now[k] - step_ocean * (upper[k] - lower[k] + y_face[k] - previous_of(y_face[k]))
        for k in range(3)
    ]


def sloped(height, bed, at, rows):
    b = bed[at : at + rows, :]
    slope_x = 0.5 * (bed[at + 1 : at + rows + 1, :] - bed[at - 1 : at + rows - 1, :])
    slope_y = 0.5 * (next_of(b) - previous_of(b))
    scale = step_ocean * height
    return scale * slope_x, scale * slope_y


def ocean_first(
    place, depth_ref, momentum_ref, bottom_ref, p1_ref, p2_ref, q1_ref, q2_ref, wide, state, cell
):
    tile_x, tile_y = depth_ref.shape
    widened(place, depth_ref, momentum_ref, bottom_ref, p1_ref, p2_ref, q1_ref, q2_ref, wide)
    cells(wide, cell)
    height, span = wide.shape[1:]
    lane = iota((STRIP, span), 1)
    outside = ((lane == span - 1) & (place[1] == 0)) | (
        (lane == tile_y) & (place[1] == place[3] - 1)
    )
    state[:, 0:8, :] = jnp.zeros((3, 8, span), F32)
    state[:, height - 8 :, :] = jnp.zeros((3, 8, span), F32)
    for at in range(8, height - 8, STRIP):
        new = moved(wide, cell, at, STRIP)
        row = iota((STRIP, span), 0) + at
        out = outside | ((row < MARGIN) & (place[0] == 0))
        out = out | ((row >= MARGIN + tile_x) & (place[0] == place[2] - 1))
        for k in range(3):
            state[k, at : at + STRIP, :] = jnp.where(out, 0.0, new[k])


def ocean_last(place, wide, first, forcing_ref, s1_ref, s2_ref, out_ref, bed_ref, state, bed, cell):
    tile_x, tile_y = bed_ref.shape
    height = wide.shape[1]
    a1, _ = unequal(place)
    force_lo = step_ocean * jnp.where(a1 > 0, s2_ref[...], s1_ref[...])[0:2]
    force_lo = jnp.where(place[0] > 0, force_lo, 0.0)
    force_hi = step_ocean * jnp.where(a1 > 0, s1_ref[...], s2_ref[...])[0:2]
    force_hi = jnp.where(place[0] < place[2] - 1, force_hi, 0.0)
    inner = slice(MARGIN, MARGIN + tile_x)

    def raised(source):
        bed[inner, :] = source[inner, :] + step_ocean * forcing_ref[...]
        bed[MARGIN - 2 : MARGIN, :] = source[MARGIN - 2 : MARGIN, :] + force_lo
        above = slice(MARGIN + tile_x, MARGIN + tile_x + 2)
        bed[above, :] = source[above, :] + force_hi

    bed[0:MARGIN, :] = wide[3, 0:MARGIN, :]
    bed[MARGIN + tile_x :, :] = wide[3, MARGIN + tile_x :, :]
    raised(wide.at[3])
    for at in range(8, height - 8, STRIP):
        here = slice(at, at + STRIP)
        change_x, change_y = sloped(wide[0, here, :], bed, at, STRIP)
        state[0, here, :] = first[0, here, :]
        state[1, here, :] = first[1, here, :] - change_x
        state[2, here, :] = first[2, here, :] - change_y
    cells(state, cell)
    raised(bed)
    for at in range(MARGIN, MARGIN + tile_x, STRIP):
        new = moved(state, cell, at, STRIP)
        change_x, change_y = sloped(state[0, at : at + STRIP, :], bed, at, STRIP)
        new[1] -= change_x
        new[2] -= change_y
        for k in range(3):
            out_ref[k, at - MARGIN : at - MARGIN + STRIP, :] = new[k][:, :tile_y]
    bed_ref[...] = bed[inner, :tile_y]


def call(body, out_shape, *args, place=None, scratch=(), held=0, copies=0, limit=VMEM_LIMIT):
    space = pltpu.HBM if held else pltpu.VMEM
    specs = [pl.BlockSpec(memory_space=space) for _ in args]
    scratch = [pltpu.VMEM(s, F32) for s in scratch]
    outer_space = pltpu.HBM if held else pltpu.VMEM
    if held:
        sems = pltpu.SemaphoreType.DMA((copies,))
        scratch = [pltpu.VMEM(x.shape, x.dtype) for x in args[:held]] + [sems] + scratch
    if place is not None:
        sizes, inner = place, body

        def body(*refs):
            here = (lax.axis_index("gx"), lax.axis_index("gy"))
            inner(here + sizes, *refs)

    shapes = [jax.ShapeDtypeStruct(s, F32) for s in out_shape]
    return pl.pallas_call(
        body,
        out_shape=shapes,
        in_specs=specs,
        out_specs=[pl.BlockSpec(memory_space=outer_space) for _ in shapes],
        scratch_shapes=scratch,
        compiler_params=pltpu.CompilerParams(vmem_limit_bytes=limit),
    )(*args)


def swap(block, axis, parity, wrap=False):
    count = lax.axis_size(axis)
    last = count + parity - 1 if wrap else count - 1
    pairs = []
    for i in range(parity, last, 2):
        pairs += [(i, (i + 1) % count), ((i + 1) % count, i)]
    taken = {source for source, _ in pairs}
    pairs += [(i, i) for i in range(count) if i not in taken]
    return lax.ppermute(block, axis, pairs)


def per_device(
    coefficients,
    jacobian,
    face_normals,
    wave_speed,
    star_mats,
    deriv_mats,
    stiff_mats,
    source_mat,
    trace_mats,
    lift_mats,
    face_partner,
    send_faces,
    sea_face,
    sea_row,
    sea_base,
    interp_mat,
    water_depth,
    momentum,
    bottom,
):
    basis, elements = coefficients.shape[1:]
    rows = FIELDS * basis
    tile_x, tile_y = water_depth.shape
    tiles = lax.axis_size("gy")
    place = (lax.axis_size("gx"), tiles)
    speed = wave_speed.reshape(1, elements)
    traces = trace_mats.transpose(1, 0, 2)
    normals = face_normals.transpose(1, 0, 2)
    lifts = lift_mats.transpose(2, 0, 1)
    spread = (FIELDS, 3 * basis, elements)
    faces = (TABLE, 4 * elements)
    solid = (rows, elements)
    wide_shape = (tile_x + 2 * MARGIN, tile_y + 128)
    state = coefficients.reshape(solid)
    packed = (2 * HALF, 8 * CAP)
    for section in range(2):
        fixed = (state, jacobian, star_mats, source_mat, deriv_mats, traces, send_faces)
        scratch = [spread, solid, solid, solid, (2 * HALF, 4 * CAP)]
        if section == 0:
            buffers = [(3 * HALF + OCEAN_ROWS, 128)] * 2 + [(HALF, 128)] * 2
            integral, table, p1, p2, own1, own2 = call(
                start, [solid, faces] + buffers, *fixed, water_depth, momentum, bottom,
                place=place, scratch=[(4, 8, tile_y)] * 2 + [solid, faces] + buffers + scratch,
                held=len(fixed), copies=len(fixed) + 14, limit=START_LIMIT,
            )
        else:
            buffers = [(3 * HALF, 128)] * 2 + [(HALF, 128)] * 2
            integral, table, p1, p2, own1, own2 = call(
                front, [solid, faces] + buffers, *fixed, place=place, scratch=scratch
            )
        p2, p1 = swap(p2, "gx", 1), swap(p1, "gx", 0)
        inside = (state, jacobian, star_mats, stiff_mats, integral)
        if section == 0:
            base, *columns = call(
                volume_and_columns, [solid] + [(OCEAN_ROWS, 128)] * 2,
                *inside, water_depth, momentum, bottom,
                place=place, scratch=[spread],
            )
            size = 3 * HALF + 2 * OCEAN_ROWS
        else:
            (base,) = call(volume, [solid], *inside, scratch=[spread])
            columns, size = [], 3 * HALF
        p1, p2, base = lax.optimization_barrier((p1, p2, base))
        q1, q2 = call(forward, [(size, 128)] * 2, p1, p2, own1, own2, *columns, place=place)
        q2, q1 = swap(q2, "gy", 1), swap(q1, "gy", 0)
        (outer,) = call(local_faces, [faces], table, face_partner)
        if section == 1:
            wide, first = call(
                ocean_first,
                [(4,) + wide_shape, (3,) + wide_shape],
                water_depth, momentum, bottom, *halos,
                place=place, scratch=[(5,) + wide_shape],
            )
            q1, q2, outer, wide, first = lax.optimization_barrier((q1, q2, outer, wide, first))
        else:
            q1, q2, outer = lax.optimization_barrier((q1, q2, outer))
        fixed = (normals, speed, star_mats, lifts)
        arrived = (p1, p2, q1, q2)
        flux = (FIELDS, 4 * FACE_PAD, elements)
        remote = (TABLE, 8 * CAP)
        if section == 0:
            (state,) = call(
                back, [solid], base, table, outer, face_partner, *fixed, *arrived,
                place=place, scratch=[flux, packed, remote],
            )
            halos = (p1, p2, q1, q2)
        else:
            state, outgoing = call(
                finish,
                [solid, (tiles, 32, 128)],
                base, table, outer, face_partner, *fixed, *arrived,
                traces, interp_mat, sea_face.reshape(1, -1), sea_base.T, sea_row.T,
                place=place, scratch=[flux, packed, remote],
            )
    incoming = lax.all_to_all(outgoing, "gy", split_axis=0, concat_axis=0, tiled=True)
    forcing, s1, s2 = call(
        forced,
        [(tile_x, tile_y + 128), (8, tile_y + 128), (8, tile_y + 128)],
        incoming,
        place=place,
    )
    s2, s1 = swap(s2, "gx", 1, wrap=True), swap(s1, "gx", 0)
    ocean_final, bed_final = call(
        ocean_last,
        [(3, tile_x, tile_y), (tile_x, tile_y)],
        wide, first, forcing, s1, s2,
        place=place,
        scratch=[(3,) + wide_shape, wide_shape, (5,) + wide_shape],
    )
    return (state.reshape(coefficients.shape), ocean_final, bed_final)


def solution(mesh):
    in_specs = (
        P(None, None, ("gx", "gy")),
        P(None, None, ("gx", "gy")),
        P(None, None, ("gx", "gy")),
        P(("gx", "gy")),
        P(),
        P(),
        P(),
        P(),
        P(),
        P(),
        P(None, ("gx", "gy")),
        P(None, ("gx", "gy")),
        P(("gx", "gy")),
        P(("gx", "gy"), None),
        P(("gx", "gy"), None),
        P(),
        P("gx", "gy"),
        P(None, "gx", "gy"),
        P("gx", "gy"),
    )
    out_specs = (P(None, None, ("gx", "gy")), P(None, "gx", "gy"), P("gx", "gy"))
    return jax.shard_map(
        per_device, mesh=mesh, in_specs=in_specs, out_specs=out_specs, check_vma=False
    )
```

```python
import jax
import jax.numpy as jnp
from jax import lax
from jax.experimental import pallas as pl
from jax.experimental.pallas import tpu as pltpu
from jax.sharding import PartitionSpec as P

FIELDS = 13
FACE_BASIS = 21
FACE_PAD = 24
POINTS = 16
ORD = 3
STEPS_OCEAN = 2
CAP = 64
TABLE = FIELDS * FACE_PAD
WIDE = 320
HALF = 144
OCEAN_ROWS = 16
MARGIN = 16

step_solid = 0.4
step_ocean = 0.2
depth_floor = 0.5
vertical_field = 6
patch_side = 4

F32 = jnp.float32
BF16 = jnp.bfloat16
NT = (((1,), (1,)), ((), ()))
VMEM_LIMIT = 24 * 1024 * 1024
START_LIMIT = 62 * 1024 * 1024


def iota(shape, dim):
    return lax.broadcasted_iota(jnp.int32, shape, dim)


def dot(a, b):
    return jnp.dot(a, b, preferred_element_type=F32)


def exact_dot(a, b):
    return jnp.dot(a, b, preferred_element_type=F32, precision=lax.Precision.HIGHEST)


def parts(x):
    high = x.astype(BF16)
    low = (x - high.astype(F32)).astype(BF16)
    return high, low


def both_parts(x):
    high = x.astype(BF16).astype(F32)
    return jnp.concatenate([high, x - high], axis=0).astype(BF16)


def folded(y):
    half = y.shape[0] // 2
    return y[:half] + y[half:]


def weights(w):
    return both_parts(w), w.astype(BF16)


def weighted(stack, high, x):
    x_high, x_low = parts(x)
    return folded(dot(stack, x_high)) + dot(high, x_low)


def selector(rows, columns, shift):
    return (iota((rows, columns), 1) == iota((rows, columns), 0) + shift).astype(F32)


def star_weights(mats):
    size = FIELDS * 8
    spread = ((iota((FIELDS, 2 * size), 1) % size) // 8 == iota((FIELDS, 2 * size), 0)).astype(F32)
    diagonal = iota((size, 2 * size), 0) % 8 == iota((size, 2 * size), 1) % 8
    first = iota((size, 2 * size), 1) < size
    high, low = [], []
    for mat in mats:
        wide = exact_dot(mat, spread)
        tall = jnp.concatenate(
            [jnp.broadcast_to(wide[g : g + 1], (8, 2 * size)) for g in range(FIELDS)], axis=0
        )
        tall = jnp.where(diagonal, tall, 0.0)
        top = tall.astype(BF16).astype(F32)
        high.append(top)
        low.append(jnp.where(first, tall - top, 0.0))
    return jnp.concatenate(high + low, axis=0).astype(BF16)


def side_by_side(mats):
    rows, columns = mats[0].shape
    total = len(mats) * columns
    return sum(exact_dot(m, selector(columns, total, i * columns)) for i, m in enumerate(mats))


def stacked_traces(trace_ref):
    place = (
        iota((FACE_PAD, FACE_BASIS), 0) == iota((FACE_PAD, FACE_BASIS), 1)
    ).astype(F32)
    return jnp.concatenate([exact_dot(place, trace_ref[:, f, :]) for f in range(4)], axis=0)


def spread_out(source, jac_ref, star, target, extra=None):
    basis = target.shape[1] // 3
    size = FIELDS * 8
    for j in range(basis // 8):
        x = jnp.concatenate(
            [source[g * basis + 8 * j : g * basis + 8 * j + 8, :] for g in range(FIELDS)], axis=0
        )
        y = folded(dot(star, both_parts(x)))
        for d in range(3):
            z = sum(jac_ref[d, c : c + 1, :] * y[c * size : (c + 1) * size] for c in range(3))
            for g in range(FIELDS):
                target[g, d * basis + 8 * j : d * basis + 8 * j + 8, :] = z[8 * g : 8 * g + 8]
        if extra is not None:
            for g in range(FIELDS):
                extra[g * basis + 8 * j : g * basis + 8 * j + 8, :] = y[
                    3 * size + 8 * g : 3 * size + 8 * g + 8
                ]


def derivative(source, target, jac_ref, star, basis_weights, spread_ref, relaxed_ref):
    basis = spread_ref.shape[1] // 3
    spread_out(source, jac_ref, star, spread_ref, relaxed_ref)
    for g in range(FIELDS):
        rows = slice(g * basis, (g + 1) * basis)
        target[rows, :] = -(weighted(*basis_weights, spread_ref[g]) + relaxed_ref[rows, :])


def unequal(place):
    a1 = jnp.where(place[0] % 2 == 0, 1, -1)
    c1 = jnp.where(place[1] % 2 == 0, 1, -1)
    return a1, c1


def column_block(a):
    return jnp.where(a > 0, 6, 1)


def row_block(c):
    return jnp.where(c > 0, 4, 3)


def front_weights(star_ref, source_ref, deriv_ref, trace_ref, ready=lambda *numbers: None):
    ready(2, 3)
    star = star_weights([star_ref[0], star_ref[1], star_ref[2], source_ref[...]])
    ready(4, 5)
    basis_weights = weights(side_by_side([deriv_ref[d] for d in range(3)]))
    return star, basis_weights, weights(stacked_traces(trace_ref))


def front_again(place, q_ref, jac_ref, star_ref, b1_ref, b2_ref, t1_ref, t2_ref, *refs):
    held = star_ref[...], (b1_ref[...], b2_ref[...]), (t1_ref[...], t2_ref[...])
    front(place, held, q_ref, jac_ref, *refs)


def front(
    place, held, q_ref, jac_ref, send_ref,
    integral_ref, table_ref, p1_ref, p2_ref, own1_ref, own2_ref,
    spread_ref, relaxed_ref, d1_ref, d2_ref, packed_ref, ready=lambda *numbers: None, made=lambda *numbers: None,
):
    elements = q_ref.shape[1]
    basis = q_ref.shape[0] // FIELDS
    star, basis_weights, trace = held
    ready(0, 1)
    derivative(q_ref, d1_ref, jac_ref, star, basis_weights, spread_ref, relaxed_ref)
    derivative(d1_ref, d2_ref, jac_ref, star, basis_weights, spread_ref, relaxed_ref)
    first = step_solid
    second = first * step_solid / 2
    third = second * step_solid / 3
    for g in range(FIELDS):
        rows = slice(g * basis, (g + 1) * basis)
        whole = first * q_ref[rows, :] + second * d1_ref[rows, :] + third * d2_ref[rows, :]
        integral_ref[rows, :] = whole
        faces = weighted(*trace, whole)
        for f in range(4):
            table_ref[g * FACE_PAD : (g + 1) * FACE_PAD, f * elements : (f + 1) * elements] = faces[
                f * FACE_PAD : (f + 1) * FACE_PAD
            ]
    made(0, 1)
    ready(6)
    a1, c1 = unequal(place)
    picks = [
        (p1_ref, 0, column_block(a1)),
        (p2_ref, 0, column_block(-a1)),
        (p1_ref, HALF, column_block(a1) + c1),
        (p1_ref, 2 * HALF, column_block(a1) - c1),
        (p2_ref, HALF, column_block(-a1) + c1),
        (p2_ref, 2 * HALF, column_block(-a1) - c1),
        (own1_ref, 0, row_block(c1)),
        (own2_ref, 0, row_block(-c1)),
    ]
    stack = table_parts(table_ref)
    left = iota((HALF, 2 * CAP), 1) < CAP
    codes = iota((4 * elements, 4 * CAP), 0)
    packed_ref[FIELDS * FACE_BASIS :, :] = jnp.zeros((2 * HALF - FIELDS * FACE_BASIS, 4 * CAP), F32)
    for n in range(0, 8, 4):
        wanted = jnp.concatenate([send_ref[pl.ds(pick[2], 1), :] for pick in picks[n : n + 4]], axis=1)
        got = folded(dot(stack, (codes == wanted).astype(F32).astype(BF16)))
        pack(got, packed_ref)
        for pair in range(2):
            lanes = slice(pair * 2 * CAP, (pair + 1) * 2 * CAP)
            low, high = packed_ref[0:HALF, lanes], packed_ref[HALF:, lanes]
            ref, at, _ = picks[n + 2 * pair]
            ref[at : at + HALF, :] = jnp.where(left, low, pltpu.roll(high, CAP, 1))
            ref, at, _ = picks[n + 2 * pair + 1]
            ref[at : at + HALF, :] = jnp.where(left, pltpu.roll(low, CAP, 1), high)


def pack(table, packed_ref):
    rest = FACE_BASIS - 16
    for g in range(FIELDS):
        packed_ref[16 * g : 16 * (g + 1), :] = table[FACE_PAD * g : FACE_PAD * g + 16]
        at = 16 * FIELDS + rest * g
        packed_ref[at : at + rest, :] = table[FACE_PAD * g + 16 : FACE_PAD * g + FACE_BASIS]


def unpack(packed_ref, table_ref):
    rest = FACE_BASIS - 16
    for g in range(FIELDS):
        table_ref[FACE_PAD * g : FACE_PAD * g + 16, :] = packed_ref[16 * g : 16 * (g + 1), :]
        at = 16 * FIELDS + rest * g
        last = FACE_PAD * g + 16
        table_ref[last : last + 8, :] = jnp.zeros((8, table_ref.shape[1]), F32)
        table_ref[last : last + rest, :] = packed_ref[at : at + rest, :]


def start(place, *refs):
    sources, water, refs = refs[:7], refs[7:10], refs[10:]
    targets, refs = refs[:6], refs[6:]
    held, outs, (sems, heads, tails, *scratch) = refs[:7], refs[7:13], refs[13:]
    depth, momentum, bottom = water
    last = depth.shape[0] - 8
    pairs = [(sources[i], held[i]) for i in range(7)]
    for rows, target in ((pl.ds(0, 8), heads), (pl.ds(last, 8), tails)):
        pairs += [
            (depth.at[rows], target.at[0]),
            (momentum.at[0, rows], target.at[1]),
            (momentum.at[1, rows], target.at[2]),
            (bottom.at[rows], target.at[3]),
        ]
    first_out = len(pairs)
    pairs += list(zip(outs, targets))
    copies = [pltpu.make_async_copy(a, b, sems.at[i]) for i, (a, b) in enumerate(pairs)]
    for copy in copies[:first_out]:
        copy.start()

    def ready(*numbers):
        for i in numbers:
            copies[i].wait()

    def made(*numbers):
        for i in numbers:
            copies[first_out + i].start()

    ready_weights = front_weights(*held[2:6], ready=ready)
    front(place, ready_weights, *held[:2], held[6], *outs, *scratch, ready=ready, made=made)
    ready(*range(7, first_out))
    edge_rows(place, heads, tails, *outs[2:4])
    made(2, 3, 4, 5)
    ready(*range(first_out, len(copies)))


def table_parts(table_ref):
    pad = jnp.zeros((WIDE - TABLE, table_ref.shape[1]), BF16)
    high, low = parts(table_ref[...])
    both = [high.astype(F32), pad.astype(F32), low.astype(F32), pad.astype(F32)]
    return jnp.concatenate(both, axis=0).astype(BF16)


def volume(q_ref, jac_ref, star_ref, stiff_ref, integral_ref, base_ref, spread_ref):
    basis = stiff_ref.shape[1]
    star = star_weights([star_ref[0], star_ref[1], star_ref[2]])
    basis_weights = weights(side_by_side([stiff_ref[d] for d in range(3)]))
    spread_out(integral_ref, jac_ref, star, spread_ref)
    for g in range(FIELDS):
        rows = slice(g * basis, (g + 1) * basis)
        base_ref[rows, :] = q_ref[rows, :] + weighted(*basis_weights, spread_ref[g])


def forward(place, p1_ref, p2_ref, *refs):
    outs = refs[-2:]
    _, c1 = unequal(place)
    for n, out in enumerate(outs):
        at = slice((n + 1) * HALF, (n + 2) * HALF)
        out[0:HALF, :] = p1_ref[at, :]
        out[HALF : 2 * HALF, :] = p2_ref[at, :]
        out[2 * HALF : 3 * HALF, :] = refs[n][...]
        if len(refs) > 4:
            at = 3 * HALF + OCEAN_ROWS
            out[3 * HALF : at, :] = refs[2 + n][...]
            for p_ref in (p1_ref, p2_ref):
                rows = p_ref[3 * HALF :, :]
                for i in range(4):
                    low, high = rows[4 * i : 4 * i + 2], rows[4 * i + 2 : 4 * i + 4]
                    ends = (high, low) if n == 0 else (low, high)
                    out[at : at + 2, :] = jnp.where(c1 > 0, *ends)
                    at += 2


def local_faces(table_ref, partner_ref, outer_ref):
    elements = partner_ref.shape[1]
    stack = table_parts(table_ref)
    codes = iota((4 * elements, elements), 0)
    for f in range(4):
        hot = (codes == partner_ref[f : f + 1, :]).astype(F32).astype(BF16)
        outer_ref[:, f * elements : (f + 1) * elements] = folded(dot(stack, hot))[:TABLE]


def remote_blocks(place, p1, p2, q1, q2):
    a1, c1 = unequal(place)
    return [
        (p1, 0, column_block(a1)),
        (p2, 0, column_block(-a1)),
        (q1, 2 * HALF, row_block(c1)),
        (q2, 2 * HALF, row_block(-c1)),
        (q1, 0, column_block(a1) + c1),
        (q1, HALF, column_block(-a1) + c1),
        (q2, 0, column_block(a1) - c1),
        (q2, HALF, column_block(-a1) - c1),
    ]


def prepared(
    place, star_ref, source_ref, deriv_ref, trace_ref, lift_ref, partner_ref,
    sea_face_ref, sea_row_ref,
    star4_ref, star3_ref, b1_ref, b2_ref, t1_ref, t2_ref, l1_ref, l2_ref, hot_ref, sea_ref, slot_ref,
):
    star, (b1_ref[...], b2_ref[...]), (t1_ref[...], t2_ref[...]) = front_weights(
        star_ref, source_ref, deriv_ref, trace_ref
    )
    star4_ref[...] = star
    star3_ref[...] = star_weights([star_ref[0], star_ref[1], star_ref[2]])
    l1_ref[...], l2_ref[...] = lift_weights(lift_ref)
    elements = partner_ref.shape[1]
    blocks = remote_blocks(place, None, None, None, None)
    slot = iota((CAP, elements), 0)
    for f in range(4):
        wanted = partner_ref[f : f + 1, :] - 4 * elements
        hot_ref[:, f * elements : (f + 1) * elements] = jnp.concatenate(
            [(slot + CAP * block[2] == wanted).astype(F32) for block in blocks], axis=0
        ).astype(BF16)
    faces = sea_face_ref.shape[1]
    sea_ref[...] = (iota((4 * elements, faces), 0) == sea_face_ref[...]).astype(F32).astype(BF16)
    row = sea_row_ref[...]
    tiles = slot_ref.shape[0]
    hits = (iota((tiles, faces), 0) == row).astype(F32)
    before = (iota((faces, faces), 0) < iota((faces, faces), 1)).astype(F32)
    count = dot(hits.astype(BF16), before.astype(BF16))
    mine = jnp.sum(count * hits, axis=0, keepdims=True).astype(jnp.int32)
    lane = iota((2 * CAP, faces), 0)
    mine = mine == lane % CAP
    for j in range(tiles):
        edges = mine & (row == jnp.where(lane < CAP, j - 1, j + 1))
        inside = mine & (row == j)
        slot_ref[j] = jnp.concatenate([edges.astype(F32), inside.astype(F32)], axis=0).astype(BF16)


def remote_faces(place, outer_ref, hot_ref, table_refs, packed_ref, table_ref):
    elements = hot_ref.shape[1] // 4
    blocks = remote_blocks(place, *table_refs)
    left = iota((HALF, 2 * CAP), 1) < CAP
    for n in range(0, 8, 2):
        one = blocks[n][0][blocks[n][1] : blocks[n][1] + HALF, :]
        two = blocks[n + 1][0][blocks[n + 1][1] : blocks[n + 1][1] + HALF, :]
        lanes = slice(n * CAP, (n + 2) * CAP)
        packed_ref[0:HALF, lanes] = jnp.where(left, one, pltpu.roll(two, CAP, 1))
        packed_ref[HALF:, lanes] = jnp.where(left, pltpu.roll(one, CAP, 1), two)
    unpack(packed_ref, table_ref)
    remote = table_parts(table_ref)
    for f in range(4):
        columns = slice(f * elements, (f + 1) * elements)
        outer_ref[:, columns] += folded(dot(remote, hot_ref[:, columns]))[:TABLE]


def lift_weights(lift_ref):
    basis = lift_ref.shape[2]
    return weights(
        lax.dot_general(
            selector(basis, basis, 0),
            stacked_traces(lift_ref),
            NT,
            preferred_element_type=F32,
            precision=lax.Precision.HIGHEST,
        )
    )


def lifted(base_ref, table_ref, outer_ref, normal_ref, speed_ref, star, lift, state_ref, flux_ref):
    elements = base_ref.shape[1]
    basis = base_ref.shape[0] // FIELDS
    size = FIELDS * 8
    for part in range(FACE_PAD // 8):
        at = [slice(g * FACE_PAD + 8 * part, g * FACE_PAD + 8 * part + 8) for g in range(FIELDS)]
        for f in range(4):
            columns = slice(f * elements, (f + 1) * elements)
            inner = jnp.concatenate([table_ref[rows, columns] for rows in at], axis=0)
            outer = jnp.concatenate([outer_ref[rows, columns] for rows in at], axis=0)
            y = folded(dot(star, both_parts(inner + outer)))
            flux = 0.5 * speed_ref[...] * (inner - outer)
            for c in range(3):
                flux = flux + 0.5 * normal_ref[c, f : f + 1, :] * y[c * size : (c + 1) * size]
            for g in range(FIELDS):
                flux_ref[g, f * FACE_PAD + 8 * part : f * FACE_PAD + 8 * part + 8, :] = flux[
                    8 * g : 8 * g + 8
                ]
    for g in range(FIELDS):
        rows = slice(g * basis, (g + 1) * basis)
        state_ref[rows, :] = base_ref[rows, :] - weighted(*lift, flux_ref[g])


def back(
    place, base_ref, table_ref, outer_ref, normal_ref, speed_ref, star_ref, l1_ref, l2_ref, hot_ref,
    p1_ref, p2_ref, q1_ref, q2_ref,
    state_ref, flux_ref, packed_ref, remote_ref,
):
    arrived = (p1_ref, p2_ref, q1_ref, q2_ref)
    remote_faces(place, outer_ref, hot_ref, arrived, packed_ref, remote_ref)
    lift = l1_ref[...], l2_ref[...]
    lifted(
        base_ref, table_ref, outer_ref, normal_ref, speed_ref, star_ref[...], lift, state_ref, flux_ref
    )


def rates_out(vertical, t1_ref, t2_ref, interp_ref, sea_base_ref, sea_ref, slot_ref, out_ref):
    tiles, _, faces = slot_ref.shape
    sea = weighted(t1_ref[...], t2_ref[...], vertical)
    sea = jnp.concatenate([sea[f * FACE_PAD : (f + 1) * FACE_PAD] for f in range(4)], axis=1)
    coeffs = folded(dot(both_parts(sea), sea_ref[...]))[:FACE_BASIS]
    rates = exact_dot(interp_ref[...], coeffs)
    corners = jnp.where(
        iota((8, faces), 0) == 0, sea_base_ref[0:1, :], sea_base_ref[1:2, :]
    ).astype(F32)
    sent = both_parts(jnp.concatenate([rates, corners], axis=0))
    left = iota((POINTS // 2, 2 * CAP), 1) < CAP
    left_1 = iota((1, 2 * CAP), 1) < CAP
    for j in range(tiles):
        got = folded(lax.dot_general(sent, slot_ref[j], NT, preferred_element_type=F32))
        near, own = got[:, : 2 * CAP], got[:, 2 * CAP :]
        out_ref[j, 0:POINTS, :] = near[:POINTS]
        out_ref[j, 16:24, :] = jnp.where(left, own[0:8], own[8:16])
        out_ref[j, 24:26, :] = near[POINTS : POINTS + 2]
        out_ref[j, 26:27, :] = jnp.where(left_1, own[16:17], own[17:18])
        out_ref[j, 27:32, :] = jnp.zeros((5, 2 * CAP), F32)


def finish(*refs):
    solid, sea, refs = refs[:14], refs[14:20], refs[20:]
    state_out, out_ref, state_ref, sems, *scratch = refs
    back(*solid, state_ref, *scratch)
    copy = pltpu.make_async_copy(state_ref, state_out, sems.at[0])
    copy.start()
    basis = state_ref.shape[0] // FIELDS
    vertical = state_ref[vertical_field * basis : (vertical_field + 1) * basis, :]
    rates_out(vertical, *sea, out_ref)
    copy.wait()


def forced(place, got_ref, forcing_ref, s1_ref, s2_ref):
    tiles = got_ref.shape[0]
    tile_x = forcing_ref.shape[0]
    tile_y = forcing_ref.shape[1] - 128
    left8 = iota((8, 2 * CAP), 1) < CAP
    left1 = iota((1, 2 * CAP), 1) < CAP
    tops, bottoms, xs, ys = [], [], [], []
    for s in range(0, tiles, 2):
        one, two = got_ref[s, 16:24, :], got_ref[s + 1, 16:24, :]
        tops.append(jnp.where(left8, one, pltpu.roll(two, CAP, 1)))
        bottoms.append(jnp.where(left8, pltpu.roll(one, CAP, 1), two))
        one, two = got_ref[s, 24:32, :], got_ref[s + 1, 24:32, :]
        xs.append(jnp.where(left8, one, pltpu.roll(two, CAP, 1))[2:3])
        ys.append(jnp.where(left8, pltpu.roll(one, CAP, 1), two)[2:3])
    lower, upper = jnp.concatenate(tops, axis=1), jnp.concatenate(bottoms, axis=1)
    x0, y0 = jnp.concatenate(xs, axis=1), jnp.concatenate(ys, axis=1)
    arrived = x0.shape[1]
    hot = (iota((tile_x, arrived), 0).astype(F32) == x0).astype(F32).astype(BF16)
    from_y = iota((tile_y, arrived), 0).astype(F32) - y0
    total = jnp.zeros((tile_x, tile_y), F32)
    for pr in range(patch_side):
        source = lower if pr < 2 else upper
        value = jnp.zeros((tile_y, arrived), F32)
        for pc in range(patch_side):
            at = (pr * patch_side + pc) % 8
            value = jnp.where(from_y == pc, source[at : at + 1], value)
        got = sum(
            lax.dot_general(hot, part, NT, preferred_element_type=F32) for part in parts(value)
        )
        total += got if pr == 0 else pltpu.roll(got, pr, 0)
    forcing_ref[:, :tile_y] = total
    near = jnp.concatenate([got_ref[s, 0:POINTS, :] for s in range(tiles)], axis=1)
    x0 = jnp.concatenate([got_ref[s, 24:25, :] for s in range(tiles)], axis=1)
    y0 = jnp.concatenate([got_ref[s, 25:26, :] for s in range(tiles)], axis=1)
    arrived = x0.shape[1]
    hot = (iota((tile_x, arrived), 0).astype(F32) == x0).astype(F32).astype(BF16)
    rows = iota((8, arrived), 0)
    before = iota((8, arrived), 1) % (2 * CAP) < CAP
    high_y = jnp.where(before & (rows >= 6), (rows + (tile_y - 8)).astype(F32) - y0, -1.0)
    low_y = jnp.where(before | (rows >= 2), -1.0, rows.astype(F32) - y0)
    chunks = [None] * 16
    for pr in range(patch_side):
        high, low = jnp.zeros((8, arrived), F32), jnp.zeros((8, arrived), F32)
        for pc in range(patch_side):
            at = pr * patch_side + pc
            high = jnp.where(high_y == pc, near[at : at + 1], high)
            low = jnp.where(low_y == pc, near[at : at + 1], low)
        chunks[(4 * pr - 1) % 16], chunks[4 * pr] = high, low
    blank = jnp.zeros((8, arrived), F32)
    value = jnp.concatenate([blank if c is None else c for c in chunks], axis=0)
    got = sum(lax.dot_general(hot, part, NT, preferred_element_type=F32) for part in parts(value))
    lane = iota((tile_x, 128), 1)
    used = (lane < 2) | (lane >= 126)
    total = jnp.where(used, got, 0.0)
    for pr in range(1, patch_side):
        moved_back = pltpu.roll(pltpu.roll(got, 128 - 32 * pr, 1), pr, 0)
        total += jnp.where(used, moved_back, 0.0)
    forcing_ref[:, tile_y:] = total
    a1, _ = unequal(place)
    head, tail = forcing_ref[0:8, :], forcing_ref[tile_x - 8 : tile_x, :]
    tail = pltpu.roll(tail, 2, 0)
    s1_ref[...] = jnp.where(a1 > 0, tail, head)
    s2_ref[...] = jnp.where(a1 > 0, head, tail)


def edge_rows(place, heads, tails, p1_ref, p2_ref):
    a1, _ = unequal(place)
    for i in range(4):
        head, tail = heads[i, 0:2, :], tails[i, 6:8, :]
        one = jnp.where(a1 > 0, tail, head)
        two = jnp.where(a1 > 0, head, tail)
        for h in range(2):
            at = slice(3 * HALF + 4 * i + 2 * h, 3 * HALF + 4 * i + 2 * h + 2)
            lanes = slice(128 * h, 128 * (h + 1))
            p1_ref[at, :] = one[:, lanes]
            p2_ref[at, :] = two[:, lanes]


def edge_columns(place, depth_ref, momentum_ref, bottom_ref, one_ref, two_ref):
    arrays = [depth_ref[...], momentum_ref[0], momentum_ref[1], bottom_ref[...]]
    _, c1 = unequal(place)
    tile_y = depth_ref.shape[1]
    row = iota((8, tile_y), 0)
    up = jnp.where(row < 2, row + (tile_y - 2), row - 2)
    down = jnp.where(row < 2, row, row + (tile_y - 4))
    wanted = jnp.where(c1 > 0, up, down)
    hot = ((row < 4) & (wanted == iota((8, tile_y), 1))).astype(F32)
    for i, array in enumerate(arrays):
        columns = lax.dot_general(
            hot, array, NT, preferred_element_type=F32, precision=lax.Precision.HIGHEST
        )
        for h in range(2):
            at = slice(4 * i + 2 * h, 4 * i + 2 * h + 2)
            lanes = slice(128 * h, 128 * (h + 1))
            one_ref[at, :] = columns[0:2, lanes]
            two_ref[at, :] = columns[2:4, lanes]


def volume_and_columns(place, *refs):
    solid, water, (base_ref, one_ref, two_ref, spread_ref) = refs[:5], refs[5:8], refs[8:]
    volume(*solid, base_ref, spread_ref)
    edge_columns(place, *water, one_ref, two_ref)


def widened(place, depth_ref, momentum_ref, bottom_ref, p1_ref, p2_ref, q1_ref, q2_ref, out_ref):
    tile_x, tile_y = depth_ref.shape
    a1, c1 = unequal(place)
    arrays = [depth_ref[...], momentum_ref[0], momentum_ref[1], bottom_ref[...]]
    p1, p2 = p1_ref[3 * HALF :, :], p2_ref[3 * HALF :, :]
    q1, q2 = q1_ref[3 * HALF :, :], q2_ref[3 * HALF :, :]
    is_below, is_above = place[0] > 0, place[0] < place[2] - 1
    below = jnp.where(is_below, jnp.where(a1 > 0, p2, p1), 0.0)
    above = jnp.where(is_above, jnp.where(a1 > 0, p1, p2), 0.0)
    before = jnp.where(place[1] > 0, jnp.where(c1 > 0, q2, q1), 0.0)
    after = jnp.where(place[1] < place[3] - 1, jnp.where(c1 > 0, q1, q2), 0.0)
    n = OCEAN_ROWS

    def ends(rows):
        one, two = rows[n : n + 8], rows[n + 8 :]
        return (
            jnp.where(is_below, jnp.where(a1 > 0, two, one), 0.0),
            jnp.where(is_above, jnp.where(a1 > 0, one, two), 0.0),
        )

    before_below, before_above = ends(before)
    after_below, after_above = ends(after)
    lane = iota((2, 128), 1)
    low, high = lane < 2, lane >= 126
    for i, array in enumerate(arrays):
        first, second = slice(4 * i, 4 * i + 2), slice(4 * i + 2, 4 * i + 4)
        out_ref[i, 0:MARGIN, :] = jnp.zeros((MARGIN, tile_y + 128), F32)
        out_ref[i, MARGIN + tile_x :, :] = jnp.zeros((MARGIN, tile_y + 128), F32)
        out_ref[i, MARGIN : MARGIN + tile_x, :tile_y] = array
        for at, rows, left, right in (
            (MARGIN - 2, below, before_below, after_below),
            (MARGIN + tile_x, above, before_above, after_above),
        ):
            out_ref[i, at : at + 2, 0:128] = rows[first]
            out_ref[i, at : at + 2, 128:256] = rows[second]
            end = slice(2 * i, 2 * i + 2)
            corner = jnp.where(low, right[end], jnp.where(high, left[end], 0.0))
            out_ref[i, at : at + 2, 256:384] = corner
        start = jnp.concatenate([after[first], after[second]], axis=1)
        finish = jnp.concatenate([before[first], before[second]], axis=1)
        columns = jnp.concatenate([start, jnp.zeros((124, tile_x), F32), finish], axis=0)
        out_ref[i, MARGIN : MARGIN + tile_x, tile_y:] = columns.T


STRIP = 16


def next_of(x):
    return pltpu.roll(x, x.shape[1] - 1, 1)


def previous_of(x):
    return pltpu.roll(x, 1, 1)


def cells(state, cell, low, high):
    for at in range(low, high, 8):
        here = slice(at, at + 8)
        h, mx, my = state[0, here, :], state[1, here, :], state[2, here, :]
        safe = jnp.maximum(h, depth_floor)
        root = lax.rsqrt(safe)
        inverse = root * root
        c = safe * root
        u, v = mx * inverse, my * inverse
        half = 0.5 * h * h
        cell[0, here, :] = mx * u + half
        cell[1, here, :] = my * u
        cell[2, here, :] = my * v + half
        cell[3, here, :] = 0.5 * (jnp.abs(u) + c)
        cell[4, here, :] = 0.5 * (jnp.abs(v) + c)


def moved(state, cell, face, at, rows):
    here, up = slice(at, at + rows), slice(at + 1, at + rows + 1)
    below = slice(at - 1, at + rows - 1)
    now = [state[k, here, :] for k in range(3)]
    cross = cell[1, here, :]
    next_now = [state[k, up, :] for k in range(3)]
    wave = jnp.maximum(cell[3, here, :], cell[3, up, :])
    pairs = ((now[1], next_now[1]), (cell[0, here, :], cell[0, up, :]), (cross, cell[1, up, :]))
    upper = [
        0.5 * (pairs[k][0] + pairs[k][1]) - wave * (next_now[k] - now[k]) for k in range(3)
    ]
    for k in range(3):
        face[k, here, :] = upper[k]
    flux = (now[2], cross, cell[2, here, :])
    speed = cell[4, here, :]
    wave = jnp.maximum(speed, next_of(speed))
    next_now = [next_of(x) for x in now]
    next_flux = (next_now[2], next_of(flux[1]), next_of(flux[2]))
    y_face = [
        0.5 * (flux[k] + next_flux[k]) - wave * (next_now[k] - now[k]) for k in range(3)
    ]
    return [
        now[k] - step_ocean * (upper[k] - face[k, below, :] + y_face[k] - previous_of(y_face[k]))
        for k in range(3)
    ]


def sloped(height, bed, at, rows):
    b = bed[at : at + rows, :]
    slope_x = 0.5 * (bed[at + 1 : at + rows + 1, :] - bed[at - 1 : at + rows - 1, :])
    slope_y = 0.5 * (next_of(b) - previous_of(b))
    scale = step_ocean * height
    return scale * slope_x, scale * slope_y


def ocean_first(
    place, depth_ref, momentum_ref, bottom_ref, p1_ref, p2_ref, q1_ref, q2_ref, wide, state, cell, face
):
    tile_x, tile_y = depth_ref.shape
    widened(place, depth_ref, momentum_ref, bottom_ref, p1_ref, p2_ref, q1_ref, q2_ref, wide)
    cells(wide, cell, 8, cell.shape[1] - 8)
    height, span = wide.shape[1:]
    lane = iota((STRIP, span), 1)
    outside = ((lane == span - 1) & (place[1] == 0)) | (
        (lane == tile_y) & (place[1] == place[3] - 1)
    )
    state[:, 0:8, :] = jnp.zeros((3, 8, span), F32)
    state[:, height - 8 :, :] = jnp.zeros((3, 8, span), F32)
    face[:, 0:8, :] = jnp.zeros((3, 8, span), F32)
    for at in range(8, height - 8, STRIP):
        new = moved(wide, cell, face, at, STRIP)
        row = iota((STRIP, span), 0) + at
        out = outside | ((row < MARGIN) & (place[0] == 0))
        out = out | ((row >= MARGIN + tile_x) & (place[0] == place[2] - 1))
        for k in range(3):
            state[k, at : at + STRIP, :] = jnp.where(out, 0.0, new[k])


def second_step(wide, first, bed, state, cell, face, rows, put, raise_bed):
    low, high = rows.start - 8, rows.stop + 8
    raise_bed(wide.at[3])
    for at in range(low, high, STRIP):
        here = slice(at, at + STRIP)
        change_x, change_y = sloped(wide[0, here, :], bed, at, STRIP)
        state[0, here, :] = first[0, here, :]
        state[1, here, :] = first[1, here, :] - change_x
        state[2, here, :] = first[2, here, :] - change_y
    cells(state, cell, low, high)
    raise_bed(bed)
    moved(state, cell, face, low, 8)
    for at in range(rows.start, rows.stop, STRIP):
        new = moved(state, cell, face, at, STRIP)
        change_x, change_y = sloped(state[0, at : at + STRIP, :], bed, at, STRIP)
        new[1] -= change_x
        new[2] -= change_y
        put(at, new)


def ocean_inner(wide, first, forcing_ref, out_ref, bed_ref, state, bed, cell, face):
    tile_x, tile_y = bed_ref.shape
    inner = slice(MARGIN, MARGIN + tile_x)
    bed[...] = wide[3]

    def raise_bed(source):
        bed[inner, :] = source[inner, :] + step_ocean * forcing_ref[...]

    def put(at, new):
        for k in range(3):
            out_ref[k, at - MARGIN : at - MARGIN + STRIP, :] = new[k][:, :tile_y]

    rows = slice(MARGIN + STRIP, MARGIN + tile_x - STRIP)
    second_step(wide, first, bed, state, cell, face, rows, put, raise_bed)
    bed_ref[...] = bed[inner, :tile_y]


def ocean_ends(
    place, wide, first, forcing_ref, s1_ref, s2_ref, inner_ref, raised_ref, out_hbm, bed_hbm,
    out_ref, bed_ref, sems, state, bed, cell, face,
):
    tile_x, tile_y = raised_ref.shape
    last = tile_x - STRIP
    middle = pl.ds(STRIP, tile_x - 2 * STRIP)
    copies = [
        pltpu.make_async_copy(raised_ref, bed_hbm, sems.at[0]),
        pltpu.make_async_copy(inner_ref.at[:, middle], out_hbm.at[:, middle], sems.at[1]),
    ]
    for copy in copies:
        copy.start()
    a1, _ = unequal(place)
    force_lo = step_ocean * jnp.where(a1 > 0, s2_ref[...], s1_ref[...])[0:2]
    force_lo = jnp.where(place[0] > 0, force_lo, 0.0)
    force_hi = step_ocean * jnp.where(a1 > 0, s1_ref[...], s2_ref[...])[0:2]
    force_hi = jnp.where(place[0] < place[2] - 1, force_hi, 0.0)

    def put(at, new):
        for k in range(3):
            out_ref[k, at - MARGIN : at - MARGIN + STRIP, :] = new[k][:, :tile_y]

    for n, start in enumerate((MARGIN, MARGIN + last)):
        outer = slice(start - 16, start) if n == 0 else slice(start + STRIP, start + STRIP + 16)
        edge = slice(MARGIN - 2, MARGIN) if n == 0 else slice(MARGIN + tile_x, MARGIN + tile_x + 2)
        force = force_lo if n == 0 else force_hi
        own = slice(start, start + 32) if n == 0 else slice(start - 16, start + 16)
        forcing = forcing_ref[own.start - MARGIN : own.stop - MARGIN, :]
        bed[outer, :] = wide[3, outer, :]

        def raise_bed(source):
            bed[own, :] = source[own, :] + step_ocean * forcing
            bed[edge, :] = source[edge, :] + force

        second_step(
            wide, first, bed, state, cell, face, slice(start, start + STRIP), put, raise_bed
        )
        at = pl.ds(start - MARGIN, STRIP)
        copies.append(pltpu.make_async_copy(out_ref.at[:, at], out_hbm.at[:, at], sems.at[2 + n]))
        copies[-1].start()
    for copy in copies:
        copy.wait()


def call(
    body, out_shape, *args, place=None, scratch=(), held=0, sent=0, copies=0, limit=VMEM_LIMIT
):
    out_space = [pltpu.HBM if i < sent else pltpu.VMEM for i in range(len(out_shape))]
    specs = [pl.BlockSpec(memory_space=pltpu.HBM if held else pltpu.VMEM) for _ in args]
    shapes = [
        s if isinstance(s, jax.ShapeDtypeStruct) else jax.ShapeDtypeStruct(s, F32) for s in out_shape
    ]
    scratch = [pltpu.VMEM(s, F32) for s in scratch]
    if copies:
        scratch = [pltpu.SemaphoreType.DMA((copies,))] + scratch
    scratch = [pltpu.VMEM(x.shape, x.dtype) for x in [*args[:held], *shapes[:sent]]] + scratch
    if place is not None:
        sizes, inner = place, body

        def body(*refs):
            here = (lax.axis_index("gx"), lax.axis_index("gy"))
            inner(here + sizes, *refs)

    return pl.pallas_call(
        body,
        out_shape=shapes,
        in_specs=specs,
        out_specs=[pl.BlockSpec(memory_space=space) for space in out_space],
        scratch_shapes=scratch,
        compiler_params=pltpu.CompilerParams(vmem_limit_bytes=limit),
    )(*args)


def swap(block, axis, parity, wrap=False):
    count = lax.axis_size(axis)
    last = count + parity - 1 if wrap else count - 1
    pairs = []
    for i in range(parity, last, 2):
        pairs += [(i, (i + 1) % count), ((i + 1) % count, i)]
    taken = {source for source, _ in pairs}
    pairs += [(i, i) for i in range(count) if i not in taken]
    return lax.ppermute(block, axis, pairs)


def per_device(
    coefficients,
    jacobian,
    face_normals,
    wave_speed,
    star_mats,
    deriv_mats,
    stiff_mats,
    source_mat,
    trace_mats,
    lift_mats,
    face_partner,
    send_faces,
    sea_face,
    sea_row,
    sea_base,
    interp_mat,
    water_depth,
    momentum,
    bottom,
):
    basis, elements = coefficients.shape[1:]
    rows = FIELDS * basis
    tile_x, tile_y = water_depth.shape
    tiles = lax.axis_size("gy")
    place = (lax.axis_size("gx"), tiles)
    speed = wave_speed.reshape(1, elements)
    traces = trace_mats.transpose(1, 0, 2)
    normals = face_normals.transpose(1, 0, 2)
    lifts = lift_mats.transpose(2, 0, 1)
    spread = (FIELDS, 3 * basis, elements)
    faces = (TABLE, 4 * elements)
    solid = (rows, elements)
    wide_shape = (tile_x + 2 * MARGIN, tile_y + 128)
    state = coefficients.reshape(solid)
    packed = (2 * HALF, 8 * CAP)
    for section in range(2):
        scratch = [spread, solid, solid, solid, (2 * HALF, 4 * CAP)]
        if section == 0:
            fixed = (state, jacobian, star_mats, source_mat, deriv_mats, traces, send_faces)
            buffers = [(3 * HALF + OCEAN_ROWS, 128)] * 2 + [(HALF, 128)] * 2
            integral, table, p1, p2, own1, own2 = call(
                start, [solid, faces] + buffers, *fixed, water_depth, momentum, bottom,
                place=place, scratch=[(4, 8, tile_y)] * 2 + scratch,
                held=len(fixed), sent=6, copies=len(fixed) + 14, limit=START_LIMIT,
            )
        else:
            buffers = [(3 * HALF, 128)] * 2 + [(HALF, 128)] * 2
            integral, table, p1, p2, own1, own2 = call(
                front_again, [solid, faces] + buffers,
                state, jacobian, star4, *derivs, *traced, send_faces, place=place, scratch=scratch,
            )
        p2, p1 = swap(p2, "gx", 1), swap(p1, "gx", 0)
        inside = (state, jacobian, star_mats, stiff_mats, integral)
        if section == 0:
            base, *columns = call(
                volume_and_columns, [solid] + [(OCEAN_ROWS, 128)] * 2,
                *inside, water_depth, momentum, bottom,
                place=place, scratch=[spread],
            )
            size = 3 * HALF + 2 * OCEAN_ROWS
        else:
            (base,) = call(volume, [solid], *inside, scratch=[spread])
            columns, size = [], 3 * HALF
        p1, p2, base = lax.optimization_barrier((p1, p2, base))
        q1, q2 = call(forward, [(size, 128)] * 2, p1, p2, own1, own2, *columns, place=place)
        q2, q1 = swap(q2, "gy", 1), swap(q1, "gy", 0)
        (outer,) = call(local_faces, [faces], table, face_partner)
        if section == 1:
            wide, first = call(
                ocean_first,
                [(4,) + wide_shape, (3,) + wide_shape],
                water_depth, momentum, bottom, *halos,
                place=place, scratch=[(5,) + wide_shape, (3,) + wide_shape],
            )
            q1, q2, outer, wide, first = lax.optimization_barrier((q1, q2, outer, wide, first))
        else:
            half = lambda *shape: jax.ShapeDtypeStruct(shape, BF16)
            size, sea = FIELDS * 8, sea_face.shape[0]
            star4, star3, *ready = call(
                prepared,
                [half(8 * size, 2 * size), half(6 * size, 2 * size)]
                + [half(2 * basis, 3 * basis), half(basis, 3 * basis)]
                + [half(8 * FACE_PAD, basis), half(4 * FACE_PAD, basis)]
                + [half(2 * basis, 4 * FACE_PAD), half(basis, 4 * FACE_PAD)]
                + [half(8 * CAP, 4 * elements), half(4 * elements, sea), half(tiles, 4 * CAP, sea)],
                star_mats, source_mat, deriv_mats, traces, lifts, face_partner,
                sea_face.reshape(1, -1), sea_row.T,
                place=place,
            )
            q1, q2, outer, *ready = lax.optimization_barrier((q1, q2, outer, *ready))
            derivs, traced, lifting, (hot, sea_hot, slot_hot) = (
                ready[0:2], ready[2:4], ready[4:6], ready[6:],
            )
        fixed = (normals, speed, star3, *lifting, hot)
        arrived = (p1, p2, q1, q2)
        flux = (FIELDS, 4 * FACE_PAD, elements)
        remote = (TABLE, 8 * CAP)
        if section == 0:
            (state,) = call(
                back, [solid], base, table, outer, *fixed, *arrived,
                place=place, scratch=[flux, packed, remote],
            )
            halos = (p1, p2, q1, q2)
        else:
            state, outgoing = call(
                finish,
                [solid, (tiles, 32, 128)],
                base, table, outer, *fixed, *arrived,
                *traced, interp_mat, sea_base.T, sea_hot, slot_hot,
                place=place, scratch=[flux, packed, remote], sent=1, copies=1,
            )
    incoming = lax.all_to_all(outgoing, "gy", split_axis=0, concat_axis=0, tiled=True)
    forcing, s1, s2 = call(
        forced,
        [(tile_x, tile_y + 128), (8, tile_y + 128), (8, tile_y + 128)],
        incoming,
        place=place,
    )
    s2, s1 = swap(s2, "gx", 1, wrap=True), swap(s1, "gx", 0)
    scratch = [(3,) + wide_shape, wide_shape, (5,) + wide_shape, (3,) + wide_shape]
    water = [(3, tile_x, tile_y), (tile_x, tile_y)]
    inner, raised = call(ocean_inner, water, wide, first, forcing, scratch=scratch)
    ocean_final, bed_final = call(
        ocean_ends, water, wide, first, forcing, s1, s2, inner, raised,
        place=place, scratch=scratch, sent=2, copies=4,
    )
    return (state.reshape(coefficients.shape), ocean_final, bed_final)


def solution(mesh):
    in_specs = (
        P(None, None, ("gx", "gy")),
        P(None, None, ("gx", "gy")),
        P(None, None, ("gx", "gy")),
        P(("gx", "gy")),
        P(),
        P(),
        P(),
        P(),
        P(),
        P(),
        P(None, ("gx", "gy")),
        P(None, ("gx", "gy")),
        P(("gx", "gy")),
        P(("gx", "gy"), None),
        P(("gx", "gy"), None),
        P(),
        P("gx", "gy"),
        P(None, "gx", "gy"),
        P("gx", "gy"),
    )
    out_specs = (P(None, None, ("gx", "gy")), P(None, "gx", "gy"), P("gx", "gy"))
    return jax.shard_map(
        per_device, mesh=mesh, in_specs=in_specs, out_specs=out_specs, check_vma=False
    )
```

```python
import jax
import jax.numpy as jnp
from jax import lax
from jax.experimental import pallas as pl
from jax.experimental.pallas import tpu as pltpu
from jax.sharding import PartitionSpec as P

FIELDS = 13
FACE_BASIS = 21
FACE_PAD = 24
POINTS = 16
ORD = 3
STEPS_OCEAN = 2
CAP = 64
TABLE = FIELDS * FACE_PAD
WIDE = 320
HALF = 137
OCEAN_ROWS = 16
MARGIN = 16

step_solid = 0.4
step_ocean = 0.2
depth_floor = 0.5
vertical_field = 6
patch_side = 4

F32 = jnp.float32
BF16 = jnp.bfloat16
NT = (((1,), (1,)), ((), ()))
VMEM_LIMIT = 24 * 1024 * 1024
START_LIMIT = 62 * 1024 * 1024


def iota(shape, dim):
    return lax.broadcasted_iota(jnp.int32, shape, dim)


def dot(a, b):
    return jnp.dot(a, b, preferred_element_type=F32)


def exact_dot(a, b):
    return jnp.dot(a, b, preferred_element_type=F32, precision=lax.Precision.HIGHEST)


def parts(x):
    high = x.astype(BF16)
    low = (x - high.astype(F32)).astype(BF16)
    return high, low


def both_parts(x):
    high = x.astype(BF16).astype(F32)
    return jnp.concatenate([high, x - high], axis=0).astype(BF16)


def folded(y):
    half = y.shape[0] // 2
    return y[:half] + y[half:]


def weights(w):
    return both_parts(w), w.astype(BF16)


def weighted(stack, high, x):
    x_high, x_low = parts(x)
    return folded(dot(stack, x_high)) + dot(high, x_low)


def side_weights(w):
    columns = w.shape[1]
    high, low = parts(w)
    place = [selector(columns, 3 * columns, i * columns).astype(BF16) for i in range(3)]
    return (dot(high, place[0] + place[1]) + dot(low, place[2])).astype(BF16)


def side_weighted(stack, x):
    high = x.astype(BF16).astype(F32)
    return dot(stack, jnp.concatenate([high, x - high, high], axis=0).astype(BF16))


def selector(rows, columns, shift):
    return (iota((rows, columns), 1) == iota((rows, columns), 0) + shift).astype(F32)


def star_weights(mats):
    size = FIELDS * 8
    spread = ((iota((FIELDS, 2 * size), 1) % size) // 8 == iota((FIELDS, 2 * size), 0)).astype(F32)
    diagonal = iota((size, 2 * size), 0) % 8 == iota((size, 2 * size), 1) % 8
    first = iota((size, 2 * size), 1) < size
    high, low = [], []
    for mat in mats:
        wide = exact_dot(mat, spread)
        tall = jnp.concatenate(
            [jnp.broadcast_to(wide[g : g + 1], (8, 2 * size)) for g in range(FIELDS)], axis=0
        )
        tall = jnp.where(diagonal, tall, 0.0)
        top = tall.astype(BF16).astype(F32)
        high.append(top)
        low.append(jnp.where(first, tall - top, 0.0))
    return jnp.concatenate(high + low, axis=0).astype(BF16)


def side_by_side(mats):
    rows, columns = mats[0].shape
    total = len(mats) * columns
    return sum(exact_dot(m, selector(columns, total, i * columns)) for i, m in enumerate(mats))


def stacked_traces(trace_ref):
    place = (
        iota((FACE_PAD, FACE_BASIS), 0) == iota((FACE_PAD, FACE_BASIS), 1)
    ).astype(F32)
    return jnp.concatenate([exact_dot(place, trace_ref[:, f, :]) for f in range(4)], axis=0)


def spread_out(source, jac_ref, star, target, extra=None):
    basis = target.shape[1] // 3
    size = FIELDS * 8
    for j in range(basis // 8):
        x = jnp.concatenate(
            [source[g * basis + 8 * j : g * basis + 8 * j + 8, :] for g in range(FIELDS)], axis=0
        )
        y = folded(dot(star, both_parts(x)))
        for d in range(3):
            z = sum(jac_ref[d, c : c + 1, :] * y[c * size : (c + 1) * size] for c in range(3))
            for g in range(FIELDS):
                target[g, d * basis + 8 * j : d * basis + 8 * j + 8, :] = z[8 * g : 8 * g + 8]
        if extra is not None:
            for g in range(FIELDS):
                extra[g * basis + 8 * j : g * basis + 8 * j + 8, :] = y[
                    3 * size + 8 * g : 3 * size + 8 * g + 8
                ]


def derivative(source, target, jac_ref, star, basis_weights, spread_ref, relaxed_ref):
    basis = spread_ref.shape[1] // 3
    spread_out(source, jac_ref, star, spread_ref, relaxed_ref)
    for g in range(FIELDS):
        rows = slice(g * basis, (g + 1) * basis)
        target[rows, :] = -(weighted(*basis_weights, spread_ref[g]) + relaxed_ref[rows, :])


def unequal(place):
    a1 = jnp.where(place[0] % 2 == 0, 1, -1)
    c1 = jnp.where(place[1] % 2 == 0, 1, -1)
    return a1, c1


def column_block(a):
    return jnp.where(a > 0, 6, 1)


def row_block(c):
    return jnp.where(c > 0, 4, 3)


def front_weights(star_ref, source_ref, deriv_ref, trace_ref, ready=lambda *numbers: None):
    ready(2, 3)
    star = star_weights([star_ref[0], star_ref[1], star_ref[2], source_ref[...]])
    ready(4, 5)
    basis_weights = weights(side_by_side([deriv_ref[d] for d in range(3)]))
    return star, basis_weights, side_weights(stacked_traces(trace_ref))


def front_again(place, q_ref, jac_ref, star_ref, b1_ref, b2_ref, trace_ref, *refs):
    held = star_ref[...], (b1_ref[...], b2_ref[...]), trace_ref[...]
    front(place, held, q_ref, jac_ref, *refs)


def front(
    place, held, q_ref, jac_ref, send_ref,
    integral_ref, table_ref, p1_ref, p2_ref, own1_ref, own2_ref,
    spread_ref, relaxed_ref, d1_ref, d2_ref, packed_ref, ready=lambda *numbers: None, made=lambda *numbers: None,
):
    elements = q_ref.shape[1]
    basis = q_ref.shape[0] // FIELDS
    star, basis_weights, trace = held
    ready(0, 1)
    derivative(q_ref, d1_ref, jac_ref, star, basis_weights, spread_ref, relaxed_ref)
    derivative(d1_ref, d2_ref, jac_ref, star, basis_weights, spread_ref, relaxed_ref)
    first = step_solid
    second = first * step_solid / 2
    third = second * step_solid / 3
    for g in range(FIELDS):
        rows = slice(g * basis, (g + 1) * basis)
        whole = first * q_ref[rows, :] + second * d1_ref[rows, :] + third * d2_ref[rows, :]
        integral_ref[rows, :] = whole
        faces = side_weighted(trace, whole)
        for f in range(4):
            table_ref[g * FACE_PAD : (g + 1) * FACE_PAD, f * elements : (f + 1) * elements] = faces[
                f * FACE_PAD : (f + 1) * FACE_PAD
            ]
    made(0, 1)
    ready(6)
    a1, c1 = unequal(place)
    picks = [
        (p1_ref, 0, column_block(a1)),
        (p2_ref, 0, column_block(-a1)),
        (p1_ref, HALF, column_block(a1) + c1),
        (p1_ref, 2 * HALF, column_block(a1) - c1),
        (p2_ref, HALF, column_block(-a1) + c1),
        (p2_ref, 2 * HALF, column_block(-a1) - c1),
        (own1_ref, 0, row_block(c1)),
        (own2_ref, 0, row_block(-c1)),
    ]
    stack = table_parts(table_ref)
    left = iota((HALF, 2 * CAP), 1) < CAP
    codes = iota((4 * elements, 4 * CAP), 0)
    packed_ref[FIELDS * FACE_BASIS :, :] = jnp.zeros((2 * HALF - FIELDS * FACE_BASIS, 4 * CAP), F32)
    for n in range(0, 8, 4):
        wanted = jnp.concatenate([send_ref[pl.ds(pick[2], 1), :] for pick in picks[n : n + 4]], axis=1)
        got = folded(dot(stack, (codes == wanted).astype(F32).astype(BF16)))
        pack(got, packed_ref)
        for pair in range(2):
            lanes = slice(pair * 2 * CAP, (pair + 1) * 2 * CAP)
            low, high = packed_ref[0:HALF, lanes], packed_ref[HALF:, lanes]
            ref, at, _ = picks[n + 2 * pair]
            ref[at : at + HALF, :] = jnp.where(left, low, pltpu.roll(high, CAP, 1))
            ref, at, _ = picks[n + 2 * pair + 1]
            ref[at : at + HALF, :] = jnp.where(left, pltpu.roll(low, CAP, 1), high)


def pack(table, packed_ref):
    rest = FACE_BASIS - 16
    for g in range(FIELDS):
        packed_ref[16 * g : 16 * (g + 1), :] = table[FACE_PAD * g : FACE_PAD * g + 16]
        at = 16 * FIELDS + rest * g
        packed_ref[at : at + rest, :] = table[FACE_PAD * g + 16 : FACE_PAD * g + FACE_BASIS]


def unpack(packed_ref, table_ref):
    rest = FACE_BASIS - 16
    for g in range(FIELDS):
        table_ref[FACE_PAD * g : FACE_PAD * g + 16, :] = packed_ref[16 * g : 16 * (g + 1), :]
        at = 16 * FIELDS + rest * g
        last = FACE_PAD * g + 16
        table_ref[last : last + 8, :] = jnp.zeros((8, table_ref.shape[1]), F32)
        table_ref[last : last + rest, :] = packed_ref[at : at + rest, :]


def start(place, *refs):
    sources, water, refs = refs[:7], refs[7:10], refs[10:]
    targets, refs = refs[:6], refs[6:]
    held, outs, (sems, heads, tails, *scratch) = refs[:7], refs[7:13], refs[13:]
    depth, momentum, bottom = water
    last = depth.shape[0] - 8
    pairs = [(sources[i], held[i]) for i in range(7)]
    for rows, target in ((pl.ds(0, 8), heads), (pl.ds(last, 8), tails)):
        pairs += [
            (depth.at[rows], target.at[0]),
            (momentum.at[0, rows], target.at[1]),
            (momentum.at[1, rows], target.at[2]),
            (bottom.at[rows], target.at[3]),
        ]
    first_out = len(pairs)
    pairs += list(zip(outs, targets))
    copies = [pltpu.make_async_copy(a, b, sems.at[i]) for i, (a, b) in enumerate(pairs)]
    for copy in copies[:first_out]:
        copy.start()

    def ready(*numbers):
        for i in numbers:
            copies[i].wait()

    def made(*numbers):
        for i in numbers:
            copies[first_out + i].start()

    ready_weights = front_weights(*held[2:6], ready=ready)
    front(place, ready_weights, *held[:2], held[6], *outs, *scratch, ready=ready, made=made)
    ready(*range(7, first_out))
    edge_rows(place, heads, tails, *outs[2:4])
    made(2, 3, 4, 5)
    ready(*range(first_out, len(copies)))


def table_parts(table_ref):
    pad = jnp.zeros((WIDE - TABLE, table_ref.shape[1]), BF16)
    high, low = parts(table_ref[...])
    both = [high.astype(F32), pad.astype(F32), low.astype(F32), pad.astype(F32)]
    return jnp.concatenate(both, axis=0).astype(BF16)


def volume(q_ref, jac_ref, star_ref, stiff_ref, integral_ref, base_ref, spread_ref):
    basis = stiff_ref.shape[1]
    star = star_weights([star_ref[0], star_ref[1], star_ref[2]])
    basis_weights = weights(side_by_side([stiff_ref[d] for d in range(3)]))
    spread_out(integral_ref, jac_ref, star, spread_ref)
    for g in range(FIELDS):
        rows = slice(g * basis, (g + 1) * basis)
        base_ref[rows, :] = q_ref[rows, :] + weighted(*basis_weights, spread_ref[g])


def forward(place, p1_ref, p2_ref, *refs):
    outs = refs[-2:]
    _, c1 = unequal(place)
    for n, out in enumerate(outs):
        at = slice((n + 1) * HALF, (n + 2) * HALF)
        out[0:HALF, :] = p1_ref[at, :]
        out[HALF : 2 * HALF, :] = p2_ref[at, :]
        out[2 * HALF : 3 * HALF, :] = refs[n][...]
        if len(refs) > 4:
            at = 3 * HALF + OCEAN_ROWS
            out[3 * HALF : at, :] = refs[2 + n][...]
            for p_ref in (p1_ref, p2_ref):
                rows = p_ref[3 * HALF :, :]
                for i in range(4):
                    low, high = rows[4 * i : 4 * i + 2], rows[4 * i + 2 : 4 * i + 4]
                    ends = (high, low) if n == 0 else (low, high)
                    out[at : at + 2, :] = jnp.where(c1 > 0, *ends)
                    at += 2


def star_flux(star, normals, speed, inner, outer):
    size = FIELDS * 8
    y = folded(dot(star, both_parts(inner + outer)))
    flux = speed * (inner - outer)
    for c in range(3):
        flux = flux + normals[c] * y[c * size : (c + 1) * size]
    return flux


def local_flux(table_ref, partner_ref, normal_ref, speed_ref, star_ref, flux_ref, outer_ref):
    elements = partner_ref.shape[1]
    stack = table_parts(table_ref)
    codes = iota((4 * elements, elements), 0)
    star = star_ref[...]
    speed = 0.5 * speed_ref[...]
    for f in range(4):
        hot = (codes == partner_ref[f : f + 1, :]).astype(F32).astype(BF16)
        outer_ref[:, f * elements : (f + 1) * elements] = folded(dot(stack, hot))[:TABLE]
    for part in range(FACE_PAD // 8):
        at = [slice(g * FACE_PAD + 8 * part, g * FACE_PAD + 8 * part + 8) for g in range(FIELDS)]
        for f in range(4):
            normals = [0.5 * normal_ref[c, f : f + 1, :] for c in range(3)]
            columns = slice(f * elements, (f + 1) * elements)
            inner = jnp.concatenate([table_ref[rows, columns] for rows in at], axis=0)
            outer = jnp.concatenate([outer_ref[rows, columns] for rows in at], axis=0)
            flux = star_flux(star, normals, speed, inner, outer)
            for g in range(FIELDS):
                flux_ref[g, f * FACE_PAD + 8 * part : f * FACE_PAD + 8 * part + 8, :] = flux[
                    8 * g : 8 * g + 8
                ]


def remote_blocks(place, p1, p2, q1, q2):
    a1, c1 = unequal(place)
    return [
        (p1, 0, column_block(a1)),
        (p2, 0, column_block(-a1)),
        (q1, 2 * HALF, row_block(c1)),
        (q2, 2 * HALF, row_block(-c1)),
        (q1, 0, column_block(a1) + c1),
        (q1, HALF, column_block(-a1) + c1),
        (q2, 0, column_block(a1) - c1),
        (q2, HALF, column_block(-a1) - c1),
    ]


def prepared(
    place, star_ref, source_ref, deriv_ref, trace_ref, lift_ref, partner_ref,
    sea_face_ref, sea_row_ref, normal_ref, speed_ref,
    star4_ref, star3_ref, b1_ref, b2_ref, t_ref, l1_ref, l2_ref, hot_ref, sea_ref, slot_ref, scale_ref,
):
    star, (b1_ref[...], b2_ref[...]), t_ref[...] = front_weights(
        star_ref, source_ref, deriv_ref, trace_ref
    )
    star4_ref[...] = star
    star3_ref[...] = star_weights([star_ref[0], star_ref[1], star_ref[2]])
    l1_ref[...], l2_ref[...] = lift_weights(lift_ref)
    elements = partner_ref.shape[1]
    blocks = remote_blocks(place, None, None, None, None)
    slot = iota((CAP, elements), 0)
    for f in range(4):
        wanted = partner_ref[f : f + 1, :] - 4 * elements
        hot_ref[:, f * elements : (f + 1) * elements] = jnp.concatenate(
            [(slot + CAP * block[2] == wanted).astype(F32) for block in blocks], axis=0
        ).astype(BF16)
    scales = [
        jnp.concatenate([normal_ref[c, f : f + 1, :] for f in range(4)], axis=1) for c in range(3)
    ]
    scales.append(jnp.concatenate([speed_ref[...]] * 4, axis=1))
    scales = 0.5 * jnp.concatenate(scales + [jnp.zeros((4, 4 * elements), F32)], axis=0)
    scale_ref[...] = folded(
        lax.dot_general(both_parts(scales), hot_ref[...], NT, preferred_element_type=F32)
    )
    faces = sea_face_ref.shape[1]
    sea_ref[...] = (iota((4 * elements, faces), 0) == sea_face_ref[...]).astype(F32).astype(BF16)
    row = sea_row_ref[...]
    tiles = slot_ref.shape[0]
    hits = (iota((tiles, faces), 0) == row).astype(F32)
    before = (iota((faces, faces), 0) < iota((faces, faces), 1)).astype(F32)
    count = dot(hits.astype(BF16), before.astype(BF16))
    mine = jnp.sum(count * hits, axis=0, keepdims=True).astype(jnp.int32)
    lane = iota((2 * CAP, faces), 0)
    mine = mine == lane % CAP
    for j in range(tiles):
        edges = mine & (row == jnp.where(lane < CAP, j - 1, j + 1))
        inside = mine & (row == j)
        slot_ref[j] = jnp.concatenate([edges.astype(F32), inside.astype(F32)], axis=0).astype(BF16)


def remote_flux(place, flux_ref, star_ref, hot_ref, scale_ref, arrived, packed_ref, table_ref):
    elements = hot_ref.shape[1] // 4
    blocks = remote_blocks(place, *arrived)
    left = iota((HALF, 2 * CAP), 1) < CAP
    for n in range(0, 8, 2):
        one = blocks[n][0][blocks[n][1] : blocks[n][1] + HALF, :]
        two = blocks[n + 1][0][blocks[n + 1][1] : blocks[n + 1][1] + HALF, :]
        lanes = slice(n * CAP, (n + 2) * CAP)
        packed_ref[0:HALF, lanes] = jnp.where(left, one, pltpu.roll(two, CAP, 1))
        packed_ref[HALF:, lanes] = jnp.where(left, pltpu.roll(one, CAP, 1), two)
    unpack(packed_ref, table_ref)
    star = star_ref[...]
    for part in range(FACE_PAD // 8):
        at = [slice(g * FACE_PAD + 8 * part, g * FACE_PAD + 8 * part + 8) for g in range(FIELDS)]
        for half in range(2):
            lanes = slice(4 * CAP * half, 4 * CAP * (half + 1))
            normals = [scale_ref[c : c + 1, lanes] for c in range(3)]
            outer = jnp.concatenate([table_ref[rows, lanes] for rows in at], axis=0)
            y = folded(dot(star, both_parts(outer)))
            size = FIELDS * 8
            flux = -scale_ref[3:4, lanes] * outer
            for c in range(3):
                flux = flux + normals[c] * y[c * size : (c + 1) * size]
            for g, rows in enumerate(at):
                table_ref[rows, lanes] = flux[8 * g : 8 * g + 8]
    remote = table_parts(table_ref)
    for f in range(4):
        columns = slice(f * elements, (f + 1) * elements)
        got = folded(dot(remote, hot_ref[:, columns]))
        for g in range(FIELDS):
            flux_ref[g, f * FACE_PAD : (f + 1) * FACE_PAD, :] += got[
                g * FACE_PAD : (g + 1) * FACE_PAD
            ]


def lift_weights(lift_ref):
    basis = lift_ref.shape[2]
    return weights(
        lax.dot_general(
            selector(basis, basis, 0),
            stacked_traces(lift_ref),
            NT,
            preferred_element_type=F32,
            precision=lax.Precision.HIGHEST,
        )
    )


def back(
    place, base_ref, local_ref, star_ref, l1_ref, l2_ref, hot_ref, scale_ref,
    p1_ref, p2_ref, q1_ref, q2_ref,
    state_ref, flux_ref, packed_ref, remote_ref,
):
    arrived = (p1_ref, p2_ref, q1_ref, q2_ref)
    flux_ref[...] = local_ref[...]
    remote_flux(place, flux_ref, star_ref, hot_ref, scale_ref, arrived, packed_ref, remote_ref)
    lift = l1_ref[...], l2_ref[...]
    basis = base_ref.shape[0] // FIELDS
    for g in range(FIELDS):
        rows = slice(g * basis, (g + 1) * basis)
        state_ref[rows, :] = base_ref[rows, :] - weighted(*lift, flux_ref[g])


def rates_out(vertical, trace_ref, interp_ref, sea_base_ref, sea_ref, slot_ref, out_ref):
    tiles, _, faces = slot_ref.shape
    sea = side_weighted(trace_ref[...], vertical)
    sea = jnp.concatenate([sea[f * FACE_PAD : (f + 1) * FACE_PAD] for f in range(4)], axis=1)
    coeffs = folded(dot(both_parts(sea), sea_ref[...]))[:FACE_BASIS]
    rates = exact_dot(interp_ref[...], coeffs)
    corners = jnp.where(
        iota((8, faces), 0) == 0, sea_base_ref[0:1, :], sea_base_ref[1:2, :]
    ).astype(F32)
    sent = both_parts(jnp.concatenate([rates, corners], axis=0))
    left = iota((POINTS // 2, 2 * CAP), 1) < CAP
    left_1 = iota((1, 2 * CAP), 1) < CAP
    for j in range(tiles):
        got = folded(lax.dot_general(sent, slot_ref[j], NT, preferred_element_type=F32))
        near, own = got[:, : 2 * CAP], got[:, 2 * CAP :]
        out_ref[j, 0:POINTS, :] = near[:POINTS]
        out_ref[j, 16:24, :] = jnp.where(left, own[0:8], own[8:16])
        out_ref[j, 24:26, :] = near[POINTS : POINTS + 2]
        out_ref[j, 26:27, :] = jnp.where(left_1, own[16:17], own[17:18])
        out_ref[j, 27:32, :] = jnp.zeros((5, 2 * CAP), F32)


def finish(*refs):
    solid, sea, refs = refs[:12], refs[12:17], refs[17:]
    state_out, out_ref, state_ref, sems, *scratch = refs
    back(*solid, state_ref, *scratch)
    copy = pltpu.make_async_copy(state_ref, state_out, sems.at[0])
    copy.start()
    basis = state_ref.shape[0] // FIELDS
    vertical = state_ref[vertical_field * basis : (vertical_field + 1) * basis, :]
    rates_out(vertical, *sea, out_ref)
    copy.wait()


def forced(place, got_ref, forcing_ref, s1_ref, s2_ref):
    tiles = got_ref.shape[0]
    tile_x = forcing_ref.shape[0]
    tile_y = forcing_ref.shape[1] - 128
    left8 = iota((8, 2 * CAP), 1) < CAP
    left1 = iota((1, 2 * CAP), 1) < CAP
    tops, bottoms, xs, ys = [], [], [], []
    for s in range(0, tiles, 2):
        one, two = got_ref[s, 16:24, :], got_ref[s + 1, 16:24, :]
        tops.append(jnp.where(left8, one, pltpu.roll(two, CAP, 1)))
        bottoms.append(jnp.where(left8, pltpu.roll(one, CAP, 1), two))
        one, two = got_ref[s, 24:32, :], got_ref[s + 1, 24:32, :]
        xs.append(jnp.where(left8, one, pltpu.roll(two, CAP, 1))[2:3])
        ys.append(jnp.where(left8, pltpu.roll(one, CAP, 1), two)[2:3])
    lower, upper = jnp.concatenate(tops, axis=1), jnp.concatenate(bottoms, axis=1)
    x0, y0 = jnp.concatenate(xs, axis=1), jnp.concatenate(ys, axis=1)
    arrived = x0.shape[1]
    hot = (iota((tile_x, arrived), 0).astype(F32) == x0).astype(F32).astype(BF16)
    from_y = iota((tile_y, arrived), 0).astype(F32) - y0
    total = jnp.zeros((tile_x, tile_y), F32)
    for pr in range(patch_side):
        source = lower if pr < 2 else upper
        value = jnp.zeros((tile_y, arrived), F32)
        for pc in range(patch_side):
            at = (pr * patch_side + pc) % 8
            value = jnp.where(from_y == pc, source[at : at + 1], value)
        got = sum(
            lax.dot_general(hot, part, NT, preferred_element_type=F32) for part in parts(value)
        )
        total += got if pr == 0 else pltpu.roll(got, pr, 0)
    forcing_ref[:, :tile_y] = total
    near = jnp.concatenate([got_ref[s, 0:POINTS, :] for s in range(tiles)], axis=1)
    x0 = jnp.concatenate([got_ref[s, 24:25, :] for s in range(tiles)], axis=1)
    y0 = jnp.concatenate([got_ref[s, 25:26, :] for s in range(tiles)], axis=1)
    arrived = x0.shape[1]
    hot = (iota((tile_x, arrived), 0).astype(F32) == x0).astype(F32).astype(BF16)
    rows = iota((8, arrived), 0)
    before = iota((8, arrived), 1) % (2 * CAP) < CAP
    high_y = jnp.where(before & (rows >= 6), (rows + (tile_y - 8)).astype(F32) - y0, -1.0)
    low_y = jnp.where(before | (rows >= 2), -1.0, rows.astype(F32) - y0)
    chunks = [None] * 16
    for pr in range(patch_side):
        high, low = jnp.zeros((8, arrived), F32), jnp.zeros((8, arrived), F32)
        for pc in range(patch_side):
            at = pr * patch_side + pc
            high = jnp.where(high_y == pc, near[at : at + 1], high)
            low = jnp.where(low_y == pc, near[at : at + 1], low)
        chunks[(4 * pr - 1) % 16], chunks[4 * pr] = high, low
    blank = jnp.zeros((8, arrived), F32)
    value = jnp.concatenate([blank if c is None else c for c in chunks], axis=0)
    got = sum(lax.dot_general(hot, part, NT, preferred_element_type=F32) for part in parts(value))
    lane = iota((tile_x, 128), 1)
    used = (lane < 2) | (lane >= 126)
    total = jnp.where(used, got, 0.0)
    for pr in range(1, patch_side):
        moved_back = pltpu.roll(pltpu.roll(got, 128 - 32 * pr, 1), pr, 0)
        total += jnp.where(used, moved_back, 0.0)
    forcing_ref[:, tile_y:] = total
    a1, _ = unequal(place)
    head, tail = forcing_ref[0:8, :], forcing_ref[tile_x - 8 : tile_x, :]
    tail = pltpu.roll(tail, 2, 0)
    s1_ref[...] = jnp.where(a1 > 0, tail, head)
    s2_ref[...] = jnp.where(a1 > 0, head, tail)


def edge_rows(place, heads, tails, p1_ref, p2_ref):
    a1, _ = unequal(place)
    for i in range(4):
        head, tail = heads[i, 0:2, :], tails[i, 6:8, :]
        one = jnp.where(a1 > 0, tail, head)
        two = jnp.where(a1 > 0, head, tail)
        for h in range(2):
            at = slice(3 * HALF + 4 * i + 2 * h, 3 * HALF + 4 * i + 2 * h + 2)
            lanes = slice(128 * h, 128 * (h + 1))
            p1_ref[at, :] = one[:, lanes]
            p2_ref[at, :] = two[:, lanes]


def edge_columns(place, depth_ref, momentum_ref, bottom_ref, one_ref, two_ref):
    arrays = [depth_ref[...], momentum_ref[0], momentum_ref[1], bottom_ref[...]]
    _, c1 = unequal(place)
    tile_y = depth_ref.shape[1]
    row = iota((8, tile_y), 0)
    up = jnp.where(row < 2, row + (tile_y - 2), row - 2)
    down = jnp.where(row < 2, row, row + (tile_y - 4))
    wanted = jnp.where(c1 > 0, up, down)
    hot = ((row < 4) & (wanted == iota((8, tile_y), 1))).astype(F32)
    for i, array in enumerate(arrays):
        columns = lax.dot_general(
            hot, array, NT, preferred_element_type=F32, precision=lax.Precision.HIGHEST
        )
        for h in range(2):
            at = slice(4 * i + 2 * h, 4 * i + 2 * h + 2)
            lanes = slice(128 * h, 128 * (h + 1))
            one_ref[at, :] = columns[0:2, lanes]
            two_ref[at, :] = columns[2:4, lanes]


def volume_and_columns(place, *refs):
    solid, water, (base_ref, one_ref, two_ref, spread_ref) = refs[:5], refs[5:8], refs[8:]
    volume(*solid, base_ref, spread_ref)
    edge_columns(place, *water, one_ref, two_ref)


def widened(place, depth_ref, momentum_ref, bottom_ref, p1_ref, p2_ref, q1_ref, q2_ref, out_ref):
    tile_x, tile_y = depth_ref.shape
    a1, c1 = unequal(place)
    arrays = [depth_ref[...], momentum_ref[0], momentum_ref[1], bottom_ref[...]]
    p1, p2 = p1_ref[3 * HALF :, :], p2_ref[3 * HALF :, :]
    q1, q2 = q1_ref[3 * HALF :, :], q2_ref[3 * HALF :, :]
    is_below, is_above = place[0] > 0, place[0] < place[2] - 1
    below = jnp.where(is_below, jnp.where(a1 > 0, p2, p1), 0.0)
    above = jnp.where(is_above, jnp.where(a1 > 0, p1, p2), 0.0)
    before = jnp.where(place[1] > 0, jnp.where(c1 > 0, q2, q1), 0.0)
    after = jnp.where(place[1] < place[3] - 1, jnp.where(c1 > 0, q1, q2), 0.0)
    n = OCEAN_ROWS

    def ends(rows):
        one, two = rows[n : n + 8], rows[n + 8 :]
        return (
            jnp.where(is_below, jnp.where(a1 > 0, two, one), 0.0),
            jnp.where(is_above, jnp.where(a1 > 0, one, two), 0.0),
        )

    before_below, before_above = ends(before)
    after_below, after_above = ends(after)
    lane = iota((2, 128), 1)
    low, high = lane < 2, lane >= 126
    for i, array in enumerate(arrays):
        first, second = slice(4 * i, 4 * i + 2), slice(4 * i + 2, 4 * i + 4)
        out_ref[i, 0:MARGIN, :] = jnp.zeros((MARGIN, tile_y + 128), F32)
        out_ref[i, MARGIN + tile_x :, :] = jnp.zeros((MARGIN, tile_y + 128), F32)
        out_ref[i, MARGIN : MARGIN + tile_x, :tile_y] = array
        for at, rows, left, right in (
            (MARGIN - 2, below, before_below, after_below),
            (MARGIN + tile_x, above, before_above, after_above),
        ):
            out_ref[i, at : at + 2, 0:128] = rows[first]
            out_ref[i, at : at + 2, 128:256] = rows[second]
            end = slice(2 * i, 2 * i + 2)
            corner = jnp.where(low, right[end], jnp.where(high, left[end], 0.0))
            out_ref[i, at : at + 2, 256:384] = corner
        start = jnp.concatenate([after[first], after[second]], axis=1)
        finish = jnp.concatenate([before[first], before[second]], axis=1)
        columns = jnp.concatenate([start, jnp.zeros((124, tile_x), F32), finish], axis=0)
        out_ref[i, MARGIN : MARGIN + tile_x, tile_y:] = columns.T


STRIP = 16


def next_of(x):
    return pltpu.roll(x, x.shape[1] - 1, 1)


def previous_of(x):
    return pltpu.roll(x, 1, 1)


def cells(state, cell, low, high):
    for at in range(low, high, 8):
        here = slice(at, at + 8)
        h, mx, my = state[0, here, :], state[1, here, :], state[2, here, :]
        safe = jnp.maximum(h, depth_floor)
        root = lax.rsqrt(safe)
        inverse = root * root
        c = safe * root
        u, v = mx * inverse, my * inverse
        half = 0.5 * h * h
        cell[0, here, :] = mx * u + half
        cell[1, here, :] = my * u
        cell[2, here, :] = my * v + half
        cell[3, here, :] = 0.5 * (jnp.abs(u) + c)
        cell[4, here, :] = 0.5 * (jnp.abs(v) + c)


def moved(state, cell, face, at, rows):
    here, up = slice(at, at + rows), slice(at + 1, at + rows + 1)
    below = slice(at - 1, at + rows - 1)
    now = [state[k, here, :] for k in range(3)]
    cross = cell[1, here, :]
    next_now = [state[k, up, :] for k in range(3)]
    wave = jnp.maximum(cell[3, here, :], cell[3, up, :])
    pairs = ((now[1], next_now[1]), (cell[0, here, :], cell[0, up, :]), (cross, cell[1, up, :]))
    upper = [
        0.5 * (pairs[k][0] + pairs[k][1]) - wave * (next_now[k] - now[k]) for k in range(3)
    ]
    for k in range(3):
        face[k, here, :] = upper[k]
    flux = (now[2], cross, cell[2, here, :])
    speed = cell[4, here, :]
    wave = jnp.maximum(speed, next_of(speed))
    next_now = [next_of(x) for x in now]
    next_flux = (next_now[2], next_of(flux[1]), next_of(flux[2]))
    y_face = [
        0.5 * (flux[k] + next_flux[k]) - wave * (next_now[k] - now[k]) for k in range(3)
    ]
    return [
        now[k] - step_ocean * (upper[k] - face[k, below, :] + y_face[k] - previous_of(y_face[k]))
        for k in range(3)
    ]


def sloped(height, bed, at, rows):
    b = bed[at : at + rows, :]
    slope_x = 0.5 * (bed[at + 1 : at + rows + 1, :] - bed[at - 1 : at + rows - 1, :])
    slope_y = 0.5 * (next_of(b) - previous_of(b))
    scale = step_ocean * height
    return scale * slope_x, scale * slope_y


def ocean_first(
    place, depth_ref, momentum_ref, bottom_ref, p1_ref, p2_ref, q1_ref, q2_ref, wide, state, cell, face
):
    tile_x, tile_y = depth_ref.shape
    widened(place, depth_ref, momentum_ref, bottom_ref, p1_ref, p2_ref, q1_ref, q2_ref, wide)
    cells(wide, cell, 8, cell.shape[1] - 8)
    height, span = wide.shape[1:]
    lane = iota((STRIP, span), 1)
    outside = ((lane == span - 1) & (place[1] == 0)) | (
        (lane == tile_y) & (place[1] == place[3] - 1)
    )
    state[:, 0:8, :] = jnp.zeros((3, 8, span), F32)
    state[:, height - 8 :, :] = jnp.zeros((3, 8, span), F32)
    face[:, 0:8, :] = jnp.zeros((3, 8, span), F32)
    for at in range(8, height - 8, STRIP):
        new = moved(wide, cell, face, at, STRIP)
        row = iota((STRIP, span), 0) + at
        out = outside | ((row < MARGIN) & (place[0] == 0))
        out = out | ((row >= MARGIN + tile_x) & (place[0] == place[2] - 1))
        for k in range(3):
            state[k, at : at + STRIP, :] = jnp.where(out, 0.0, new[k])


def second_step(wide, first, bed, state, cell, face, rows, put, raise_bed):
    low, high = rows.start - 8, rows.stop + 8
    raise_bed(wide.at[3])
    for at in range(low, high, STRIP):
        here = slice(at, at + STRIP)
        change_x, change_y = sloped(wide[0, here, :], bed, at, STRIP)
        state[0, here, :] = first[0, here, :]
        state[1, here, :] = first[1, here, :] - change_x
        state[2, here, :] = first[2, here, :] - change_y
    cells(state, cell, low, high)
    raise_bed(bed)
    moved(state, cell, face, low, 8)
    for at in range(rows.start, rows.stop, STRIP):
        new = moved(state, cell, face, at, STRIP)
        change_x, change_y = sloped(state[0, at : at + STRIP, :], bed, at, STRIP)
        new[1] -= change_x
        new[2] -= change_y
        put(at, new)


def ocean_inner(wide, first, forcing_ref, out_ref, bed_ref, state, bed, cell, face):
    tile_x, tile_y = bed_ref.shape
    inner = slice(MARGIN, MARGIN + tile_x)
    bed[...] = wide[3]

    def raise_bed(source):
        bed[inner, :] = source[inner, :] + step_ocean * forcing_ref[...]

    def put(at, new):
        for k in range(3):
            out_ref[k, at - MARGIN : at - MARGIN + STRIP, :] = new[k][:, :tile_y]

    rows = slice(MARGIN + STRIP, MARGIN + tile_x - STRIP)
    second_step(wide, first, bed, state, cell, face, rows, put, raise_bed)
    bed_ref[...] = bed[inner, :tile_y]


def ocean_ends(
    place, wide, first, forcing_ref, s1_ref, s2_ref, inner_ref, raised_ref, out_hbm, bed_hbm,
    out_ref, bed_ref, sems, state, bed, cell, face,
):
    tile_x, tile_y = raised_ref.shape
    last = tile_x - STRIP
    middle = pl.ds(STRIP, tile_x - 2 * STRIP)
    copies = [
        pltpu.make_async_copy(raised_ref, bed_hbm, sems.at[0]),
        pltpu.make_async_copy(inner_ref.at[:, middle], out_hbm.at[:, middle], sems.at[1]),
    ]
    for copy in copies:
        copy.start()
    a1, _ = unequal(place)
    force_lo = step_ocean * jnp.where(a1 > 0, s2_ref[...], s1_ref[...])[0:2]
    force_lo = jnp.where(place[0] > 0, force_lo, 0.0)
    force_hi = step_ocean * jnp.where(a1 > 0, s1_ref[...], s2_ref[...])[0:2]
    force_hi = jnp.where(place[0] < place[2] - 1, force_hi, 0.0)

    def put(at, new):
        for k in range(3):
            out_ref[k, at - MARGIN : at - MARGIN + STRIP, :] = new[k][:, :tile_y]

    for n, start in enumerate((MARGIN, MARGIN + last)):
        outer = slice(start - 16, start) if n == 0 else slice(start + STRIP, start + STRIP + 16)
        edge = slice(MARGIN - 2, MARGIN) if n == 0 else slice(MARGIN + tile_x, MARGIN + tile_x + 2)
        force = force_lo if n == 0 else force_hi
        own = slice(start, start + 32) if n == 0 else slice(start - 16, start + 16)
        forcing = forcing_ref[own.start - MARGIN : own.stop - MARGIN, :]
        bed[outer, :] = wide[3, outer, :]

        def raise_bed(source):
            bed[own, :] = source[own, :] + step_ocean * forcing
            bed[edge, :] = source[edge, :] + force

        second_step(
            wide, first, bed, state, cell, face, slice(start, start + STRIP), put, raise_bed
        )
        at = pl.ds(start - MARGIN, STRIP)
        copies.append(pltpu.make_async_copy(out_ref.at[:, at], out_hbm.at[:, at], sems.at[2 + n]))
        copies[-1].start()
    for copy in copies:
        copy.wait()


def call(
    body, out_shape, *args, place=None, scratch=(), held=0, sent=0, copies=0, limit=VMEM_LIMIT
):
    out_space = [pltpu.HBM if i < sent else pltpu.VMEM for i in range(len(out_shape))]
    specs = [pl.BlockSpec(memory_space=pltpu.HBM if held else pltpu.VMEM) for _ in args]
    shapes = [
        s if isinstance(s, jax.ShapeDtypeStruct) else jax.ShapeDtypeStruct(s, F32) for s in out_shape
    ]
    scratch = [pltpu.VMEM(s, F32) for s in scratch]
    if copies:
        scratch = [pltpu.SemaphoreType.DMA((copies,))] + scratch
    scratch = [pltpu.VMEM(x.shape, x.dtype) for x in [*args[:held], *shapes[:sent]]] + scratch
    if place is not None:
        sizes, inner = place, body

        def body(*refs):
            here = (lax.axis_index("gx"), lax.axis_index("gy"))
            inner(here + sizes, *refs)

    return pl.pallas_call(
        body,
        out_shape=shapes,
        in_specs=specs,
        out_specs=[pl.BlockSpec(memory_space=space) for space in out_space],
        scratch_shapes=scratch,
        compiler_params=pltpu.CompilerParams(vmem_limit_bytes=limit),
    )(*args)


def swap(block, axis, parity, wrap=False):
    count = lax.axis_size(axis)
    last = count + parity - 1 if wrap else count - 1
    pairs = []
    for i in range(parity, last, 2):
        pairs += [(i, (i + 1) % count), ((i + 1) % count, i)]
    taken = {source for source, _ in pairs}
    pairs += [(i, i) for i in range(count) if i not in taken]
    return lax.ppermute(block, axis, pairs)


def per_device(
    coefficients,
    jacobian,
    face_normals,
    wave_speed,
    star_mats,
    deriv_mats,
    stiff_mats,
    source_mat,
    trace_mats,
    lift_mats,
    face_partner,
    send_faces,
    sea_face,
    sea_row,
    sea_base,
    interp_mat,
    water_depth,
    momentum,
    bottom,
):
    basis, elements = coefficients.shape[1:]
    rows = FIELDS * basis
    tile_x, tile_y = water_depth.shape
    tiles = lax.axis_size("gy")
    place = (lax.axis_size("gx"), tiles)
    speed = wave_speed.reshape(1, elements)
    traces = trace_mats.transpose(1, 0, 2)
    normals = face_normals.transpose(1, 0, 2)
    lifts = lift_mats.transpose(2, 0, 1)
    spread = (FIELDS, 3 * basis, elements)
    faces = (TABLE, 4 * elements)
    solid = (rows, elements)
    wide_shape = (tile_x + 2 * MARGIN, tile_y + 128)
    state = coefficients.reshape(solid)
    packed = (2 * HALF, 8 * CAP)
    flux_shape = (FIELDS, 4 * FACE_PAD, elements)
    for section in range(2):
        scratch = [spread, solid, solid, solid, (2 * HALF, 4 * CAP)]
        if section == 0:
            fixed = (state, jacobian, star_mats, source_mat, deriv_mats, traces, send_faces)
            buffers = [(3 * HALF + OCEAN_ROWS, 128)] * 2 + [(HALF, 128)] * 2
            integral, table, p1, p2, own1, own2 = call(
                start, [solid, faces] + buffers, *fixed, water_depth, momentum, bottom,
                place=place, scratch=[(4, 8, tile_y)] * 2 + scratch,
                held=len(fixed), sent=6, copies=len(fixed) + 14, limit=START_LIMIT,
            )
        else:
            buffers = [(3 * HALF, 128)] * 2 + [(HALF, 128)] * 2
            integral, table, p1, p2, own1, own2 = call(
                front_again, [solid, faces] + buffers,
                state, jacobian, star4, *derivs, *traced, send_faces, place=place, scratch=scratch,
            )
        p2, p1 = swap(p2, "gx", 1), swap(p1, "gx", 0)
        inside = (state, jacobian, star_mats, stiff_mats, integral)
        if section == 0:
            base, *columns = call(
                volume_and_columns, [solid] + [(OCEAN_ROWS, 128)] * 2,
                *inside, water_depth, momentum, bottom,
                place=place, scratch=[spread],
            )
            size = 3 * HALF + 2 * OCEAN_ROWS
        else:
            (base,) = call(volume, [solid], *inside, scratch=[spread])
            columns, size = [], 3 * HALF
        p1, p2, base = lax.optimization_barrier((p1, p2, base))
        q1, q2 = call(forward, [(size, 128)] * 2, p1, p2, own1, own2, *columns, place=place)
        q2, q1 = swap(q2, "gy", 1), swap(q1, "gy", 0)
        if section == 1:
            wide, first = call(
                ocean_first,
                [(4,) + wide_shape, (3,) + wide_shape],
                water_depth, momentum, bottom, *halos,
                place=place, scratch=[(5,) + wide_shape, (3,) + wide_shape],
            )
            (flux,) = call(
                local_flux, [flux_shape], table, face_partner, normals, speed, star3,
                scratch=[faces],
            )
            q1, q2, flux, wide, first = lax.optimization_barrier((q1, q2, flux, wide, first))
        else:
            half = lambda *shape: jax.ShapeDtypeStruct(shape, BF16)
            size, sea = FIELDS * 8, sea_face.shape[0]
            star4, star3, *ready = call(
                prepared,
                [half(8 * size, 2 * size), half(6 * size, 2 * size)]
                + [half(2 * basis, 3 * basis), half(basis, 3 * basis)]
                + [half(4 * FACE_PAD, 3 * basis)]
                + [half(2 * basis, 4 * FACE_PAD), half(basis, 4 * FACE_PAD)]
                + [half(8 * CAP, 4 * elements), half(4 * elements, sea), half(tiles, 4 * CAP, sea), (8, 8 * CAP)],
                star_mats, source_mat, deriv_mats, traces, lifts, face_partner,
                sea_face.reshape(1, -1), sea_row.T, normals, speed,
                place=place,
            )
            (flux,) = call(
                local_flux, [flux_shape], table, face_partner, normals, speed, star3,
                scratch=[faces],
            )
            q1, q2, flux, *ready = lax.optimization_barrier((q1, q2, flux, *ready))
            derivs, traced, lifting, (hot, sea_hot, slot_hot, scales) = (
                ready[0:2], ready[2:3], ready[3:5], ready[5:],
            )
        fixed = (star3, *lifting, hot, scales)
        arrived = (p1, p2, q1, q2)
        remote = (TABLE, 8 * CAP)
        if section == 0:
            (state,) = call(
                back, [solid], base, flux, *fixed, *arrived,
                place=place, scratch=[flux_shape, packed, remote],
            )
            halos = (p1, p2, q1, q2)
        else:
            state, outgoing = call(
                finish,
                [solid, (tiles, 32, 128)],
                base, flux, *fixed, *arrived,
                *traced, interp_mat, sea_base.T, sea_hot, slot_hot,
                place=place, scratch=[flux_shape, packed, remote], sent=1, copies=1,
            )
    incoming = lax.all_to_all(outgoing, "gy", split_axis=0, concat_axis=0, tiled=True)
    forcing, s1, s2 = call(
        forced,
        [(tile_x, tile_y + 128), (8, tile_y + 128), (8, tile_y + 128)],
        incoming,
        place=place,
    )
    s2, s1 = swap(s2, "gx", 1, wrap=True), swap(s1, "gx", 0)
    scratch = [(3,) + wide_shape, wide_shape, (5,) + wide_shape, (3,) + wide_shape]
    water = [(3, tile_x, tile_y), (tile_x, tile_y)]
    inner, raised = call(ocean_inner, water, wide, first, forcing, scratch=scratch)
    ocean_final, bed_final = call(
        ocean_ends, water, wide, first, forcing, s1, s2, inner, raised,
        place=place, scratch=scratch, sent=2, copies=4,
    )
    return (state.reshape(coefficients.shape), ocean_final, bed_final)


def solution(mesh):
    in_specs = (
        P(None, None, ("gx", "gy")),
        P(None, None, ("gx", "gy")),
        P(None, None, ("gx", "gy")),
        P(("gx", "gy")),
        P(),
        P(),
        P(),
        P(),
        P(),
        P(),
        P(None, ("gx", "gy")),
        P(None, ("gx", "gy")),
        P(("gx", "gy")),
        P(("gx", "gy"), None),
        P(("gx", "gy"), None),
        P(),
        P("gx", "gy"),
        P(None, "gx", "gy"),
        P("gx", "gy"),
    )
    out_specs = (P(None, None, ("gx", "gy")), P(None, "gx", "gy"), P("gx", "gy"))
    return jax.shard_map(
        per_device, mesh=mesh, in_specs=in_specs, out_specs=out_specs, check_vma=False
    )
```

```python
import jax
import jax.numpy as jnp
from jax import lax
from jax.experimental import pallas as pl
from jax.experimental.pallas import tpu as pltpu
from jax.sharding import PartitionSpec as P

FIELDS = 13
FACE_BASIS = 21
FACE_PAD = 24
POINTS = 16
ORD = 3
STEPS_OCEAN = 2
CAP = 64
TABLE = FIELDS * FACE_PAD
WIDE = 320
HALF = (FIELDS * FACE_BASIS + 1) // 2
OCEAN_ROWS = 16
MARGIN = 16
FOUR = 4

step_solid = 0.4
step_ocean = 0.2
depth_floor = 0.5
vertical_field = 6
patch_side = 4

F32 = jnp.float32
BF16 = jnp.bfloat16
NT = (((1,), (1,)), ((), ()))
VMEM_LIMIT = 24 * 1024 * 1024
START_LIMIT = 62 * 1024 * 1024


def iota(shape, dim):
    return lax.broadcasted_iota(jnp.int32, shape, dim)


def dot(a, b):
    return jnp.dot(a, b, preferred_element_type=F32)


def exact_dot(a, b):
    return jnp.dot(a, b, preferred_element_type=F32, precision=lax.Precision.HIGHEST)


def parts(x):
    high = x.astype(BF16)
    low = (x - high.astype(F32)).astype(BF16)
    return high, low


def both_parts(x):
    high = x.astype(BF16).astype(F32)
    return jnp.concatenate([high, x - high], axis=0).astype(BF16)


def folded(y):
    half = y.shape[0] // 2
    return y[:half] + y[half:]


def weights(w):
    return both_parts(w), w.astype(BF16)


def weighted(stack, high, x):
    x_high, x_low = parts(x)
    return folded(dot(stack, x_high)) + dot(high, x_low)


def side_weights(w):
    columns = w.shape[1]
    high, low = parts(w)
    place = [selector(columns, 3 * columns, i * columns).astype(BF16) for i in range(3)]
    return (dot(high, place[0] + place[1]) + dot(low, place[2])).astype(BF16)


def side_weighted(stack, x):
    high = x.astype(BF16).astype(F32)
    return dot(stack, jnp.concatenate([high, x - high, high], axis=0).astype(BF16))


def selector(rows, columns, shift):
    return (iota((rows, columns), 1) == iota((rows, columns), 0) + shift).astype(F32)


def star_weights(mats):
    size = FIELDS * 8
    spread = ((iota((FIELDS, 2 * size), 1) % size) // 8 == iota((FIELDS, 2 * size), 0)).astype(F32)
    diagonal = iota((size, 2 * size), 0) % 8 == iota((size, 2 * size), 1) % 8
    first = iota((size, 2 * size), 1) < size
    high, low = [], []
    for mat in mats:
        wide = exact_dot(mat, spread)
        tall = jnp.concatenate(
            [jnp.broadcast_to(wide[g : g + 1], (8, 2 * size)) for g in range(FIELDS)], axis=0
        )
        tall = jnp.where(diagonal, tall, 0.0)
        top = tall.astype(BF16).astype(F32)
        high.append(top)
        low.append(jnp.where(first, tall - top, 0.0))
    return jnp.concatenate(high + low, axis=0).astype(BF16)


def side_by_side(mats):
    rows, columns = mats[0].shape
    total = len(mats) * columns
    return sum(exact_dot(m, selector(columns, total, i * columns)) for i, m in enumerate(mats))


def stacked_traces(trace_ref):
    place = (
        iota((FACE_PAD, FACE_BASIS), 0) == iota((FACE_PAD, FACE_BASIS), 1)
    ).astype(F32)
    return jnp.concatenate([exact_dot(place, trace_ref[:, f, :]) for f in range(4)], axis=0)


def star_quarters(mats):
    size = FOUR * (FIELDS + FIELDS % 2)
    columns = 3 * size
    spread = ((iota((FIELDS, columns), 1) % size) // FOUR == iota((FIELDS, columns), 0)).astype(F32)
    upper = iota((8, columns), 0) < FOUR
    diagonal = iota((size, columns), 0) % FOUR == iota((size, columns), 1) % FOUR
    first = iota((size, columns), 1) < 2 * size
    out = []
    for mat in mats:
        wide = exact_dot(mat, spread)
        wide = [jnp.broadcast_to(wide[g : g + 1], (8, columns)) for g in range(FIELDS)]
        wide += [jnp.zeros((8, columns), F32)] * (FIELDS % 2)
        tall = jnp.concatenate(
            [jnp.where(upper, wide[g], wide[g + 1]) for g in range(0, FIELDS, 2)], axis=0
        )
        tall = jnp.where(diagonal, tall, 0.0)
        high = tall.astype(BF16).astype(F32)
        out.append(jnp.where(first, high, tall - high))
    return jnp.concatenate(out, axis=0).astype(BF16)


def interleaved(one, two, upper):
    return jnp.where(upper, one, pltpu.roll(two, FOUR, 0)), jnp.where(
        upper, pltpu.roll(one, FOUR, 0), two
    )


def spread_out(source, jac_ref, star, target, extra=None):
    basis = target.shape[1] // 3
    lanes = target.shape[2]
    pairs = (FIELDS + 1) // 2
    size = 8 * pairs
    upper = iota((8, lanes), 0) < FOUR
    for j in range(basis // 8):
        x = [source[g * basis + 8 * j : g * basis + 8 * j + 8, :] for g in range(FIELDS)]
        x += [jnp.zeros((8, lanes), F32)] * (2 * pairs - FIELDS)
        mixed = [interleaved(x[2 * p], x[2 * p + 1], upper) for p in range(pairs)]
        halves = []
        for half in range(2):
            y = side_weighted(star, jnp.concatenate([m[half] for m in mixed], axis=0))
            z = [
                sum(jac_ref[d, c : c + 1, :] * y[c * size : (c + 1) * size] for c in range(3))
                for d in range(3)
            ]
            halves.append(z + ([] if extra is None else [y[3 * size :]]))
        for d, (one, two) in enumerate(zip(*halves)):
            for p in range(pairs):
                rows = slice(8 * p, 8 * p + 8)
                for g, value in zip(
                    range(2 * p, FIELDS), interleaved(one[rows], two[rows], upper)
                ):
                    if d < 3:
                        target[g, d * basis + 8 * j : d * basis + 8 * j + 8, :] = value
                    else:
                        extra[g * basis + 8 * j : g * basis + 8 * j + 8, :] = value


def derivative(source, target, jac_ref, star, basis_weights, spread_ref, relaxed_ref):
    basis = spread_ref.shape[1] // 3
    spread_out(source, jac_ref, star, spread_ref, relaxed_ref)
    for g in range(FIELDS):
        rows = slice(g * basis, (g + 1) * basis)
        target[rows, :] = -(weighted(*basis_weights, spread_ref[g]) + relaxed_ref[rows, :])


def unequal(place):
    a1 = jnp.where(place[0] % 2 == 0, 1, -1)
    c1 = jnp.where(place[1] % 2 == 0, 1, -1)
    return a1, c1


def column_block(a):
    return jnp.where(a > 0, 6, 1)


def row_block(c):
    return jnp.where(c > 0, 4, 3)


def front_weights(star_ref, source_ref, deriv_ref, trace_ref, ready=lambda *numbers: None):
    ready(2, 3)
    star = star_quarters([star_ref[0], star_ref[1], star_ref[2], source_ref[...]])
    ready(4, 5)
    basis_weights = weights(side_by_side([deriv_ref[d] for d in range(3)]))
    return star, basis_weights, side_weights(stacked_traces(trace_ref))


def front_again(place, q_ref, jac_ref, star_ref, b1_ref, b2_ref, trace_ref, *refs):
    held = star_ref[...], (b1_ref[...], b2_ref[...]), trace_ref[...]
    front(place, held, q_ref, jac_ref, *refs)


def front(
    place, held, q_ref, jac_ref, send_ref,
    integral_ref, table_ref, p1_ref, p2_ref, own1_ref, own2_ref,
    spread_ref, relaxed_ref, d1_ref, d2_ref, packed_ref, ready=lambda *numbers: None, made=lambda *numbers: None,
):
    elements = q_ref.shape[1]
    basis = q_ref.shape[0] // FIELDS
    star, basis_weights, trace = held
    ready(0, 1)
    derivative(q_ref, d1_ref, jac_ref, star, basis_weights, spread_ref, relaxed_ref)
    derivative(d1_ref, d2_ref, jac_ref, star, basis_weights, spread_ref, relaxed_ref)
    first = step_solid
    second = first * step_solid / 2
    third = second * step_solid / 3
    for g in range(FIELDS):
        rows = slice(g * basis, (g + 1) * basis)
        whole = first * q_ref[rows, :] + second * d1_ref[rows, :] + third * d2_ref[rows, :]
        integral_ref[rows, :] = whole
        faces = side_weighted(trace, whole)
        for f in range(4):
            table_ref[g * FACE_PAD : (g + 1) * FACE_PAD, f * elements : (f + 1) * elements] = faces[
                f * FACE_PAD : (f + 1) * FACE_PAD
            ]
    made(0, 1)
    ready(6)
    a1, c1 = unequal(place)
    picks = [
        (p1_ref, 0, column_block(a1)),
        (p2_ref, 0, column_block(-a1)),
        (p1_ref, HALF, column_block(a1) + c1),
        (p1_ref, 2 * HALF, column_block(a1) - c1),
        (p2_ref, HALF, column_block(-a1) + c1),
        (p2_ref, 2 * HALF, column_block(-a1) - c1),
        (own1_ref, 0, row_block(c1)),
        (own2_ref, 0, row_block(-c1)),
    ]
    stack = table_parts(table_ref)
    left = iota((HALF, 2 * CAP), 1) < CAP
    codes = iota((4 * elements, 4 * CAP), 0)
    packed_ref[FIELDS * FACE_BASIS :, :] = jnp.zeros((2 * HALF - FIELDS * FACE_BASIS, 4 * CAP), F32)
    for n in range(0, 8, 4):
        wanted = jnp.concatenate([send_ref[pl.ds(pick[2], 1), :] for pick in picks[n : n + 4]], axis=1)
        got = folded(dot(stack, (codes == wanted).astype(F32).astype(BF16)))
        pack(got, packed_ref)
        for pair in range(2):
            lanes = slice(pair * 2 * CAP, (pair + 1) * 2 * CAP)
            low, high = packed_ref[0:HALF, lanes], packed_ref[HALF:, lanes]
            ref, at, _ = picks[n + 2 * pair]
            ref[at : at + HALF, :] = jnp.where(left, low, pltpu.roll(high, CAP, 1))
            ref, at, _ = picks[n + 2 * pair + 1]
            ref[at : at + HALF, :] = jnp.where(left, pltpu.roll(low, CAP, 1), high)


def pack(table, packed_ref):
    rest = FACE_BASIS - 16
    for g in range(FIELDS):
        packed_ref[16 * g : 16 * (g + 1), :] = table[FACE_PAD * g : FACE_PAD * g + 16]
        at = 16 * FIELDS + rest * g
        packed_ref[at : at + rest, :] = table[FACE_PAD * g + 16 : FACE_PAD * g + FACE_BASIS]


def unpack(packed_ref, table_ref):
    rest = FACE_BASIS - 16
    for g in range(FIELDS):
        table_ref[FACE_PAD * g : FACE_PAD * g + 16, :] = packed_ref[16 * g : 16 * (g + 1), :]
        at = 16 * FIELDS + rest * g
        last = FACE_PAD * g + 16
        table_ref[last : last + 8, :] = jnp.zeros((8, table_ref.shape[1]), F32)
        table_ref[last : last + rest, :] = packed_ref[at : at + rest, :]


def start(place, *refs):
    sources, water, refs = refs[:7], refs[7:10], refs[10:]
    targets, refs = refs[:6], refs[6:]
    held, outs, (sems, heads, tails, *scratch) = refs[:7], refs[7:13], refs[13:]
    depth, momentum, bottom = water
    last = depth.shape[0] - 8
    pairs = [(sources[i], held[i]) for i in range(7)]
    for rows, target in ((pl.ds(0, 8), heads), (pl.ds(last, 8), tails)):
        pairs += [
            (depth.at[rows], target.at[0]),
            (momentum.at[0, rows], target.at[1]),
            (momentum.at[1, rows], target.at[2]),
            (bottom.at[rows], target.at[3]),
        ]
    first_out = len(pairs)
    pairs += list(zip(outs, targets))
    copies = [pltpu.make_async_copy(a, b, sems.at[i]) for i, (a, b) in enumerate(pairs)]
    for copy in copies[:first_out]:
        copy.start()

    def ready(*numbers):
        for i in numbers:
            copies[i].wait()

    def made(*numbers):
        for i in numbers:
            copies[first_out + i].start()

    ready_weights = front_weights(*held[2:6], ready=ready)
    front(place, ready_weights, *held[:2], held[6], *outs, *scratch, ready=ready, made=made)
    ready(*range(7, first_out))
    edge_rows(place, heads, tails, *outs[2:4])
    made(2, 3, 4, 5)
    ready(*range(first_out, len(copies)))


def table_parts(table_ref):
    pad = jnp.zeros((WIDE - TABLE, table_ref.shape[1]), BF16)
    high, low = parts(table_ref[...])
    both = [high.astype(F32), pad.astype(F32), low.astype(F32), pad.astype(F32)]
    return jnp.concatenate(both, axis=0).astype(BF16)


def volume(q_ref, jac_ref, star_ref, stiff_ref, integral_ref, base_ref, spread_ref):
    basis = stiff_ref.shape[1]
    star = star_quarters([star_ref[0], star_ref[1], star_ref[2]])
    basis_weights = weights(side_by_side([stiff_ref[d] for d in range(3)]))
    spread_out(integral_ref, jac_ref, star, spread_ref)
    for g in range(FIELDS):
        rows = slice(g * basis, (g + 1) * basis)
        base_ref[rows, :] = q_ref[rows, :] + weighted(*basis_weights, spread_ref[g])


def forward(place, p1_ref, p2_ref, *refs):
    outs = refs[-2:]
    _, c1 = unequal(place)
    for n, out in enumerate(outs):
        at = slice((n + 1) * HALF, (n + 2) * HALF)
        out[0:HALF, :] = p1_ref[at, :]
        out[HALF : 2 * HALF, :] = p2_ref[at, :]
        out[2 * HALF : 3 * HALF, :] = refs[n][...]
        if len(refs) > 4:
            at = 3 * HALF + OCEAN_ROWS
            out[3 * HALF : at, :] = refs[2 + n][...]
            for p_ref in (p1_ref, p2_ref):
                rows = p_ref[3 * HALF :, :]
                for i in range(4):
                    low, high = rows[4 * i : 4 * i + 2], rows[4 * i + 2 : 4 * i + 4]
                    ends = (high, low) if n == 0 else (low, high)
                    out[at : at + 2, :] = jnp.where(c1 > 0, *ends)
                    at += 2


def star_flux(star, normals, speed, inner, outer):
    size = FIELDS * 8
    y = folded(dot(star, both_parts(inner + outer)))
    flux = speed * (inner - outer)
    for c in range(3):
        flux = flux + normals[c] * y[c * size : (c + 1) * size]
    return flux


def local_flux(table_ref, partner_ref, normal_ref, speed_ref, star_ref, flux_ref, outer_ref):
    elements = partner_ref.shape[1]
    stack = table_parts(table_ref)
    codes = iota((4 * elements, elements), 0)
    star = star_ref[...]
    speed = 0.5 * speed_ref[...]
    for f in range(4):
        hot = (codes == partner_ref[f : f + 1, :]).astype(F32).astype(BF16)
        outer_ref[:, f * elements : (f + 1) * elements] = folded(dot(stack, hot))[:TABLE]
    for part in range(FACE_PAD // 8):
        at = [slice(g * FACE_PAD + 8 * part, g * FACE_PAD + 8 * part + 8) for g in range(FIELDS)]
        for f in range(4):
            normals = [0.5 * normal_ref[c, f : f + 1, :] for c in range(3)]
            columns = slice(f * elements, (f + 1) * elements)
            inner = jnp.concatenate([table_ref[rows, columns] for rows in at], axis=0)
            outer = jnp.concatenate([outer_ref[rows, columns] for rows in at], axis=0)
            flux = star_flux(star, normals, speed, inner, outer)
            for g in range(FIELDS):
                flux_ref[g, f * FACE_PAD + 8 * part : f * FACE_PAD + 8 * part + 8, :] = flux[
                    8 * g : 8 * g + 8
                ]


def remote_blocks(place, p1, p2, q1, q2):
    a1, c1 = unequal(place)
    return [
        (p1, 0, column_block(a1)),
        (p2, 0, column_block(-a1)),
        (q1, 2 * HALF, row_block(c1)),
        (q2, 2 * HALF, row_block(-c1)),
        (q1, 0, column_block(a1) + c1),
        (q1, HALF, column_block(-a1) + c1),
        (q2, 0, column_block(a1) - c1),
        (q2, HALF, column_block(-a1) - c1),
    ]


def prepared(
    place, star_ref, source_ref, deriv_ref, trace_ref, lift_ref, partner_ref,
    sea_face_ref, sea_row_ref, normal_ref, speed_ref, interp_ref,
    star4_ref, star3_ref, b1_ref, b2_ref, t_ref, l1_ref, l2_ref, hot_ref, sea_ref, slot_ref, scale_ref, uplift_ref,
):
    star, (b1_ref[...], b2_ref[...]), t_ref[...] = front_weights(
        star_ref, source_ref, deriv_ref, trace_ref
    )
    star4_ref[...] = star
    star3_ref[...] = star_weights([star_ref[0], star_ref[1], star_ref[2]])
    l1_ref[...], l2_ref[...] = lift_weights(lift_ref)
    elements = partner_ref.shape[1]
    blocks = remote_blocks(place, None, None, None, None)
    slot = iota((CAP, elements), 0)
    for f in range(4):
        wanted = partner_ref[f : f + 1, :] - 4 * elements
        hot_ref[:, f * elements : (f + 1) * elements] = jnp.concatenate(
            [(slot + CAP * block[2] == wanted).astype(F32) for block in blocks], axis=0
        ).astype(BF16)
    scales = [
        jnp.concatenate([normal_ref[c, f : f + 1, :] for f in range(4)], axis=1) for c in range(3)
    ]
    scales.append(jnp.concatenate([speed_ref[...]] * 4, axis=1))
    scales = 0.5 * jnp.concatenate(scales + [jnp.zeros((4, 4 * elements), F32)], axis=0)
    scale_ref[...] = folded(
        lax.dot_general(both_parts(scales), hot_ref[...], NT, preferred_element_type=F32)
    )
    uplift_ref[...] = side_weights(
        jnp.concatenate(
            [exact_dot(interp_ref[...], trace_ref[:, f, :]) for f in range(4)], axis=0
        )
    )
    faces = sea_face_ref.shape[1]
    sea_ref[...] = (iota((4 * elements, faces), 0) == sea_face_ref[...]).astype(F32).astype(BF16)
    row = sea_row_ref[...]
    tiles = slot_ref.shape[0]
    hits = (iota((tiles, faces), 0) == row).astype(F32)
    before = (iota((faces, faces), 0) < iota((faces, faces), 1)).astype(F32)
    count = dot(hits.astype(BF16), before.astype(BF16))
    mine = jnp.sum(count * hits, axis=0, keepdims=True).astype(jnp.int32)
    lane = iota((2 * CAP, faces), 0)
    mine = mine == lane % CAP
    for j in range(tiles):
        edges = mine & (row == jnp.where(lane < CAP, j - 1, j + 1))
        inside = mine & (row == j)
        slot_ref[j] = jnp.concatenate([edges.astype(F32), inside.astype(F32)], axis=0).astype(BF16)


def remote_flux(place, flux_ref, star_ref, hot_ref, scale_ref, arrived, packed_ref, table_ref):
    elements = hot_ref.shape[1] // 4
    blocks = remote_blocks(place, *arrived)
    left = iota((HALF, 2 * CAP), 1) < CAP
    for n in range(0, 8, 2):
        one = blocks[n][0][blocks[n][1] : blocks[n][1] + HALF, :]
        two = blocks[n + 1][0][blocks[n + 1][1] : blocks[n + 1][1] + HALF, :]
        lanes = slice(n * CAP, (n + 2) * CAP)
        packed_ref[0:HALF, lanes] = jnp.where(left, one, pltpu.roll(two, CAP, 1))
        packed_ref[HALF:, lanes] = jnp.where(left, pltpu.roll(one, CAP, 1), two)
    unpack(packed_ref, table_ref)
    star = star_ref[...]
    for part in range(FACE_PAD // 8):
        at = [slice(g * FACE_PAD + 8 * part, g * FACE_PAD + 8 * part + 8) for g in range(FIELDS)]
        for half in range(2):
            lanes = slice(4 * CAP * half, 4 * CAP * (half + 1))
            normals = [scale_ref[c : c + 1, lanes] for c in range(3)]
            outer = jnp.concatenate([table_ref[rows, lanes] for rows in at], axis=0)
            y = folded(dot(star, both_parts(outer)))
            size = FIELDS * 8
            flux = -scale_ref[3:4, lanes] * outer
            for c in range(3):
                flux = flux + normals[c] * y[c * size : (c + 1) * size]
            for g, rows in enumerate(at):
                table_ref[rows, lanes] = flux[8 * g : 8 * g + 8]
    remote = table_parts(table_ref)
    for f in range(4):
        columns = slice(f * elements, (f + 1) * elements)
        got = folded(dot(remote, hot_ref[:, columns]))
        for g in range(FIELDS):
            flux_ref[g, f * FACE_PAD : (f + 1) * FACE_PAD, :] += got[
                g * FACE_PAD : (g + 1) * FACE_PAD
            ]


def lift_weights(lift_ref):
    basis = lift_ref.shape[2]
    return weights(
        lax.dot_general(
            selector(basis, basis, 0),
            stacked_traces(lift_ref),
            NT,
            preferred_element_type=F32,
            precision=lax.Precision.HIGHEST,
        )
    )


def back(
    place, base_ref, local_ref, star_ref, l1_ref, l2_ref, hot_ref, scale_ref,
    p1_ref, p2_ref, q1_ref, q2_ref,
    state_ref, flux_ref, packed_ref, remote_ref,
):
    arrived = (p1_ref, p2_ref, q1_ref, q2_ref)
    flux_ref[...] = local_ref[...]
    remote_flux(place, flux_ref, star_ref, hot_ref, scale_ref, arrived, packed_ref, remote_ref)
    lift = l1_ref[...], l2_ref[...]
    basis = base_ref.shape[0] // FIELDS
    for g in range(FIELDS):
        rows = slice(g * basis, (g + 1) * basis)
        state_ref[rows, :] = base_ref[rows, :] - weighted(*lift, flux_ref[g])


def rates_out(vertical, uplift_ref, sea_base_ref, sea_ref, slot_ref, out_ref):
    tiles, _, faces = slot_ref.shape
    sea = side_weighted(uplift_ref[...], vertical)
    sea = jnp.concatenate([sea[f * POINTS : (f + 1) * POINTS] for f in range(4)], axis=1)
    rates = folded(dot(both_parts(sea), sea_ref[...]))
    corners = jnp.where(
        iota((8, faces), 0) == 0, sea_base_ref[0:1, :], sea_base_ref[1:2, :]
    ).astype(F32)
    sent = both_parts(jnp.concatenate([rates, corners], axis=0))
    left = iota((POINTS // 2, 2 * CAP), 1) < CAP
    left_1 = iota((1, 2 * CAP), 1) < CAP
    for j in range(tiles):
        got = folded(lax.dot_general(sent, slot_ref[j], NT, preferred_element_type=F32))
        near, own = got[:, : 2 * CAP], got[:, 2 * CAP :]
        out_ref[j, 0:POINTS, :] = near[:POINTS]
        out_ref[j, 16:24, :] = jnp.where(left, own[0:8], own[8:16])
        out_ref[j, 24:26, :] = near[POINTS : POINTS + 2]
        out_ref[j, 26:27, :] = jnp.where(left_1, own[16:17], own[17:18])
        out_ref[j, 27:32, :] = jnp.zeros((5, 2 * CAP), F32)


def finish(*refs):
    solid, sea, refs = refs[:12], refs[12:16], refs[16:]
    state_out, out_ref, state_ref, sems, *scratch = refs
    back(*solid, state_ref, *scratch)
    copy = pltpu.make_async_copy(state_ref, state_out, sems.at[0])
    copy.start()
    basis = state_ref.shape[0] // FIELDS
    vertical = state_ref[vertical_field * basis : (vertical_field + 1) * basis, :]
    rates_out(vertical, *sea, out_ref)
    copy.wait()


def forced(place, got_ref, forcing_ref, s1_ref, s2_ref):
    tiles = got_ref.shape[0]
    tile_x = forcing_ref.shape[0]
    tile_y = forcing_ref.shape[1] - 128
    left8 = iota((8, 2 * CAP), 1) < CAP
    left1 = iota((1, 2 * CAP), 1) < CAP
    tops, bottoms, xs, ys = [], [], [], []
    for s in range(0, tiles, 2):
        one, two = got_ref[s, 16:24, :], got_ref[s + 1, 16:24, :]
        tops.append(jnp.where(left8, one, pltpu.roll(two, CAP, 1)))
        bottoms.append(jnp.where(left8, pltpu.roll(one, CAP, 1), two))
        one, two = got_ref[s, 24:32, :], got_ref[s + 1, 24:32, :]
        xs.append(jnp.where(left8, one, pltpu.roll(two, CAP, 1))[2:3])
        ys.append(jnp.where(left8, pltpu.roll(one, CAP, 1), two)[2:3])
    lower, upper = jnp.concatenate(tops, axis=1), jnp.concatenate(bottoms, axis=1)
    x0, y0 = jnp.concatenate(xs, axis=1), jnp.concatenate(ys, axis=1)
    arrived = x0.shape[1]
    hot = (iota((tile_x, arrived), 0).astype(F32) == x0).astype(F32).astype(BF16)
    from_y = iota((tile_y, arrived), 0).astype(F32) - y0
    total = jnp.zeros((tile_x, tile_y), F32)
    for pr in range(patch_side):
        source = lower if pr < 2 else upper
        value = jnp.zeros((tile_y, arrived), F32)
        for pc in range(patch_side):
            at = (pr * patch_side + pc) % 8
            value = jnp.where(from_y == pc, source[at : at + 1], value)
        got = sum(
            lax.dot_general(hot, part, NT, preferred_element_type=F32) for part in parts(value)
        )
        total += got if pr == 0 else pltpu.roll(got, pr, 0)
    forcing_ref[:, :tile_y] = total
    near = jnp.concatenate([got_ref[s, 0:POINTS, :] for s in range(tiles)], axis=1)
    x0 = jnp.concatenate([got_ref[s, 24:25, :] for s in range(tiles)], axis=1)
    y0 = jnp.concatenate([got_ref[s, 25:26, :] for s in range(tiles)], axis=1)
    arrived = x0.shape[1]
    hot = (iota((tile_x, arrived), 0).astype(F32) == x0).astype(F32).astype(BF16)
    rows = iota((8, arrived), 0)
    before = iota((8, arrived), 1) % (2 * CAP) < CAP
    high_y = jnp.where(before & (rows >= 6), (rows + (tile_y - 8)).astype(F32) - y0, -1.0)
    low_y = jnp.where(before | (rows >= 2), -1.0, rows.astype(F32) - y0)
    chunks = [None] * 16
    for pr in range(patch_side):
        high, low = jnp.zeros((8, arrived), F32), jnp.zeros((8, arrived), F32)
        for pc in range(patch_side):
            at = pr * patch_side + pc
            high = jnp.where(high_y == pc, near[at : at + 1], high)
            low = jnp.where(low_y == pc, near[at : at + 1], low)
        chunks[(4 * pr - 1) % 16], chunks[4 * pr] = high, low
    blank = jnp.zeros((8, arrived), F32)
    value = jnp.concatenate([blank if c is None else c for c in chunks], axis=0)
    got = sum(lax.dot_general(hot, part, NT, preferred_element_type=F32) for part in parts(value))
    lane = iota((tile_x, 128), 1)
    used = (lane < 2) | (lane >= 126)
    total = jnp.where(used, got, 0.0)
    for pr in range(1, patch_side):
        moved_back = pltpu.roll(pltpu.roll(got, 128 - 32 * pr, 1), pr, 0)
        total += jnp.where(used, moved_back, 0.0)
    forcing_ref[:, tile_y:] = total
    a1, _ = unequal(place)
    head, tail = forcing_ref[0:8, :], forcing_ref[tile_x - 8 : tile_x, :]
    tail = pltpu.roll(tail, 2, 0)
    s1_ref[...] = jnp.where(a1 > 0, tail, head)
    s2_ref[...] = jnp.where(a1 > 0, head, tail)


def edge_rows(place, heads, tails, p1_ref, p2_ref):
    a1, _ = unequal(place)
    for i in range(4):
        head, tail = heads[i, 0:2, :], tails[i, 6:8, :]
        one = jnp.where(a1 > 0, tail, head)
        two = jnp.where(a1 > 0, head, tail)
        for h in range(2):
            at = slice(3 * HALF + 4 * i + 2 * h, 3 * HALF + 4 * i + 2 * h + 2)
            lanes = slice(128 * h, 128 * (h + 1))
            p1_ref[at, :] = one[:, lanes]
            p2_ref[at, :] = two[:, lanes]


def edge_columns(place, depth_ref, momentum_ref, bottom_ref, one_ref, two_ref):
    arrays = [depth_ref[...], momentum_ref[0], momentum_ref[1], bottom_ref[...]]
    _, c1 = unequal(place)
    tile_y = depth_ref.shape[1]
    row = iota((8, tile_y), 0)
    up = jnp.where(row < 2, row + (tile_y - 2), row - 2)
    down = jnp.where(row < 2, row, row + (tile_y - 4))
    wanted = jnp.where(c1 > 0, up, down)
    hot = ((row < 4) & (wanted == iota((8, tile_y), 1))).astype(F32)
    for i, array in enumerate(arrays):
        columns = lax.dot_general(
            hot, array, NT, preferred_element_type=F32, precision=lax.Precision.HIGHEST
        )
        for h in range(2):
            at = slice(4 * i + 2 * h, 4 * i + 2 * h + 2)
            lanes = slice(128 * h, 128 * (h + 1))
            one_ref[at, :] = columns[0:2, lanes]
            two_ref[at, :] = columns[2:4, lanes]


def widened(place, depth_ref, momentum_ref, bottom_ref, p1_ref, p2_ref, q1_ref, q2_ref, out_ref):
    tile_x, tile_y = depth_ref.shape
    a1, c1 = unequal(place)
    arrays = [depth_ref[...], momentum_ref[0], momentum_ref[1], bottom_ref[...]]
    p1, p2 = p1_ref[3 * HALF :, :], p2_ref[3 * HALF :, :]
    q1, q2 = q1_ref[3 * HALF :, :], q2_ref[3 * HALF :, :]
    is_below, is_above = place[0] > 0, place[0] < place[2] - 1
    below = jnp.where(is_below, jnp.where(a1 > 0, p2, p1), 0.0)
    above = jnp.where(is_above, jnp.where(a1 > 0, p1, p2), 0.0)
    before = jnp.where(place[1] > 0, jnp.where(c1 > 0, q2, q1), 0.0)
    after = jnp.where(place[1] < place[3] - 1, jnp.where(c1 > 0, q1, q2), 0.0)
    n = OCEAN_ROWS

    def ends(rows):
        one, two = rows[n : n + 8], rows[n + 8 :]
        return (
            jnp.where(is_below, jnp.where(a1 > 0, two, one), 0.0),
            jnp.where(is_above, jnp.where(a1 > 0, one, two), 0.0),
        )

    before_below, before_above = ends(before)
    after_below, after_above = ends(after)
    lane = iota((2, 128), 1)
    low, high = lane < 2, lane >= 126
    for i, array in enumerate(arrays):
        first, second = slice(4 * i, 4 * i + 2), slice(4 * i + 2, 4 * i + 4)
        out_ref[i, 0:MARGIN, :] = jnp.zeros((MARGIN, tile_y + 128), F32)
        out_ref[i, MARGIN + tile_x :, :] = jnp.zeros((MARGIN, tile_y + 128), F32)
        out_ref[i, MARGIN : MARGIN + tile_x, :tile_y] = array
        for at, rows, left, right in (
            (MARGIN - 2, below, before_below, after_below),
            (MARGIN + tile_x, above, before_above, after_above),
        ):
            out_ref[i, at : at + 2, 0:128] = rows[first]
            out_ref[i, at : at + 2, 128:256] = rows[second]
            end = slice(2 * i, 2 * i + 2)
            corner = jnp.where(low, right[end], jnp.where(high, left[end], 0.0))
            out_ref[i, at : at + 2, 256:384] = corner
        start = jnp.concatenate([after[first], after[second]], axis=1)
        finish = jnp.concatenate([before[first], before[second]], axis=1)
        columns = jnp.concatenate([start, jnp.zeros((124, tile_x), F32), finish], axis=0)
        out_ref[i, MARGIN : MARGIN + tile_x, tile_y:] = columns.T


STRIP = 16


def next_of(x):
    return pltpu.roll(x, x.shape[1] - 1, 1)


def previous_of(x):
    return pltpu.roll(x, 1, 1)


def cells(state, cell, low, high):
    for at in range(low, high, 8):
        here = slice(at, at + 8)
        h, mx, my = state[0, here, :], state[1, here, :], state[2, here, :]
        safe = jnp.maximum(h, depth_floor)
        root = lax.rsqrt(safe)
        inverse = root * root
        c = safe * root
        u, v = mx * inverse, my * inverse
        half = 0.5 * h * h
        cell[0, here, :] = mx * u + half
        cell[1, here, :] = my * u
        cell[2, here, :] = my * v + half
        cell[3, here, :] = 0.5 * (jnp.abs(u) + c)
        cell[4, here, :] = 0.5 * (jnp.abs(v) + c)


def moved(state, cell, face, at, rows):
    here, up = slice(at, at + rows), slice(at + 1, at + rows + 1)
    below = slice(at - 1, at + rows - 1)
    now = [state[k, here, :] for k in range(3)]
    cross = cell[1, here, :]
    next_now = [state[k, up, :] for k in range(3)]
    wave = jnp.maximum(cell[3, here, :], cell[3, up, :])
    pairs = ((now[1], next_now[1]), (cell[0, here, :], cell[0, up, :]), (cross, cell[1, up, :]))
    upper = [
        0.5 * (pairs[k][0] + pairs[k][1]) - wave * (next_now[k] - now[k]) for k in range(3)
    ]
    for k in range(3):
        face[k, here, :] = upper[k]
    flux = (now[2], cross, cell[2, here, :])
    speed = cell[4, here, :]
    wave = jnp.maximum(speed, next_of(speed))
    next_now = [next_of(x) for x in now]
    next_flux = (next_now[2], next_of(flux[1]), next_of(flux[2]))
    y_face = [
        0.5 * (flux[k] + next_flux[k]) - wave * (next_now[k] - now[k]) for k in range(3)
    ]
    return [
        now[k] - step_ocean * (upper[k] - face[k, below, :] + y_face[k] - previous_of(y_face[k]))
        for k in range(3)
    ]


def sloped(height, bed, at, rows):
    b = bed[at : at + rows, :]
    slope_x = 0.5 * (bed[at + 1 : at + rows + 1, :] - bed[at - 1 : at + rows - 1, :])
    slope_y = 0.5 * (next_of(b) - previous_of(b))
    scale = step_ocean * height
    return scale * slope_x, scale * slope_y


def ocean_cells(
    place, depth_ref, momentum_ref, bottom_ref, p1_ref, p2_ref, q1_ref, q2_ref, wide, cell
):
    widened(place, depth_ref, momentum_ref, bottom_ref, p1_ref, p2_ref, q1_ref, q2_ref, wide)
    height, span = wide.shape[1:]
    cell[:, 0:8, :] = jnp.zeros((5, 8, span), F32)
    cell[:, height - 8 :, :] = jnp.zeros((5, 8, span), F32)
    cells(wide, cell, 8, height - 8)


def ocean_first(place, wide, cell, state, face):
    tile_x, tile_y = wide.shape[1] - 2 * MARGIN, wide.shape[2] - 128
    height, span = wide.shape[1:]
    lane = iota((STRIP, span), 1)
    outside = ((lane == span - 1) & (place[1] == 0)) | (
        (lane == tile_y) & (place[1] == place[3] - 1)
    )
    state[:, 0:8, :] = jnp.zeros((3, 8, span), F32)
    state[:, height - 8 :, :] = jnp.zeros((3, 8, span), F32)
    face[:, 0:8, :] = jnp.zeros((3, 8, span), F32)
    for at in range(8, height - 8, STRIP):
        new = moved(wide, cell, face, at, STRIP)
        row = iota((STRIP, span), 0) + at
        out = outside | ((row < MARGIN) & (place[0] == 0))
        out = out | ((row >= MARGIN + tile_x) & (place[0] == place[2] - 1))
        for k in range(3):
            state[k, at : at + STRIP, :] = jnp.where(out, 0.0, new[k])


def second_step(wide, first, bed, state, cell, face, rows, put, raise_bed):
    low, high = rows.start - 8, rows.stop + 8
    raise_bed(wide.at[3])
    for at in range(low, high, STRIP):
        here = slice(at, at + STRIP)
        change_x, change_y = sloped(wide[0, here, :], bed, at, STRIP)
        state[0, here, :] = first[0, here, :]
        state[1, here, :] = first[1, here, :] - change_x
        state[2, here, :] = first[2, here, :] - change_y
    cells(state, cell, low, high)
    raise_bed(bed)
    moved(state, cell, face, low, 8)
    for at in range(rows.start, rows.stop, STRIP):
        new = moved(state, cell, face, at, STRIP)
        change_x, change_y = sloped(state[0, at : at + STRIP, :], bed, at, STRIP)
        new[1] -= change_x
        new[2] -= change_y
        put(at, new)


def ocean_inner(wide, first, forcing_ref, out_ref, bed_ref, state, bed, cell, face):
    tile_x, tile_y = bed_ref.shape
    inner = slice(MARGIN, MARGIN + tile_x)
    bed[...] = wide[3]

    def raise_bed(source):
        bed[inner, :] = source[inner, :] + step_ocean * forcing_ref[...]

    def put(at, new):
        for k in range(3):
            out_ref[k, at - MARGIN : at - MARGIN + STRIP, :] = new[k][:, :tile_y]

    rows = slice(MARGIN + STRIP, MARGIN + tile_x - STRIP)
    second_step(wide, first, bed, state, cell, face, rows, put, raise_bed)
    bed_ref[...] = bed[inner, :tile_y]


def ocean_ends(
    place, wide, first, forcing_ref, s1_ref, s2_ref, inner_ref, raised_ref, out_hbm, bed_hbm,
    out_ref, bed_ref, sems, state, bed, cell, face,
):
    tile_x, tile_y = raised_ref.shape
    last = tile_x - STRIP
    middle = pl.ds(STRIP, tile_x - 2 * STRIP)
    copies = [
        pltpu.make_async_copy(raised_ref, bed_hbm, sems.at[0]),
        pltpu.make_async_copy(inner_ref.at[:, middle], out_hbm.at[:, middle], sems.at[1]),
    ]
    for copy in copies:
        copy.start()
    a1, _ = unequal(place)
    force_lo = step_ocean * jnp.where(a1 > 0, s2_ref[...], s1_ref[...])[0:2]
    force_lo = jnp.where(place[0] > 0, force_lo, 0.0)
    force_hi = step_ocean * jnp.where(a1 > 0, s1_ref[...], s2_ref[...])[0:2]
    force_hi = jnp.where(place[0] < place[2] - 1, force_hi, 0.0)

    def put(at, new):
        for k in range(3):
            out_ref[k, at - MARGIN : at - MARGIN + STRIP, :] = new[k][:, :tile_y]

    for n, start in enumerate((MARGIN, MARGIN + last)):
        outer = slice(start - 16, start) if n == 0 else slice(start + STRIP, start + STRIP + 16)
        edge = slice(MARGIN - 2, MARGIN) if n == 0 else slice(MARGIN + tile_x, MARGIN + tile_x + 2)
        force = force_lo if n == 0 else force_hi
        own = slice(start, start + 32) if n == 0 else slice(start - 16, start + 16)
        forcing = forcing_ref[own.start - MARGIN : own.stop - MARGIN, :]
        bed[outer, :] = wide[3, outer, :]

        def raise_bed(source):
            bed[own, :] = source[own, :] + step_ocean * forcing
            bed[edge, :] = source[edge, :] + force

        second_step(
            wide, first, bed, state, cell, face, slice(start, start + STRIP), put, raise_bed
        )
        at = pl.ds(start - MARGIN, STRIP)
        copies.append(pltpu.make_async_copy(out_ref.at[:, at], out_hbm.at[:, at], sems.at[2 + n]))
        copies[-1].start()
    for copy in copies:
        copy.wait()


def call(
    body, out_shape, *args, place=None, scratch=(), held=0, sent=0, copies=0, limit=VMEM_LIMIT
):
    out_space = [pltpu.HBM if i < sent else pltpu.VMEM for i in range(len(out_shape))]
    specs = [pl.BlockSpec(memory_space=pltpu.HBM if held else pltpu.VMEM) for _ in args]
    shapes = [
        s if isinstance(s, jax.ShapeDtypeStruct) else jax.ShapeDtypeStruct(s, F32) for s in out_shape
    ]
    scratch = [pltpu.VMEM(s, F32) for s in scratch]
    if copies:
        scratch = [pltpu.SemaphoreType.DMA((copies,))] + scratch
    scratch = [pltpu.VMEM(x.shape, x.dtype) for x in [*args[:held], *shapes[:sent]]] + scratch
    if place is not None:
        sizes, inner = place, body

        def body(*refs):
            here = (lax.axis_index("gx"), lax.axis_index("gy"))
            inner(here + sizes, *refs)

    return pl.pallas_call(
        body,
        out_shape=shapes,
        in_specs=specs,
        out_specs=[pl.BlockSpec(memory_space=space) for space in out_space],
        scratch_shapes=scratch,
        compiler_params=pltpu.CompilerParams(vmem_limit_bytes=limit),
    )(*args)


def swap(block, axis, parity, wrap=False):
    count = lax.axis_size(axis)
    last = count + parity - 1 if wrap else count - 1
    pairs = []
    for i in range(parity, last, 2):
        pairs += [(i, (i + 1) % count), ((i + 1) % count, i)]
    taken = {source for source, _ in pairs}
    pairs += [(i, i) for i in range(count) if i not in taken]
    return lax.ppermute(block, axis, pairs)


def per_device(
    coefficients,
    jacobian,
    face_normals,
    wave_speed,
    star_mats,
    deriv_mats,
    stiff_mats,
    source_mat,
    trace_mats,
    lift_mats,
    face_partner,
    send_faces,
    sea_face,
    sea_row,
    sea_base,
    interp_mat,
    water_depth,
    momentum,
    bottom,
):
    basis, elements = coefficients.shape[1:]
    rows = FIELDS * basis
    tile_x, tile_y = water_depth.shape
    tiles = lax.axis_size("gy")
    place = (lax.axis_size("gx"), tiles)
    speed = wave_speed.reshape(1, elements)
    traces = trace_mats.transpose(1, 0, 2)
    normals = face_normals.transpose(1, 0, 2)
    lifts = lift_mats.transpose(2, 0, 1)
    spread = (FIELDS, 3 * basis, elements)
    faces = (TABLE, 4 * elements)
    solid = (rows, elements)
    wide_shape = (tile_x + 2 * MARGIN, tile_y + 128)
    state = coefficients.reshape(solid)
    packed = (2 * HALF, 8 * CAP)
    flux_shape = (FIELDS, 4 * FACE_PAD, elements)
    for section in range(2):
        scratch = [spread, solid, solid, solid, (2 * HALF, 4 * CAP)]
        if section == 0:
            fixed = (state, jacobian, star_mats, source_mat, deriv_mats, traces, send_faces)
            buffers = [(3 * HALF + OCEAN_ROWS, 128)] * 2 + [(HALF, 128)] * 2
            integral, table, p1, p2, own1, own2 = call(
                start, [solid, faces] + buffers, *fixed, water_depth, momentum, bottom,
                place=place, scratch=[(4, 8, tile_y)] * 2 + scratch,
                held=len(fixed), sent=6, copies=len(fixed) + 14, limit=START_LIMIT,
            )
        else:
            buffers = [(3 * HALF, 128)] * 2 + [(HALF, 128)] * 2
            integral, table, p1, p2, own1, own2 = call(
                front_again, [solid, faces] + buffers,
                state, jacobian, star4, *derivs, *traced, send_faces, place=place, scratch=scratch,
            )
        p2, p1 = swap(p2, "gx", 1), swap(p1, "gx", 0)
        inside = (state, jacobian, star_mats, stiff_mats, integral)
        (base,) = call(volume, [solid], *inside, scratch=[spread])
        if section == 0:
            columns = call(
                edge_columns, [(OCEAN_ROWS, 128)] * 2, water_depth, momentum, bottom, place=place
            )
            size = 3 * HALF + 2 * OCEAN_ROWS
        else:
            columns, size = [], 3 * HALF
            wide, cell = call(
                ocean_cells,
                [(4,) + wide_shape, (5,) + wide_shape],
                water_depth, momentum, bottom, *halos,
                place=place,
            )
            base, wide, cell = lax.optimization_barrier((base, wide, cell))
        p1, p2, base = lax.optimization_barrier((p1, p2, base))
        q1, q2 = call(forward, [(size, 128)] * 2, p1, p2, own1, own2, *columns, place=place)
        q2, q1 = swap(q2, "gy", 1), swap(q1, "gy", 0)
        if section == 1:
            (flux,) = call(
                local_flux, [flux_shape], table, face_partner, normals, speed, star3,
                scratch=[faces],
            )
            (first,) = call(
                ocean_first,
                [(3,) + wide_shape],
                wide, cell,
                place=place, scratch=[(3,) + wide_shape],
            )
            q1, q2, flux, first = lax.optimization_barrier((q1, q2, flux, first))
        else:
            half = lambda *shape: jax.ShapeDtypeStruct(shape, BF16)
            size, sea = FIELDS * 8, sea_face.shape[0]
            star4, star3, *ready = call(
                prepared,
                [half(16 * (FIELDS + FIELDS % 2), 12 * (FIELDS + FIELDS % 2)), half(6 * size, 2 * size)]
                + [half(2 * basis, 3 * basis), half(basis, 3 * basis)]
                + [half(4 * FACE_PAD, 3 * basis)]
                + [half(2 * basis, 4 * FACE_PAD), half(basis, 4 * FACE_PAD)]
                + [half(8 * CAP, 4 * elements), half(4 * elements, sea), half(tiles, 4 * CAP, sea), (8, 8 * CAP)]
                + [half(4 * POINTS, 3 * basis)],
                star_mats, source_mat, deriv_mats, traces, lifts, face_partner,
                sea_face.reshape(1, -1), sea_row.T, normals, speed, interp_mat,
                place=place,
            )
            (flux,) = call(
                local_flux, [flux_shape], table, face_partner, normals, speed, star3,
                scratch=[faces],
            )
            q1, q2, flux, *ready = lax.optimization_barrier((q1, q2, flux, *ready))
            derivs, traced, lifting, (hot, sea_hot, slot_hot, scales, uplift) = (
                ready[0:2], ready[2:3], ready[3:5], ready[5:],
            )
        fixed = (star3, *lifting, hot, scales)
        arrived = (p1, p2, q1, q2)
        remote = (TABLE, 8 * CAP)
        if section == 0:
            (state,) = call(
                back, [solid], base, flux, *fixed, *arrived,
                place=place, scratch=[flux_shape, packed, remote],
            )
            halos = (p1, p2, q1, q2)
        else:
            state, outgoing = call(
                finish,
                [solid, (tiles, 32, 128)],
                base, flux, *fixed, *arrived,
                uplift, sea_base.T, sea_hot, slot_hot,
                place=place, scratch=[flux_shape, packed, remote], sent=1, copies=1,
            )
    incoming = lax.all_to_all(outgoing, "gy", split_axis=0, concat_axis=0, tiled=True)
    forcing, s1, s2 = call(
        forced,
        [(tile_x, tile_y + 128), (8, tile_y + 128), (8, tile_y + 128)],
        incoming,
        place=place,
    )
    s2, s1 = swap(s2, "gx", 1, wrap=True), swap(s1, "gx", 0)
    scratch = [(3,) + wide_shape, wide_shape, (5,) + wide_shape, (3,) + wide_shape]
    water = [(3, tile_x, tile_y), (tile_x, tile_y)]
    inner, raised = call(ocean_inner, water, wide, first, forcing, scratch=scratch)
    ocean_final, bed_final = call(
        ocean_ends, water, wide, first, forcing, s1, s2, inner, raised,
        place=place, scratch=scratch, sent=2, copies=4,
    )
    return (state.reshape(coefficients.shape), ocean_final, bed_final)


def solution(mesh):
    in_specs = (
        P(None, None, ("gx", "gy")),
        P(None, None, ("gx", "gy")),
        P(None, None, ("gx", "gy")),
        P(("gx", "gy")),
        P(),
        P(),
        P(),
        P(),
        P(),
        P(),
        P(None, ("gx", "gy")),
        P(None, ("gx", "gy")),
        P(("gx", "gy")),
        P(("gx", "gy"), None),
        P(("gx", "gy"), None),
        P(),
        P("gx", "gy"),
        P(None, "gx", "gy"),
        P("gx", "gy"),
    )
    out_specs = (P(None, None, ("gx", "gy")), P(None, "gx", "gy"), P("gx", "gy"))
    return jax.shard_map(
        per_device, mesh=mesh, in_specs=in_specs, out_specs=out_specs, check_vma=False
    )
```

```python
import jax
import jax.numpy as jnp
from jax import lax
from jax.experimental import pallas as pl
from jax.experimental.pallas import tpu as pltpu
from jax.sharding import PartitionSpec as P

FIELDS = 13
FACE_BASIS = 21
FACE_PAD = 24
POINTS = 16
ORD = 3
STEPS_OCEAN = 2
CAP = 64
TABLE = FIELDS * FACE_PAD
WIDE = 320
HALF = (FIELDS * FACE_BASIS + 1) // 2
OCEAN_ROWS = 16
MARGIN = 16
FOUR = 4

step_solid = 0.4
step_ocean = 0.2
depth_floor = 0.5
vertical_field = 6
patch_side = 4

F32 = jnp.float32
BF16 = jnp.bfloat16
NT = (((1,), (1,)), ((), ()))
VMEM_LIMIT = 24 * 1024 * 1024
START_LIMIT = 62 * 1024 * 1024


def iota(shape, dim):
    return lax.broadcasted_iota(jnp.int32, shape, dim)


def dot(a, b):
    return jnp.dot(a, b, preferred_element_type=F32)


def exact_dot(a, b):
    return jnp.dot(a, b, preferred_element_type=F32, precision=lax.Precision.HIGHEST)


def parts(x):
    high = x.astype(BF16)
    low = (x - high.astype(F32)).astype(BF16)
    return high, low


def both_parts(x):
    high = x.astype(BF16).astype(F32)
    return jnp.concatenate([high, x - high], axis=0).astype(BF16)


def folded(y):
    half = y.shape[0] // 2
    return y[:half] + y[half:]


def weights(w):
    return both_parts(w), w.astype(BF16)


def weighted(stack, high, x):
    x_high, x_low = parts(x)
    return folded(dot(stack, x_high)) + dot(high, x_low)


def side_weights(w):
    columns = w.shape[1]
    high, low = parts(w)
    place = [selector(columns, 3 * columns, i * columns).astype(BF16) for i in range(3)]
    return (dot(high, place[0] + place[1]) + dot(low, place[2])).astype(BF16)


def side_weighted(stack, x):
    high = x.astype(BF16).astype(F32)
    return dot(stack, jnp.concatenate([high, x - high, high], axis=0).astype(BF16))


def selector(rows, columns, shift):
    return (iota((rows, columns), 1) == iota((rows, columns), 0) + shift).astype(F32)


def star_weights(mats):
    size = FIELDS * 8
    spread = ((iota((FIELDS, 2 * size), 1) % size) // 8 == iota((FIELDS, 2 * size), 0)).astype(F32)
    diagonal = iota((size, 2 * size), 0) % 8 == iota((size, 2 * size), 1) % 8
    first = iota((size, 2 * size), 1) < size
    high, low = [], []
    for mat in mats:
        wide = exact_dot(mat, spread)
        tall = jnp.concatenate(
            [jnp.broadcast_to(wide[g : g + 1], (8, 2 * size)) for g in range(FIELDS)], axis=0
        )
        tall = jnp.where(diagonal, tall, 0.0)
        top = tall.astype(BF16).astype(F32)
        high.append(top)
        low.append(jnp.where(first, tall - top, 0.0))
    return jnp.concatenate(high + low, axis=0).astype(BF16)


def side_by_side(mats):
    rows, columns = mats[0].shape
    total = len(mats) * columns
    return sum(exact_dot(m, selector(columns, total, i * columns)) for i, m in enumerate(mats))


def stacked_traces(trace_ref):
    place = (
        iota((FACE_PAD, FACE_BASIS), 0) == iota((FACE_PAD, FACE_BASIS), 1)
    ).astype(F32)
    return jnp.concatenate([exact_dot(place, trace_ref[:, f, :]) for f in range(4)], axis=0)


def star_quarters(mats):
    size = FOUR * (FIELDS + FIELDS % 2)
    columns = 3 * size
    spread = ((iota((FIELDS, columns), 1) % size) // FOUR == iota((FIELDS, columns), 0)).astype(F32)
    upper = iota((8, columns), 0) < FOUR
    diagonal = iota((size, columns), 0) % FOUR == iota((size, columns), 1) % FOUR
    first = iota((size, columns), 1) < 2 * size
    out = []
    for mat in mats:
        wide = exact_dot(mat, spread)
        wide = [jnp.broadcast_to(wide[g : g + 1], (8, columns)) for g in range(FIELDS)]
        wide += [jnp.zeros((8, columns), F32)] * (FIELDS % 2)
        tall = jnp.concatenate(
            [jnp.where(upper, wide[g], wide[g + 1]) for g in range(0, FIELDS, 2)], axis=0
        )
        tall = jnp.where(diagonal, tall, 0.0)
        high = tall.astype(BF16).astype(F32)
        out.append(jnp.where(first, high, tall - high))
    return jnp.concatenate(out, axis=0).astype(BF16)


def interleaved(one, two, upper):
    return jnp.where(upper, one, pltpu.roll(two, FOUR, 0)), jnp.where(
        upper, pltpu.roll(one, FOUR, 0), two
    )


def spread_out(source, jac_ref, star, target, extra=None):
    basis = target.shape[1] // 3
    lanes = target.shape[2]
    pairs = (FIELDS + 1) // 2
    size = 8 * pairs
    upper = iota((8, lanes), 0) < FOUR
    for j in range(basis // 8):
        x = [source[g * basis + 8 * j : g * basis + 8 * j + 8, :] for g in range(FIELDS)]
        x += [jnp.zeros((8, lanes), F32)] * (2 * pairs - FIELDS)
        mixed = [interleaved(x[2 * p], x[2 * p + 1], upper) for p in range(pairs)]
        halves = []
        for half in range(2):
            y = side_weighted(star, jnp.concatenate([m[half] for m in mixed], axis=0))
            z = [
                sum(jac_ref[d, c : c + 1, :] * y[c * size : (c + 1) * size] for c in range(3))
                for d in range(3)
            ]
            halves.append(z + ([] if extra is None else [y[3 * size :]]))
        for d, (one, two) in enumerate(zip(*halves)):
            for p in range(pairs):
                rows = slice(8 * p, 8 * p + 8)
                for g, value in zip(
                    range(2 * p, FIELDS), interleaved(one[rows], two[rows], upper)
                ):
                    if d < 3:
                        target[g, d * basis + 8 * j : d * basis + 8 * j + 8, :] = value
                    else:
                        extra[g * basis + 8 * j : g * basis + 8 * j + 8, :] = value


def derivative(source, target, jac_ref, star, basis_weights, spread_ref, relaxed_ref):
    basis = spread_ref.shape[1] // 3
    spread_out(source, jac_ref, star, spread_ref, relaxed_ref)
    for g in range(FIELDS):
        rows = slice(g * basis, (g + 1) * basis)
        target[rows, :] = -(weighted(*basis_weights, spread_ref[g]) + relaxed_ref[rows, :])


def unequal(place):
    a1 = jnp.where(place[0] % 2 == 0, 1, -1)
    c1 = jnp.where(place[1] % 2 == 0, 1, -1)
    return a1, c1


def column_block(a):
    return jnp.where(a > 0, 6, 1)


def row_block(c):
    return jnp.where(c > 0, 4, 3)


def front_weights(star_ref, source_ref, deriv_ref, trace_ref, ready=lambda *numbers: None):
    ready(2, 3)
    star = star_quarters([star_ref[0], star_ref[1], star_ref[2], source_ref[...]])
    ready(4, 5)
    basis_weights = weights(side_by_side([deriv_ref[d] for d in range(3)]))
    return star, basis_weights, side_weights(stacked_traces(trace_ref))


def front_again(place, q_ref, jac_ref, star_ref, b1_ref, b2_ref, trace_ref, *refs):
    held = star_ref[...], (b1_ref[...], b2_ref[...]), trace_ref[...]
    front(place, held, q_ref, jac_ref, *refs)


def front(
    place, held, q_ref, jac_ref, send_ref,
    integral_ref, table_ref, p1_ref, p2_ref, own1_ref, own2_ref,
    spread_ref, relaxed_ref, d1_ref, d2_ref, packed_ref, ready=lambda *numbers: None, made=lambda *numbers: None,
):
    elements = q_ref.shape[1]
    basis = q_ref.shape[0] // FIELDS
    star, basis_weights, trace = held
    ready(0, 1)
    derivative(q_ref, d1_ref, jac_ref, star, basis_weights, spread_ref, relaxed_ref)
    derivative(d1_ref, d2_ref, jac_ref, star, basis_weights, spread_ref, relaxed_ref)
    first = step_solid
    second = first * step_solid / 2
    third = second * step_solid / 3
    for g in range(FIELDS):
        rows = slice(g * basis, (g + 1) * basis)
        whole = first * q_ref[rows, :] + second * d1_ref[rows, :] + third * d2_ref[rows, :]
        integral_ref[rows, :] = whole
        faces = side_weighted(trace, whole)
        for f in range(4):
            table_ref[g * FACE_PAD : (g + 1) * FACE_PAD, f * elements : (f + 1) * elements] = faces[
                f * FACE_PAD : (f + 1) * FACE_PAD
            ]
    made(0, 1)
    ready(6)
    a1, c1 = unequal(place)
    picks = [
        (p1_ref, 0, column_block(a1)),
        (p2_ref, 0, column_block(-a1)),
        (p1_ref, HALF, column_block(a1) + c1),
        (p1_ref, 2 * HALF, column_block(a1) - c1),
        (p2_ref, HALF, column_block(-a1) + c1),
        (p2_ref, 2 * HALF, column_block(-a1) - c1),
        (own1_ref, 0, row_block(c1)),
        (own2_ref, 0, row_block(-c1)),
    ]
    stack = table_parts(table_ref)
    left = iota((HALF, 2 * CAP), 1) < CAP
    codes = iota((4 * elements, 4 * CAP), 0)
    packed_ref[FIELDS * FACE_BASIS :, :] = jnp.zeros((2 * HALF - FIELDS * FACE_BASIS, 4 * CAP), F32)
    for n in range(0, 8, 4):
        wanted = jnp.concatenate([send_ref[pl.ds(pick[2], 1), :] for pick in picks[n : n + 4]], axis=1)
        got = folded(dot(stack, (codes == wanted).astype(F32).astype(BF16)))
        pack(got, packed_ref)
        for pair in range(2):
            lanes = slice(pair * 2 * CAP, (pair + 1) * 2 * CAP)
            low, high = packed_ref[0:HALF, lanes], packed_ref[HALF:, lanes]
            ref, at, _ = picks[n + 2 * pair]
            ref[at : at + HALF, :] = jnp.where(left, low, pltpu.roll(high, CAP, 1))
            ref, at, _ = picks[n + 2 * pair + 1]
            ref[at : at + HALF, :] = jnp.where(left, pltpu.roll(low, CAP, 1), high)


def pack(table, packed_ref):
    rest = FACE_BASIS - 16
    for g in range(FIELDS):
        packed_ref[16 * g : 16 * (g + 1), :] = table[FACE_PAD * g : FACE_PAD * g + 16]
        at = 16 * FIELDS + rest * g
        packed_ref[at : at + rest, :] = table[FACE_PAD * g + 16 : FACE_PAD * g + FACE_BASIS]


def unpack(packed_ref, table_ref):
    rest = FACE_BASIS - 16
    for g in range(FIELDS):
        table_ref[FACE_PAD * g : FACE_PAD * g + 16, :] = packed_ref[16 * g : 16 * (g + 1), :]
        at = 16 * FIELDS + rest * g
        last = FACE_PAD * g + 16
        table_ref[last : last + 8, :] = jnp.zeros((8, table_ref.shape[1]), F32)
        table_ref[last : last + rest, :] = packed_ref[at : at + rest, :]


def start(place, *refs):
    sources, water, refs = refs[:7], refs[7:10], refs[10:]
    targets, refs = refs[:6], refs[6:]
    held, outs, (sems, heads, tails, *scratch) = refs[:7], refs[7:13], refs[13:]
    depth, momentum, bottom = water
    last = depth.shape[0] - 8
    pairs = [(sources[i], held[i]) for i in range(7)]
    for rows, target in ((pl.ds(0, 8), heads), (pl.ds(last, 8), tails)):
        pairs += [
            (depth.at[rows], target.at[0]),
            (momentum.at[0, rows], target.at[1]),
            (momentum.at[1, rows], target.at[2]),
            (bottom.at[rows], target.at[3]),
        ]
    first_out = len(pairs)
    pairs += list(zip(outs, targets))
    copies = [pltpu.make_async_copy(a, b, sems.at[i]) for i, (a, b) in enumerate(pairs)]
    for copy in copies[:first_out]:
        copy.start()

    def ready(*numbers):
        for i in numbers:
            copies[i].wait()

    def made(*numbers):
        for i in numbers:
            copies[first_out + i].start()

    ready_weights = front_weights(*held[2:6], ready=ready)
    front(place, ready_weights, *held[:2], held[6], *outs, *scratch, ready=ready, made=made)
    ready(*range(7, first_out))
    edge_rows(place, heads, tails, *outs[2:4])
    made(2, 3, 4, 5)
    ready(*range(first_out, len(copies)))


def table_parts(table_ref):
    pad = jnp.zeros((WIDE - TABLE, table_ref.shape[1]), BF16)
    high, low = parts(table_ref[...])
    both = [high.astype(F32), pad.astype(F32), low.astype(F32), pad.astype(F32)]
    return jnp.concatenate(both, axis=0).astype(BF16)


def volume(q_ref, jac_ref, star_ref, stiff_ref, integral_ref, base_ref, spread_ref):
    basis = stiff_ref.shape[1]
    star = star_quarters([star_ref[0], star_ref[1], star_ref[2]])
    basis_weights = weights(side_by_side([stiff_ref[d] for d in range(3)]))
    spread_out(integral_ref, jac_ref, star, spread_ref)
    for g in range(FIELDS):
        rows = slice(g * basis, (g + 1) * basis)
        base_ref[rows, :] = q_ref[rows, :] + weighted(*basis_weights, spread_ref[g])


def forward(place, p1_ref, p2_ref, *refs):
    outs = refs[-2:]
    _, c1 = unequal(place)
    for n, out in enumerate(outs):
        at = slice((n + 1) * HALF, (n + 2) * HALF)
        out[0:HALF, :] = p1_ref[at, :]
        out[HALF : 2 * HALF, :] = p2_ref[at, :]
        out[2 * HALF : 3 * HALF, :] = refs[n][...]
        if len(refs) > 4:
            at = 3 * HALF + OCEAN_ROWS
            out[3 * HALF : at, :] = refs[2 + n][...]
            for p_ref in (p1_ref, p2_ref):
                rows = p_ref[3 * HALF :, :]
                for i in range(4):
                    low, high = rows[4 * i : 4 * i + 2], rows[4 * i + 2 : 4 * i + 4]
                    ends = (high, low) if n == 0 else (low, high)
                    out[at : at + 2, :] = jnp.where(c1 > 0, *ends)
                    at += 2


def star_flux(star, normals, speed, inner, outer):
    size = FIELDS * 8
    y = folded(dot(star, both_parts(inner + outer)))
    flux = speed * (inner - outer)
    for c in range(3):
        flux = flux + normals[c] * y[c * size : (c + 1) * size]
    return flux


def local_flux(table_ref, partner_ref, normal_ref, speed_ref, star_ref, flux_ref, outer_ref):
    elements = partner_ref.shape[1]
    stack = table_parts(table_ref)
    codes = iota((4 * elements, elements), 0)
    star = star_ref[...]
    speed = 0.5 * speed_ref[...]
    for f in range(4):
        hot = (codes == partner_ref[f : f + 1, :]).astype(F32).astype(BF16)
        outer_ref[:, f * elements : (f + 1) * elements] = folded(dot(stack, hot))[:TABLE]
    for part in range(FACE_PAD // 8):
        at = [slice(g * FACE_PAD + 8 * part, g * FACE_PAD + 8 * part + 8) for g in range(FIELDS)]
        for f in range(4):
            normals = [0.5 * normal_ref[c, f : f + 1, :] for c in range(3)]
            columns = slice(f * elements, (f + 1) * elements)
            inner = jnp.concatenate([table_ref[rows, columns] for rows in at], axis=0)
            outer = jnp.concatenate([outer_ref[rows, columns] for rows in at], axis=0)
            flux = star_flux(star, normals, speed, inner, outer)
            for g in range(FIELDS):
                flux_ref[g, f * FACE_PAD + 8 * part : f * FACE_PAD + 8 * part + 8, :] = flux[
                    8 * g : 8 * g + 8
                ]


def remote_blocks(place, p1, p2, q1, q2):
    a1, c1 = unequal(place)
    return [
        (p1, 0, column_block(a1)),
        (p2, 0, column_block(-a1)),
        (q1, 2 * HALF, row_block(c1)),
        (q2, 2 * HALF, row_block(-c1)),
        (q1, 0, column_block(a1) + c1),
        (q1, HALF, column_block(-a1) + c1),
        (q2, 0, column_block(a1) - c1),
        (q2, HALF, column_block(-a1) - c1),
    ]


def prepared(
    place, star_ref, source_ref, deriv_ref, trace_ref, lift_ref, partner_ref,
    sea_face_ref, sea_row_ref, normal_ref, speed_ref, interp_ref,
    star4_ref, star3_ref, b1_ref, b2_ref, t_ref, l1_ref, l2_ref, hot_ref, sea_ref, slot_ref, scale_ref, uplift_ref,
):
    star, (b1_ref[...], b2_ref[...]), t_ref[...] = front_weights(
        star_ref, source_ref, deriv_ref, trace_ref
    )
    star4_ref[...] = star
    star3_ref[...] = star_weights([star_ref[0], star_ref[1], star_ref[2]])
    l1_ref[...], l2_ref[...] = lift_weights(lift_ref)
    elements = partner_ref.shape[1]
    blocks = remote_blocks(place, None, None, None, None)
    slot = iota((CAP, elements), 0)
    for f in range(4):
        wanted = partner_ref[f : f + 1, :] - 4 * elements
        hot_ref[:, f * elements : (f + 1) * elements] = jnp.concatenate(
            [(slot + CAP * block[2] == wanted).astype(F32) for block in blocks], axis=0
        ).astype(BF16)
    scales = [
        jnp.concatenate([normal_ref[c, f : f + 1, :] for f in range(4)], axis=1) for c in range(3)
    ]
    scales.append(jnp.concatenate([speed_ref[...]] * 4, axis=1))
    scales = 0.5 * jnp.concatenate(scales + [jnp.zeros((4, 4 * elements), F32)], axis=0)
    scale_ref[...] = folded(
        lax.dot_general(both_parts(scales), hot_ref[...], NT, preferred_element_type=F32)
    )
    uplift_ref[...] = side_weights(
        jnp.concatenate(
            [exact_dot(interp_ref[...], trace_ref[:, f, :]) for f in range(4)], axis=0
        )
    )
    faces = sea_face_ref.shape[1]
    sea_ref[...] = (iota((4 * elements, faces), 0) == sea_face_ref[...]).astype(F32).astype(BF16)
    row = sea_row_ref[...]
    tiles = slot_ref.shape[0]
    hits = (iota((tiles, faces), 0) == row).astype(F32)
    before = (iota((faces, faces), 0) < iota((faces, faces), 1)).astype(F32)
    count = dot(hits.astype(BF16), before.astype(BF16))
    mine = jnp.sum(count * hits, axis=0, keepdims=True).astype(jnp.int32)
    lane = iota((2 * CAP, faces), 0)
    mine = mine == lane % CAP
    for j in range(tiles):
        edges = mine & (row == jnp.where(lane < CAP, j - 1, j + 1))
        inside = mine & (row == j)
        slot_ref[j] = jnp.concatenate([edges.astype(F32), inside.astype(F32)], axis=0).astype(BF16)


def remote_flux(place, flux_ref, star_ref, hot_ref, scale_ref, arrived, packed_ref, table_ref):
    elements = hot_ref.shape[1] // 4
    blocks = remote_blocks(place, *arrived)
    left = iota((HALF, 2 * CAP), 1) < CAP
    for n in range(0, 8, 2):
        one = blocks[n][0][blocks[n][1] : blocks[n][1] + HALF, :]
        two = blocks[n + 1][0][blocks[n + 1][1] : blocks[n + 1][1] + HALF, :]
        lanes = slice(n * CAP, (n + 2) * CAP)
        packed_ref[0:HALF, lanes] = jnp.where(left, one, pltpu.roll(two, CAP, 1))
        packed_ref[HALF:, lanes] = jnp.where(left, pltpu.roll(one, CAP, 1), two)
    unpack(packed_ref, table_ref)
    star = star_ref[...]
    for part in range(FACE_PAD // 8):
        at = [slice(g * FACE_PAD + 8 * part, g * FACE_PAD + 8 * part + 8) for g in range(FIELDS)]
        for half in range(2):
            lanes = slice(4 * CAP * half, 4 * CAP * (half + 1))
            normals = [scale_ref[c : c + 1, lanes] for c in range(3)]
            outer = jnp.concatenate([table_ref[rows, lanes] for rows in at], axis=0)
            y = folded(dot(star, both_parts(outer)))
            size = FIELDS * 8
            flux = -scale_ref[3:4, lanes] * outer
            for c in range(3):
                flux = flux + normals[c] * y[c * size : (c + 1) * size]
            for g, rows in enumerate(at):
                table_ref[rows, lanes] = flux[8 * g : 8 * g + 8]
    remote = table_parts(table_ref)
    for f in range(4):
        columns = slice(f * elements, (f + 1) * elements)
        got = folded(dot(remote, hot_ref[:, columns]))
        for g in range(FIELDS):
            flux_ref[g, f * FACE_PAD : (f + 1) * FACE_PAD, :] += got[
                g * FACE_PAD : (g + 1) * FACE_PAD
            ]


def lift_weights(lift_ref):
    basis = lift_ref.shape[2]
    return weights(
        lax.dot_general(
            selector(basis, basis, 0),
            stacked_traces(lift_ref),
            NT,
            preferred_element_type=F32,
            precision=lax.Precision.HIGHEST,
        )
    )


def back(
    place, base_ref, local_ref, star_ref, l1_ref, l2_ref, hot_ref, scale_ref,
    p1_ref, p2_ref, q1_ref, q2_ref,
    state_ref, flux_ref, packed_ref, remote_ref,
):
    arrived = (p1_ref, p2_ref, q1_ref, q2_ref)
    flux_ref[...] = local_ref[...]
    remote_flux(place, flux_ref, star_ref, hot_ref, scale_ref, arrived, packed_ref, remote_ref)
    lift = l1_ref[...], l2_ref[...]
    basis = base_ref.shape[0] // FIELDS
    for g in range(FIELDS):
        rows = slice(g * basis, (g + 1) * basis)
        state_ref[rows, :] = base_ref[rows, :] - weighted(*lift, flux_ref[g])


def rates_out(vertical, uplift_ref, sea_base_ref, sea_ref, slot_ref, out_ref):
    tiles, _, faces = slot_ref.shape
    sea = side_weighted(uplift_ref[...], vertical)
    sea = jnp.concatenate([sea[f * POINTS : (f + 1) * POINTS] for f in range(4)], axis=1)
    rates = folded(dot(both_parts(sea), sea_ref[...]))
    corners = jnp.where(
        iota((8, faces), 0) == 0, sea_base_ref[0:1, :], sea_base_ref[1:2, :]
    ).astype(F32)
    sent = both_parts(jnp.concatenate([rates, corners], axis=0))
    left = iota((POINTS // 2, 2 * CAP), 1) < CAP
    left_1 = iota((1, 2 * CAP), 1) < CAP
    for j in range(tiles):
        got = folded(lax.dot_general(sent, slot_ref[j], NT, preferred_element_type=F32))
        near, own = got[:, : 2 * CAP], got[:, 2 * CAP :]
        out_ref[j, 0:POINTS, :] = near[:POINTS]
        out_ref[j, 16:24, :] = jnp.where(left, own[0:8], own[8:16])
        out_ref[j, 24:26, :] = near[POINTS : POINTS + 2]
        out_ref[j, 26:27, :] = jnp.where(left_1, own[16:17], own[17:18])
        out_ref[j, 27:32, :] = jnp.zeros((5, 2 * CAP), F32)


def finish(*refs):
    solid, sea, refs = refs[:12], refs[12:16], refs[16:]
    state_out, out_ref, state_ref, sems, *scratch = refs
    back(*solid, state_ref, *scratch)
    copy = pltpu.make_async_copy(state_ref, state_out, sems.at[0])
    copy.start()
    basis = state_ref.shape[0] // FIELDS
    vertical = state_ref[vertical_field * basis : (vertical_field + 1) * basis, :]
    rates_out(vertical, *sea, out_ref)
    copy.wait()


def forced(place, got_ref, forcing_ref, s1_ref, s2_ref):
    tiles = got_ref.shape[0]
    tile_x = forcing_ref.shape[0]
    tile_y = forcing_ref.shape[1] - 128
    left8 = iota((8, 2 * CAP), 1) < CAP
    left1 = iota((1, 2 * CAP), 1) < CAP
    tops, bottoms, xs, ys = [], [], [], []
    for s in range(0, tiles, 2):
        one, two = got_ref[s, 16:24, :], got_ref[s + 1, 16:24, :]
        tops.append(jnp.where(left8, one, pltpu.roll(two, CAP, 1)))
        bottoms.append(jnp.where(left8, pltpu.roll(one, CAP, 1), two))
        one, two = got_ref[s, 24:32, :], got_ref[s + 1, 24:32, :]
        xs.append(jnp.where(left8, one, pltpu.roll(two, CAP, 1))[2:3])
        ys.append(jnp.where(left8, pltpu.roll(one, CAP, 1), two)[2:3])
    lower, upper = jnp.concatenate(tops, axis=1), jnp.concatenate(bottoms, axis=1)
    x0, y0 = jnp.concatenate(xs, axis=1), jnp.concatenate(ys, axis=1)
    arrived = x0.shape[1]
    hot = (iota((tile_x, arrived), 0).astype(F32) == x0).astype(F32).astype(BF16)
    from_y = iota((tile_y, arrived), 0).astype(F32) - y0
    stack = []
    for pr in range(patch_side):
        source = lower if pr < 2 else upper
        value = jnp.zeros((tile_y, arrived), F32)
        for pc in range(patch_side):
            at = (pr * patch_side + pc) % 8
            value = jnp.where(from_y == pc, source[at : at + 1], value)
        stack += parts(value)
    got = lax.dot_general(jnp.concatenate(stack, axis=0), hot, NT, preferred_element_type=F32)
    total = jnp.zeros((tile_y, tile_x), F32)
    for pr in range(patch_side):
        part = folded(got[2 * pr * tile_y : 2 * (pr + 1) * tile_y])
        total += part if pr == 0 else pltpu.roll(part, pr, 1)
    total = total.T
    forcing_ref[:, :tile_y] = total
    near = jnp.concatenate([got_ref[s, 0:POINTS, :] for s in range(tiles)], axis=1)
    x0 = jnp.concatenate([got_ref[s, 24:25, :] for s in range(tiles)], axis=1)
    y0 = jnp.concatenate([got_ref[s, 25:26, :] for s in range(tiles)], axis=1)
    arrived = x0.shape[1]
    hot = (iota((tile_x, arrived), 0).astype(F32) == x0).astype(F32).astype(BF16)
    rows = iota((8, arrived), 0)
    before = iota((8, arrived), 1) % (2 * CAP) < CAP
    high_y = jnp.where(before & (rows >= 6), (rows + (tile_y - 8)).astype(F32) - y0, -1.0)
    low_y = jnp.where(before | (rows >= 2), -1.0, rows.astype(F32) - y0)
    chunks = [None] * 16
    for pr in range(patch_side):
        high, low = jnp.zeros((8, arrived), F32), jnp.zeros((8, arrived), F32)
        for pc in range(patch_side):
            at = pr * patch_side + pc
            high = jnp.where(high_y == pc, near[at : at + 1], high)
            low = jnp.where(low_y == pc, near[at : at + 1], low)
        chunks[(4 * pr - 1) % 16], chunks[4 * pr] = high, low
    blank = jnp.zeros((8, arrived), F32)
    value = jnp.concatenate([blank if c is None else c for c in chunks], axis=0)
    got = folded(lax.dot_general(both_parts(value), hot, NT, preferred_element_type=F32))
    row = iota((128, tile_x), 0)
    used = (row < 2) | (row >= 126)
    total = jnp.where(used, got, 0.0)
    for pr in range(1, patch_side):
        moved_back = pltpu.roll(pltpu.roll(got, 128 - 32 * pr, 0), pr, 1)
        total += jnp.where(used, moved_back, 0.0)
    total = total.T
    forcing_ref[:, tile_y:] = total
    a1, _ = unequal(place)
    head, tail = forcing_ref[0:8, :], forcing_ref[tile_x - 8 : tile_x, :]
    tail = pltpu.roll(tail, 2, 0)
    s1_ref[...] = jnp.where(a1 > 0, tail, head)
    s2_ref[...] = jnp.where(a1 > 0, head, tail)


def edge_rows(place, heads, tails, p1_ref, p2_ref):
    a1, _ = unequal(place)
    for i in range(4):
        head, tail = heads[i, 0:2, :], tails[i, 6:8, :]
        one = jnp.where(a1 > 0, tail, head)
        two = jnp.where(a1 > 0, head, tail)
        for h in range(2):
            at = slice(3 * HALF + 4 * i + 2 * h, 3 * HALF + 4 * i + 2 * h + 2)
            lanes = slice(128 * h, 128 * (h + 1))
            p1_ref[at, :] = one[:, lanes]
            p2_ref[at, :] = two[:, lanes]


def edge_columns(place, depth_ref, momentum_ref, bottom_ref, one_ref, two_ref):
    arrays = [depth_ref[...], momentum_ref[0], momentum_ref[1], bottom_ref[...]]
    _, c1 = unequal(place)
    tile_y = depth_ref.shape[1]
    row = iota((8, tile_y), 0)
    up = jnp.where(row < 2, row + (tile_y - 2), row - 2)
    down = jnp.where(row < 2, row, row + (tile_y - 4))
    wanted = jnp.where(c1 > 0, up, down)
    hot = ((row < 4) & (wanted == iota((8, tile_y), 1))).astype(F32)
    for i, array in enumerate(arrays):
        columns = lax.dot_general(
            hot, array, NT, preferred_element_type=F32, precision=lax.Precision.HIGHEST
        )
        for h in range(2):
            at = slice(4 * i + 2 * h, 4 * i + 2 * h + 2)
            lanes = slice(128 * h, 128 * (h + 1))
            one_ref[at, :] = columns[0:2, lanes]
            two_ref[at, :] = columns[2:4, lanes]


def widened(place, depth_ref, momentum_ref, bottom_ref, p1_ref, p2_ref, q1_ref, q2_ref, out_ref):
    tile_x, tile_y = depth_ref.shape
    a1, c1 = unequal(place)
    arrays = [depth_ref[...], momentum_ref[0], momentum_ref[1], bottom_ref[...]]
    p1, p2 = p1_ref[3 * HALF :, :], p2_ref[3 * HALF :, :]
    q1, q2 = q1_ref[3 * HALF :, :], q2_ref[3 * HALF :, :]
    is_below, is_above = place[0] > 0, place[0] < place[2] - 1
    below = jnp.where(is_below, jnp.where(a1 > 0, p2, p1), 0.0)
    above = jnp.where(is_above, jnp.where(a1 > 0, p1, p2), 0.0)
    before = jnp.where(place[1] > 0, jnp.where(c1 > 0, q2, q1), 0.0)
    after = jnp.where(place[1] < place[3] - 1, jnp.where(c1 > 0, q1, q2), 0.0)
    n = OCEAN_ROWS

    def ends(rows):
        one, two = rows[n : n + 8], rows[n + 8 :]
        return (
            jnp.where(is_below, jnp.where(a1 > 0, two, one), 0.0),
            jnp.where(is_above, jnp.where(a1 > 0, one, two), 0.0),
        )

    before_below, before_above = ends(before)
    after_below, after_above = ends(after)
    lane = iota((2, 128), 1)
    low, high = lane < 2, lane >= 126
    for i, array in enumerate(arrays):
        first, second = slice(4 * i, 4 * i + 2), slice(4 * i + 2, 4 * i + 4)
        out_ref[i, 0:MARGIN, :] = jnp.zeros((MARGIN, tile_y + 128), F32)
        out_ref[i, MARGIN + tile_x :, :] = jnp.zeros((MARGIN, tile_y + 128), F32)
        out_ref[i, MARGIN : MARGIN + tile_x, :tile_y] = array
        for at, rows, left, right in (
            (MARGIN - 2, below, before_below, after_below),
            (MARGIN + tile_x, above, before_above, after_above),
        ):
            out_ref[i, at : at + 2, 0:128] = rows[first]
            out_ref[i, at : at + 2, 128:256] = rows[second]
            end = slice(2 * i, 2 * i + 2)
            corner = jnp.where(low, right[end], jnp.where(high, left[end], 0.0))
            out_ref[i, at : at + 2, 256:384] = corner
        start = jnp.concatenate([after[first], after[second]], axis=1)
        finish = jnp.concatenate([before[first], before[second]], axis=1)
        columns = jnp.concatenate([start, jnp.zeros((124, tile_x), F32), finish], axis=0)
        out_ref[i, MARGIN : MARGIN + tile_x, tile_y:] = columns.T


STRIP = 16


def next_of(x):
    return pltpu.roll(x, x.shape[1] - 1, 1)


def previous_of(x):
    return pltpu.roll(x, 1, 1)


def cells(state, cell, low, high):
    for at in range(low, high, 8):
        here = slice(at, at + 8)
        h, mx, my = state[0, here, :], state[1, here, :], state[2, here, :]
        safe = jnp.maximum(h, depth_floor)
        root = lax.rsqrt(safe)
        inverse = root * root
        c = safe * root
        u, v = mx * inverse, my * inverse
        half = 0.5 * h * h
        cell[0, here, :] = mx * u + half
        cell[1, here, :] = my * u
        cell[2, here, :] = my * v + half
        cell[3, here, :] = 0.5 * (jnp.abs(u) + c)
        cell[4, here, :] = 0.5 * (jnp.abs(v) + c)


def moved(state, cell, face, at, rows):
    here, up = slice(at, at + rows), slice(at + 1, at + rows + 1)
    below = slice(at - 1, at + rows - 1)
    now = [state[k, here, :] for k in range(3)]
    cross = cell[1, here, :]
    next_now = [state[k, up, :] for k in range(3)]
    wave = jnp.maximum(cell[3, here, :], cell[3, up, :])
    pairs = ((now[1], next_now[1]), (cell[0, here, :], cell[0, up, :]), (cross, cell[1, up, :]))
    upper = [
        0.5 * (pairs[k][0] + pairs[k][1]) - wave * (next_now[k] - now[k]) for k in range(3)
    ]
    for k in range(3):
        face[k, here, :] = upper[k]
    flux = (now[2], cross, cell[2, here, :])
    speed = cell[4, here, :]
    wave = jnp.maximum(speed, next_of(speed))
    next_now = [next_of(x) for x in now]
    next_flux = (next_now[2], next_of(flux[1]), next_of(flux[2]))
    y_face = [
        0.5 * (flux[k] + next_flux[k]) - wave * (next_now[k] - now[k]) for k in range(3)
    ]
    return [
        now[k] - step_ocean * (upper[k] - face[k, below, :] + y_face[k] - previous_of(y_face[k]))
        for k in range(3)
    ]


def sloped(height, bed, at, rows):
    b = bed[at : at + rows, :]
    slope_x = 0.5 * (bed[at + 1 : at + rows + 1, :] - bed[at - 1 : at + rows - 1, :])
    slope_y = 0.5 * (next_of(b) - previous_of(b))
    scale = step_ocean * height
    return scale * slope_x, scale * slope_y


def ocean_cells(
    place, depth_ref, momentum_ref, bottom_ref, p1_ref, p2_ref, q1_ref, q2_ref, wide, cell
):
    widened(place, depth_ref, momentum_ref, bottom_ref, p1_ref, p2_ref, q1_ref, q2_ref, wide)
    height, span = wide.shape[1:]
    cell[:, 0:8, :] = jnp.zeros((5, 8, span), F32)
    cell[:, height - 8 :, :] = jnp.zeros((5, 8, span), F32)
    cells(wide, cell, 8, height - 8)


def ocean_first(place, wide, cell, state, face):
    tile_x, tile_y = wide.shape[1] - 2 * MARGIN, wide.shape[2] - 128
    height, span = wide.shape[1:]
    lane = iota((STRIP, span), 1)
    outside = ((lane == span - 1) & (place[1] == 0)) | (
        (lane == tile_y) & (place[1] == place[3] - 1)
    )
    state[:, 0:8, :] = jnp.zeros((3, 8, span), F32)
    state[:, height - 8 :, :] = jnp.zeros((3, 8, span), F32)
    face[:, 0:8, :] = jnp.zeros((3, 8, span), F32)
    for at in range(8, height - 8, STRIP):
        new = moved(wide, cell, face, at, STRIP)
        row = iota((STRIP, span), 0) + at
        out = outside | ((row < MARGIN) & (place[0] == 0))
        out = out | ((row >= MARGIN + tile_x) & (place[0] == place[2] - 1))
        for k in range(3):
            state[k, at : at + STRIP, :] = jnp.where(out, 0.0, new[k])


def second_step(wide, first, bed, state, cell, face, rows, put, raise_bed):
    low, high = rows.start - 8, rows.stop + 8
    raise_bed(wide.at[3])
    for at in range(low, high, STRIP):
        here = slice(at, at + STRIP)
        change_x, change_y = sloped(wide[0, here, :], bed, at, STRIP)
        state[0, here, :] = first[0, here, :]
        state[1, here, :] = first[1, here, :] - change_x
        state[2, here, :] = first[2, here, :] - change_y
    cells(state, cell, low, high)
    raise_bed(bed)
    moved(state, cell, face, low, 8)
    for at in range(rows.start, rows.stop, STRIP):
        new = moved(state, cell, face, at, STRIP)
        change_x, change_y = sloped(state[0, at : at + STRIP, :], bed, at, STRIP)
        new[1] -= change_x
        new[2] -= change_y
        put(at, new)


def ocean_inner(wide, first, forcing_ref, out_ref, bed_ref, state, bed, cell, face):
    tile_x, tile_y = bed_ref.shape
    inner = slice(MARGIN, MARGIN + tile_x)
    bed[...] = wide[3]

    def raise_bed(source):
        bed[inner, :] = source[inner, :] + step_ocean * forcing_ref[...]

    def put(at, new):
        for k in range(3):
            out_ref[k, at - MARGIN : at - MARGIN + STRIP, :] = new[k][:, :tile_y]

    rows = slice(MARGIN + STRIP, MARGIN + tile_x - STRIP)
    second_step(wide, first, bed, state, cell, face, rows, put, raise_bed)
    bed_ref[...] = bed[inner, :tile_y]


def ocean_ends(
    place, wide, first, forcing_ref, s1_ref, s2_ref, inner_ref, raised_ref, out_hbm, bed_hbm,
    out_ref, bed_ref, sems, state, bed, cell, face,
):
    tile_x, tile_y = raised_ref.shape
    last = tile_x - STRIP
    middle = pl.ds(STRIP, tile_x - 2 * STRIP)
    copies = [
        pltpu.make_async_copy(raised_ref, bed_hbm, sems.at[0]),
        pltpu.make_async_copy(inner_ref.at[:, middle], out_hbm.at[:, middle], sems.at[1]),
    ]
    for copy in copies:
        copy.start()
    a1, _ = unequal(place)
    force_lo = step_ocean * jnp.where(a1 > 0, s2_ref[...], s1_ref[...])[0:2]
    force_lo = jnp.where(place[0] > 0, force_lo, 0.0)
    force_hi = step_ocean * jnp.where(a1 > 0, s1_ref[...], s2_ref[...])[0:2]
    force_hi = jnp.where(place[0] < place[2] - 1, force_hi, 0.0)

    def put(at, new):
        for k in range(3):
            out_ref[k, at - MARGIN : at - MARGIN + STRIP, :] = new[k][:, :tile_y]

    for n, start in enumerate((MARGIN, MARGIN + last)):
        outer = slice(start - 16, start) if n == 0 else slice(start + STRIP, start + STRIP + 16)
        edge = slice(MARGIN - 2, MARGIN) if n == 0 else slice(MARGIN + tile_x, MARGIN + tile_x + 2)
        force = force_lo if n == 0 else force_hi
        own = slice(start, start + 32) if n == 0 else slice(start - 16, start + 16)
        forcing = forcing_ref[own.start - MARGIN : own.stop - MARGIN, :]
        bed[outer, :] = wide[3, outer, :]

        def raise_bed(source):
            bed[own, :] = source[own, :] + step_ocean * forcing
            bed[edge, :] = source[edge, :] + force

        second_step(
            wide, first, bed, state, cell, face, slice(start, start + STRIP), put, raise_bed
        )
        at = pl.ds(start - MARGIN, STRIP)
        copies.append(pltpu.make_async_copy(out_ref.at[:, at], out_hbm.at[:, at], sems.at[2 + n]))
        copies[-1].start()
    for copy in copies:
        copy.wait()


def call(
    body, out_shape, *args, place=None, scratch=(), held=0, sent=0, copies=0, limit=VMEM_LIMIT
):
    out_space = [pltpu.HBM if i < sent else pltpu.VMEM for i in range(len(out_shape))]
    specs = [pl.BlockSpec(memory_space=pltpu.HBM if held else pltpu.VMEM) for _ in args]
    shapes = [
        s if isinstance(s, jax.ShapeDtypeStruct) else jax.ShapeDtypeStruct(s, F32) for s in out_shape
    ]
    scratch = [pltpu.VMEM(s, F32) for s in scratch]
    if copies:
        scratch = [pltpu.SemaphoreType.DMA((copies,))] + scratch
    scratch = [pltpu.VMEM(x.shape, x.dtype) for x in [*args[:held], *shapes[:sent]]] + scratch
    if place is not None:
        sizes, inner = place, body

        def body(*refs):
            here = (lax.axis_index("gx"), lax.axis_index("gy"))
            inner(here + sizes, *refs)

    return pl.pallas_call(
        body,
        out_shape=shapes,
        in_specs=specs,
        out_specs=[pl.BlockSpec(memory_space=space) for space in out_space],
        scratch_shapes=scratch,
        compiler_params=pltpu.CompilerParams(vmem_limit_bytes=limit),
    )(*args)


def swap(block, axis, parity, wrap=False):
    count = lax.axis_size(axis)
    last = count + parity - 1 if wrap else count - 1
    pairs = []
    for i in range(parity, last, 2):
        pairs += [(i, (i + 1) % count), ((i + 1) % count, i)]
    taken = {source for source, _ in pairs}
    pairs += [(i, i) for i in range(count) if i not in taken]
    return lax.ppermute(block, axis, pairs)


def per_device(
    coefficients,
    jacobian,
    face_normals,
    wave_speed,
    star_mats,
    deriv_mats,
    stiff_mats,
    source_mat,
    trace_mats,
    lift_mats,
    face_partner,
    send_faces,
    sea_face,
    sea_row,
    sea_base,
    interp_mat,
    water_depth,
    momentum,
    bottom,
):
    basis, elements = coefficients.shape[1:]
    rows = FIELDS * basis
    tile_x, tile_y = water_depth.shape
    tiles = lax.axis_size("gy")
    place = (lax.axis_size("gx"), tiles)
    speed = wave_speed.reshape(1, elements)
    traces = trace_mats.transpose(1, 0, 2)
    normals = face_normals.transpose(1, 0, 2)
    lifts = lift_mats.transpose(2, 0, 1)
    spread = (FIELDS, 3 * basis, elements)
    faces = (TABLE, 4 * elements)
    solid = (rows, elements)
    wide_shape = (tile_x + 2 * MARGIN, tile_y + 128)
    state = coefficients.reshape(solid)
    packed = (2 * HALF, 8 * CAP)
    flux_shape = (FIELDS, 4 * FACE_PAD, elements)
    for section in range(2):
        scratch = [spread, solid, solid, solid, (2 * HALF, 4 * CAP)]
        if section == 0:
            fixed = (state, jacobian, star_mats, source_mat, deriv_mats, traces, send_faces)
            buffers = [(3 * HALF + OCEAN_ROWS, 128)] * 2 + [(HALF, 128)] * 2
            integral, table, p1, p2, own1, own2 = call(
                start, [solid, faces] + buffers, *fixed, water_depth, momentum, bottom,
                place=place, scratch=[(4, 8, tile_y)] * 2 + scratch,
                held=len(fixed), sent=6, copies=len(fixed) + 14, limit=START_LIMIT,
            )
        else:
            buffers = [(3 * HALF, 128)] * 2 + [(HALF, 128)] * 2
            integral, table, p1, p2, own1, own2 = call(
                front_again, [solid, faces] + buffers,
                state, jacobian, star4, *derivs, *traced, send_faces, place=place, scratch=scratch,
            )
        p2, p1 = swap(p2, "gx", 1), swap(p1, "gx", 0)
        inside = (state, jacobian, star_mats, stiff_mats, integral)
        (base,) = call(volume, [solid], *inside, scratch=[spread])
        if section == 0:
            columns = call(
                edge_columns, [(OCEAN_ROWS, 128)] * 2, water_depth, momentum, bottom, place=place
            )
            size = 3 * HALF + 2 * OCEAN_ROWS
        else:
            columns, size = [], 3 * HALF
            wide, cell = call(
                ocean_cells,
                [(4,) + wide_shape, (5,) + wide_shape],
                water_depth, momentum, bottom, *halos,
                place=place,
            )
            base, wide, cell = lax.optimization_barrier((base, wide, cell))
        p1, p2, base = lax.optimization_barrier((p1, p2, base))
        q1, q2 = call(forward, [(size, 128)] * 2, p1, p2, own1, own2, *columns, place=place)
        q2, q1 = swap(q2, "gy", 1), swap(q1, "gy", 0)
        if section == 1:
            (flux,) = call(
                local_flux, [flux_shape], table, face_partner, normals, speed, star3,
                scratch=[faces],
            )
            (first,) = call(
                ocean_first,
                [(3,) + wide_shape],
                wide, cell,
                place=place, scratch=[(3,) + wide_shape],
            )
            q1, q2, flux, first = lax.optimization_barrier((q1, q2, flux, first))
        else:
            half = lambda *shape: jax.ShapeDtypeStruct(shape, BF16)
            size, sea = FIELDS * 8, sea_face.shape[0]
            star4, star3, *ready = call(
                prepared,
                [half(16 * (FIELDS + FIELDS % 2), 12 * (FIELDS + FIELDS % 2)), half(6 * size, 2 * size)]
                + [half(2 * basis, 3 * basis), half(basis, 3 * basis)]
                + [half(4 * FACE_PAD, 3 * basis)]
                + [half(2 * basis, 4 * FACE_PAD), half(basis, 4 * FACE_PAD)]
                + [half(8 * CAP, 4 * elements), half(4 * elements, sea), half(tiles, 4 * CAP, sea), (8, 8 * CAP)]
                + [half(4 * POINTS, 3 * basis)],
                star_mats, source_mat, deriv_mats, traces, lifts, face_partner,
                sea_face.reshape(1, -1), sea_row.T, normals, speed, interp_mat,
                place=place,
            )
            (flux,) = call(
                local_flux, [flux_shape], table, face_partner, normals, speed, star3,
                scratch=[faces],
            )
            q1, q2, flux, *ready = lax.optimization_barrier((q1, q2, flux, *ready))
            derivs, traced, lifting, (hot, sea_hot, slot_hot, scales, uplift) = (
                ready[0:2], ready[2:3], ready[3:5], ready[5:],
            )
        fixed = (star3, *lifting, hot, scales)
        arrived = (p1, p2, q1, q2)
        remote = (TABLE, 8 * CAP)
        if section == 0:
            (state,) = call(
                back, [solid], base, flux, *fixed, *arrived,
                place=place, scratch=[flux_shape, packed, remote],
            )
            halos = (p1, p2, q1, q2)
        else:
            state, outgoing = call(
                finish,
                [solid, (tiles, 32, 128)],
                base, flux, *fixed, *arrived,
                uplift, sea_base.T, sea_hot, slot_hot,
                place=place, scratch=[flux_shape, packed, remote], sent=1, copies=1,
            )
    incoming = lax.all_to_all(outgoing, "gy", split_axis=0, concat_axis=0, tiled=True)
    forcing, s1, s2 = call(
        forced,
        [(tile_x, tile_y + 128), (8, tile_y + 128), (8, tile_y + 128)],
        incoming,
        place=place,
    )
    s2, s1 = swap(s2, "gx", 1, wrap=True), swap(s1, "gx", 0)
    scratch = [(3,) + wide_shape, wide_shape, (5,) + wide_shape, (3,) + wide_shape]
    water = [(3, tile_x, tile_y), (tile_x, tile_y)]
    inner, raised = call(ocean_inner, water, wide, first, forcing, scratch=scratch)
    ocean_final, bed_final = call(
        ocean_ends, water, wide, first, forcing, s1, s2, inner, raised,
        place=place, scratch=scratch, sent=2, copies=4,
    )
    return (state.reshape(coefficients.shape), ocean_final, bed_final)


def solution(mesh):
    in_specs = (
        P(None, None, ("gx", "gy")),
        P(None, None, ("gx", "gy")),
        P(None, None, ("gx", "gy")),
        P(("gx", "gy")),
        P(),
        P(),
        P(),
        P(),
        P(),
        P(),
        P(None, ("gx", "gy")),
        P(None, ("gx", "gy")),
        P(("gx", "gy")),
        P(("gx", "gy"), None),
        P(("gx", "gy"), None),
        P(),
        P("gx", "gy"),
        P(None, "gx", "gy"),
        P("gx", "gy"),
    )
    out_specs = (P(None, None, ("gx", "gy")), P(None, "gx", "gy"), P("gx", "gy"))
    return jax.shard_map(
        per_device, mesh=mesh, in_specs=in_specs, out_specs=out_specs, check_vma=False
    )
```

```python
import jax
import jax.numpy as jnp
from jax import lax
from jax.experimental import pallas as pl
from jax.experimental.pallas import tpu as pltpu
from jax.sharding import PartitionSpec as P

FIELDS = 13
FACE_BASIS = 21
FACE_PAD = 24
POINTS = 16
ORD = 3
STEPS_OCEAN = 2
CAP = 64
TABLE = FIELDS * FACE_PAD
HALF = (FIELDS * FACE_BASIS + 1) // 2
OCEAN_ROWS = 16
MARGIN = 16
FOUR = 4

step_solid = 0.4
step_ocean = 0.2
depth_floor = 0.5
vertical_field = 6
patch_side = 4

F32 = jnp.float32
BF16 = jnp.bfloat16
NT = (((1,), (1,)), ((), ()))
VMEM_LIMIT = 24 * 1024 * 1024
START_LIMIT = 62 * 1024 * 1024


def iota(shape, dim):
    return lax.broadcasted_iota(jnp.int32, shape, dim)


def dot(a, b):
    return jnp.dot(a, b, preferred_element_type=F32)


def exact_dot(a, b):
    return jnp.dot(a, b, preferred_element_type=F32, precision=lax.Precision.HIGHEST)


def parts(x):
    high = x.astype(BF16)
    low = (x - high.astype(F32)).astype(BF16)
    return high, low


def both_parts(x):
    high = x.astype(BF16).astype(F32)
    return jnp.concatenate([high, x - high], axis=0).astype(BF16)


def folded(y):
    half = y.shape[0] // 2
    return y[:half] + y[half:]


def weights(w):
    return both_parts(w), w.astype(BF16)


def weighted(stack, high, x):
    x_high, x_low = parts(x)
    return folded(dot(stack, x_high)) + dot(high, x_low)


def side_weights(w):
    columns = w.shape[1]
    high, low = parts(w)
    place = [selector(columns, 3 * columns, i * columns).astype(BF16) for i in range(3)]
    return (dot(high, place[0] + place[1]) + dot(low, place[2])).astype(BF16)


def side_weighted(stack, x):
    high = x.astype(BF16).astype(F32)
    return dot(stack, jnp.concatenate([high, x - high, high], axis=0).astype(BF16))


def selector(rows, columns, shift):
    return (iota((rows, columns), 1) == iota((rows, columns), 0) + shift).astype(F32)


def star_weights(mats):
    size = FIELDS * 8
    spread = ((iota((FIELDS, 2 * size), 1) % size) // 8 == iota((FIELDS, 2 * size), 0)).astype(F32)
    diagonal = iota((size, 2 * size), 0) % 8 == iota((size, 2 * size), 1) % 8
    first = iota((size, 2 * size), 1) < size
    high, low = [], []
    for mat in mats:
        wide = exact_dot(mat, spread)
        tall = jnp.concatenate(
            [jnp.broadcast_to(wide[g : g + 1], (8, 2 * size)) for g in range(FIELDS)], axis=0
        )
        tall = jnp.where(diagonal, tall, 0.0)
        top = tall.astype(BF16).astype(F32)
        high.append(top)
        low.append(jnp.where(first, tall - top, 0.0))
    return jnp.concatenate(high + low, axis=0).astype(BF16)


def side_by_side(mats):
    rows, columns = mats[0].shape
    total = len(mats) * columns
    return sum(exact_dot(m, selector(columns, total, i * columns)) for i, m in enumerate(mats))


def stacked_traces(trace_ref):
    place = (
        iota((FACE_PAD, FACE_BASIS), 0) == iota((FACE_PAD, FACE_BASIS), 1)
    ).astype(F32)
    return jnp.concatenate([exact_dot(place, trace_ref[:, f, :]) for f in range(4)], axis=0)


def star_quarters(mats):
    size = FOUR * (FIELDS + FIELDS % 2)
    columns = 3 * size
    spread = ((iota((FIELDS, columns), 1) % size) // FOUR == iota((FIELDS, columns), 0)).astype(F32)
    upper = iota((8, columns), 0) < FOUR
    diagonal = iota((size, columns), 0) % FOUR == iota((size, columns), 1) % FOUR
    first = iota((size, columns), 1) < 2 * size
    out = []
    for mat in mats:
        wide = exact_dot(mat, spread)
        wide = [jnp.broadcast_to(wide[g : g + 1], (8, columns)) for g in range(FIELDS)]
        wide += [jnp.zeros((8, columns), F32)] * (FIELDS % 2)
        tall = jnp.concatenate(
            [jnp.where(upper, wide[g], wide[g + 1]) for g in range(0, FIELDS, 2)], axis=0
        )
        tall = jnp.where(diagonal, tall, 0.0)
        high = tall.astype(BF16).astype(F32)
        out.append(jnp.where(first, high, tall - high))
    return jnp.concatenate(out, axis=0).astype(BF16)


def interleaved(one, two, upper):
    return jnp.where(upper, one, pltpu.roll(two, FOUR, 0)), jnp.where(
        upper, pltpu.roll(one, FOUR, 0), two
    )


def spread_out(source, jac_ref, star, target, extra=None):
    basis = target.shape[1] // 3
    lanes = target.shape[2]
    pairs = (FIELDS + 1) // 2
    size = 8 * pairs
    upper = iota((8, lanes), 0) < FOUR
    for j in range(basis // 8):
        x = [source[g * basis + 8 * j : g * basis + 8 * j + 8, :] for g in range(FIELDS)]
        x += [jnp.zeros((8, lanes), F32)] * (2 * pairs - FIELDS)
        mixed = [interleaved(x[2 * p], x[2 * p + 1], upper) for p in range(pairs)]
        halves = []
        for half in range(2):
            y = side_weighted(star, jnp.concatenate([m[half] for m in mixed], axis=0))
            z = [
                sum(jac_ref[d, c : c + 1, :] * y[c * size : (c + 1) * size] for c in range(3))
                for d in range(3)
            ]
            halves.append(z + ([] if extra is None else [y[3 * size :]]))
        for d, (one, two) in enumerate(zip(*halves)):
            for p in range(pairs):
                rows = slice(8 * p, 8 * p + 8)
                for g, value in zip(
                    range(2 * p, FIELDS), interleaved(one[rows], two[rows], upper)
                ):
                    if d < 3:
                        target[g, d * basis + 8 * j : d * basis + 8 * j + 8, :] = value
                    else:
                        extra[g * basis + 8 * j : g * basis + 8 * j + 8, :] = value


def derivative(source, target, jac_ref, star, basis_weights, spread_ref, relaxed_ref):
    basis = spread_ref.shape[1] // 3
    spread_out(source, jac_ref, star, spread_ref, relaxed_ref)
    for g in range(FIELDS):
        rows = slice(g * basis, (g + 1) * basis)
        target[rows, :] = -(weighted(*basis_weights, spread_ref[g]) + relaxed_ref[rows, :])


def unequal(place):
    a1 = jnp.where(place[0] % 2 == 0, 1, -1)
    c1 = jnp.where(place[1] % 2 == 0, 1, -1)
    return a1, c1


def column_block(a):
    return jnp.where(a > 0, 6, 1)


def row_block(c):
    return jnp.where(c > 0, 4, 3)


def front_weights(star_ref, source_ref, deriv_ref, trace_ref, ready=lambda *numbers: None):
    ready(2, 3)
    star = star_quarters([star_ref[0], star_ref[1], star_ref[2], source_ref[...]])
    ready(4, 5)
    basis_weights = weights(side_by_side([deriv_ref[d] for d in range(3)]))
    return star, basis_weights, side_weights(stacked_traces(trace_ref))


def front_again(place, q_ref, jac_ref, star_ref, b1_ref, b2_ref, trace_ref, *refs):
    held = star_ref[...], (b1_ref[...], b2_ref[...]), trace_ref[...]
    front(place, held, q_ref, jac_ref, *refs)


def front(
    place, held, q_ref, jac_ref, send_ref,
    integral_ref, table_ref, p1_ref, p2_ref, own1_ref, own2_ref,
    spread_ref, relaxed_ref, d1_ref, d2_ref, packed_ref, ready=lambda *numbers: None, made=lambda *numbers: None,
):
    elements = q_ref.shape[1]
    basis = q_ref.shape[0] // FIELDS
    star, basis_weights, trace = held
    ready(0, 1)
    derivative(q_ref, d1_ref, jac_ref, star, basis_weights, spread_ref, relaxed_ref)
    derivative(d1_ref, d2_ref, jac_ref, star, basis_weights, spread_ref, relaxed_ref)
    first = step_solid
    second = first * step_solid / 2
    third = second * step_solid / 3
    for g in range(FIELDS):
        rows = slice(g * basis, (g + 1) * basis)
        whole = first * q_ref[rows, :] + second * d1_ref[rows, :] + third * d2_ref[rows, :]
        integral_ref[rows, :] = whole
        faces = side_weighted(trace, whole)
        for f in range(4):
            table_ref[g * FACE_PAD : (g + 1) * FACE_PAD, f * elements : (f + 1) * elements] = faces[
                f * FACE_PAD : (f + 1) * FACE_PAD
            ]
    made(0, 1)
    ready(6)
    a1, c1 = unequal(place)
    picks = [
        (p1_ref, 0, column_block(a1)),
        (p2_ref, 0, column_block(-a1)),
        (p1_ref, HALF, column_block(a1) + c1),
        (p1_ref, 2 * HALF, column_block(a1) - c1),
        (p2_ref, HALF, column_block(-a1) + c1),
        (p2_ref, 2 * HALF, column_block(-a1) - c1),
        (own1_ref, 0, row_block(c1)),
        (own2_ref, 0, row_block(-c1)),
    ]
    stack = table_parts(table_ref)
    left = iota((HALF, 2 * CAP), 1) < CAP
    codes = iota((4 * elements, 4 * CAP), 0)
    packed_ref[FIELDS * FACE_BASIS :, :] = jnp.zeros((2 * HALF - FIELDS * FACE_BASIS, 4 * CAP), F32)
    for n in range(0, 8, 4):
        wanted = jnp.concatenate([send_ref[pl.ds(pick[2], 1), :] for pick in picks[n : n + 4]], axis=1)
        got = folded(dot(stack, (codes == wanted).astype(F32).astype(BF16)))
        pack(got, packed_ref)
        for pair in range(2):
            lanes = slice(pair * 2 * CAP, (pair + 1) * 2 * CAP)
            low, high = packed_ref[0:HALF, lanes], packed_ref[HALF:, lanes]
            ref, at, _ = picks[n + 2 * pair]
            ref[at : at + HALF, :] = jnp.where(left, low, pltpu.roll(high, CAP, 1))
            ref, at, _ = picks[n + 2 * pair + 1]
            ref[at : at + HALF, :] = jnp.where(left, pltpu.roll(low, CAP, 1), high)


def pack(table, packed_ref):
    rest = FACE_BASIS - 16
    for g in range(FIELDS):
        packed_ref[16 * g : 16 * (g + 1), :] = table[FACE_PAD * g : FACE_PAD * g + 16]
        at = 16 * FIELDS + rest * g
        packed_ref[at : at + rest, :] = table[FACE_PAD * g + 16 : FACE_PAD * g + FACE_BASIS]


def unpack(packed_ref, table_ref):
    rest = FACE_BASIS - 16
    for g in range(FIELDS):
        table_ref[FACE_PAD * g : FACE_PAD * g + 16, :] = packed_ref[16 * g : 16 * (g + 1), :]
        at = 16 * FIELDS + rest * g
        last = FACE_PAD * g + 16
        table_ref[last : last + 8, :] = jnp.zeros((8, table_ref.shape[1]), F32)
        table_ref[last : last + rest, :] = packed_ref[at : at + rest, :]


def start(place, *refs):
    sources, water, refs = refs[:7], refs[7:10], refs[10:]
    targets, refs = refs[:6], refs[6:]
    held, outs, (sems, heads, tails, *scratch) = refs[:7], refs[7:13], refs[13:]
    depth, momentum, bottom = water
    last = depth.shape[0] - 8
    pairs = [(sources[i], held[i]) for i in range(7)]
    for rows, target in ((pl.ds(0, 8), heads), (pl.ds(last, 8), tails)):
        pairs += [
            (depth.at[rows], target.at[0]),
            (momentum.at[0, rows], target.at[1]),
            (momentum.at[1, rows], target.at[2]),
            (bottom.at[rows], target.at[3]),
        ]
    first_out = len(pairs)
    pairs += list(zip(outs, targets))
    copies = [pltpu.make_async_copy(a, b, sems.at[i]) for i, (a, b) in enumerate(pairs)]
    for copy in copies[:first_out]:
        copy.start()

    def ready(*numbers):
        for i in numbers:
            copies[i].wait()

    def made(*numbers):
        for i in numbers:
            copies[first_out + i].start()

    ready_weights = front_weights(*held[2:6], ready=ready)
    front(place, ready_weights, *held[:2], held[6], *outs, *scratch, ready=ready, made=made)
    ready(*range(7, first_out))
    edge_rows(place, heads, tails, *outs[2:4])
    made(2, 3, 4, 5)
    ready(*range(first_out, len(copies)))


def table_parts(table_ref):
    return both_parts(table_ref[...])


def volume(q_ref, jac_ref, star_ref, stiff_ref, integral_ref, base_ref, spread_ref):
    basis = stiff_ref.shape[1]
    star = star_quarters([star_ref[0], star_ref[1], star_ref[2]])
    basis_weights = weights(side_by_side([stiff_ref[d] for d in range(3)]))
    spread_out(integral_ref, jac_ref, star, spread_ref)
    for g in range(FIELDS):
        rows = slice(g * basis, (g + 1) * basis)
        base_ref[rows, :] = q_ref[rows, :] + weighted(*basis_weights, spread_ref[g])


def forward(place, p1_ref, p2_ref, *refs):
    outs = refs[-2:]
    _, c1 = unequal(place)
    for n, out in enumerate(outs):
        at = slice((n + 1) * HALF, (n + 2) * HALF)
        out[0:HALF, :] = p1_ref[at, :]
        out[HALF : 2 * HALF, :] = p2_ref[at, :]
        out[2 * HALF : 3 * HALF, :] = refs[n][...]
        if len(refs) > 4:
            at = 3 * HALF + OCEAN_ROWS
            out[3 * HALF : at, :] = refs[2 + n][...]
            for p_ref in (p1_ref, p2_ref):
                rows = p_ref[3 * HALF :, :]
                for i in range(4):
                    low, high = rows[4 * i : 4 * i + 2], rows[4 * i + 2 : 4 * i + 4]
                    ends = (high, low) if n == 0 else (low, high)
                    out[at : at + 2, :] = jnp.where(c1 > 0, *ends)
                    at += 2


def star_flux(star, normals, speed, inner, outer):
    size = FIELDS * 8
    y = folded(dot(star, both_parts(inner + outer)))
    flux = speed * (inner - outer)
    for c in range(3):
        flux = flux + normals[c] * y[c * size : (c + 1) * size]
    return flux


def local_flux(table_ref, partner_ref, normal_ref, speed_ref, star_ref, flux_ref, outer_ref):
    elements = partner_ref.shape[1]
    stack = table_parts(table_ref)
    codes = iota((4 * elements, elements), 0)
    star = star_ref[...]
    speed = 0.5 * speed_ref[...]
    for f in range(4):
        hot = (codes == partner_ref[f : f + 1, :]).astype(F32).astype(BF16)
        outer_ref[:, f * elements : (f + 1) * elements] = folded(dot(stack, hot))[:TABLE]
    for part in range(FACE_PAD // 8):
        at = [slice(g * FACE_PAD + 8 * part, g * FACE_PAD + 8 * part + 8) for g in range(FIELDS)]
        for f in range(4):
            normals = [0.5 * normal_ref[c, f : f + 1, :] for c in range(3)]
            columns = slice(f * elements, (f + 1) * elements)
            inner = jnp.concatenate([table_ref[rows, columns] for rows in at], axis=0)
            outer = jnp.concatenate([outer_ref[rows, columns] for rows in at], axis=0)
            flux = star_flux(star, normals, speed, inner, outer)
            for g in range(FIELDS):
                flux_ref[g, f * FACE_PAD + 8 * part : f * FACE_PAD + 8 * part + 8, :] = flux[
                    8 * g : 8 * g + 8
                ]


def remote_blocks(place, p1, p2, q1, q2):
    a1, c1 = unequal(place)
    return [
        (p1, 0, column_block(a1)),
        (p2, 0, column_block(-a1)),
        (q1, 2 * HALF, row_block(c1)),
        (q2, 2 * HALF, row_block(-c1)),
        (q1, 0, column_block(a1) + c1),
        (q1, HALF, column_block(-a1) + c1),
        (q2, 0, column_block(a1) - c1),
        (q2, HALF, column_block(-a1) - c1),
    ]


def prepared(
    place, star_ref, source_ref, deriv_ref, trace_ref, lift_ref, partner_ref,
    sea_face_ref, sea_row_ref, normal_ref, speed_ref, interp_ref,
    star4_ref, star3_ref, b1_ref, b2_ref, t_ref, l1_ref, l2_ref, hot_ref, sea_ref, slot_ref, scale_ref, uplift_ref,
):
    star, (b1_ref[...], b2_ref[...]), t_ref[...] = front_weights(
        star_ref, source_ref, deriv_ref, trace_ref
    )
    star4_ref[...] = star
    star3_ref[...] = star_weights([star_ref[0], star_ref[1], star_ref[2]])
    l1_ref[...], l2_ref[...] = lift_weights(lift_ref)
    elements = partner_ref.shape[1]
    blocks = remote_blocks(place, None, None, None, None)
    slot = iota((CAP, elements), 0)
    for f in range(4):
        wanted = partner_ref[f : f + 1, :] - 4 * elements
        hot_ref[:, f * elements : (f + 1) * elements] = jnp.concatenate(
            [(slot + CAP * block[2] == wanted).astype(F32) for block in blocks], axis=0
        ).astype(BF16)
    scales = [
        jnp.concatenate([normal_ref[c, f : f + 1, :] for f in range(4)], axis=1) for c in range(3)
    ]
    scales.append(jnp.concatenate([speed_ref[...]] * 4, axis=1))
    scales = 0.5 * jnp.concatenate(scales + [jnp.zeros((4, 4 * elements), F32)], axis=0)
    scale_ref[...] = folded(
        lax.dot_general(both_parts(scales), hot_ref[...], NT, preferred_element_type=F32)
    )
    uplift_ref[...] = side_weights(
        jnp.concatenate(
            [exact_dot(interp_ref[...], trace_ref[:, f, :]) for f in range(4)], axis=0
        )
    )
    faces = sea_face_ref.shape[1]
    sea_ref[...] = (iota((4 * elements, faces), 0) == sea_face_ref[...]).astype(F32).astype(BF16)
    row = sea_row_ref[...]
    tiles = slot_ref.shape[0]
    hits = (iota((tiles, faces), 0) == row).astype(F32)
    before = (iota((faces, faces), 0) < iota((faces, faces), 1)).astype(F32)
    count = dot(hits.astype(BF16), before.astype(BF16))
    mine = jnp.sum(count * hits, axis=0, keepdims=True).astype(jnp.int32)
    lane = iota((2 * CAP, faces), 0)
    mine = mine == lane % CAP
    for j in range(tiles):
        edges = mine & (row == jnp.where(lane < CAP, j - 1, j + 1))
        inside = mine & (row == j)
        slot_ref[j] = jnp.concatenate([edges.astype(F32), inside.astype(F32)], axis=0).astype(BF16)


def remote_flux(place, flux_ref, star_ref, hot_ref, scale_ref, arrived, packed_ref, table_ref):
    elements = hot_ref.shape[1] // 4
    blocks = remote_blocks(place, *arrived)
    left = iota((HALF, 2 * CAP), 1) < CAP
    for n in range(0, 8, 2):
        one = blocks[n][0][blocks[n][1] : blocks[n][1] + HALF, :]
        two = blocks[n + 1][0][blocks[n + 1][1] : blocks[n + 1][1] + HALF, :]
        lanes = slice(n * CAP, (n + 2) * CAP)
        packed_ref[0:HALF, lanes] = jnp.where(left, one, pltpu.roll(two, CAP, 1))
        packed_ref[HALF:, lanes] = jnp.where(left, pltpu.roll(one, CAP, 1), two)
    unpack(packed_ref, table_ref)
    star = star_ref[...]
    for part in range(FACE_PAD // 8):
        at = [slice(g * FACE_PAD + 8 * part, g * FACE_PAD + 8 * part + 8) for g in range(FIELDS)]
        for half in range(2):
            lanes = slice(4 * CAP * half, 4 * CAP * (half + 1))
            normals = [scale_ref[c : c + 1, lanes] for c in range(3)]
            outer = jnp.concatenate([table_ref[rows, lanes] for rows in at], axis=0)
            y = folded(dot(star, both_parts(outer)))
            size = FIELDS * 8
            flux = -scale_ref[3:4, lanes] * outer
            for c in range(3):
                flux = flux + normals[c] * y[c * size : (c + 1) * size]
            for g, rows in enumerate(at):
                table_ref[rows, lanes] = flux[8 * g : 8 * g + 8]
    remote = table_parts(table_ref)
    for f in range(4):
        columns = slice(f * elements, (f + 1) * elements)
        got = folded(dot(remote, hot_ref[:, columns]))
        for g in range(FIELDS):
            flux_ref[g, f * FACE_PAD : (f + 1) * FACE_PAD, :] += got[
                g * FACE_PAD : (g + 1) * FACE_PAD
            ]


def lift_weights(lift_ref):
    basis = lift_ref.shape[2]
    return weights(
        lax.dot_general(
            selector(basis, basis, 0),
            stacked_traces(lift_ref),
            NT,
            preferred_element_type=F32,
            precision=lax.Precision.HIGHEST,
        )
    )


def back(
    place, base_ref, local_ref, star_ref, l1_ref, l2_ref, hot_ref, scale_ref,
    p1_ref, p2_ref, q1_ref, q2_ref,
    state_ref, flux_ref, packed_ref, remote_ref,
):
    arrived = (p1_ref, p2_ref, q1_ref, q2_ref)
    flux_ref[...] = local_ref[...]
    remote_flux(place, flux_ref, star_ref, hot_ref, scale_ref, arrived, packed_ref, remote_ref)
    lift = l1_ref[...], l2_ref[...]
    basis = base_ref.shape[0] // FIELDS
    for g in range(FIELDS):
        rows = slice(g * basis, (g + 1) * basis)
        state_ref[rows, :] = base_ref[rows, :] - weighted(*lift, flux_ref[g])


def rates_out(vertical, uplift_ref, sea_base_ref, sea_ref, slot_ref, out_ref):
    tiles, _, faces = slot_ref.shape
    sea = side_weighted(uplift_ref[...], vertical)
    sea = jnp.concatenate([sea[f * POINTS : (f + 1) * POINTS] for f in range(4)], axis=1)
    rates = folded(dot(both_parts(sea), sea_ref[...]))
    corners = jnp.where(
        iota((8, faces), 0) == 0, sea_base_ref[0:1, :], sea_base_ref[1:2, :]
    ).astype(F32)
    sent = both_parts(jnp.concatenate([rates, corners], axis=0))
    left = iota((POINTS // 2, 2 * CAP), 1) < CAP
    left_1 = iota((1, 2 * CAP), 1) < CAP
    for j in range(tiles):
        got = folded(lax.dot_general(sent, slot_ref[j], NT, preferred_element_type=F32))
        near, own = got[:, : 2 * CAP], got[:, 2 * CAP :]
        out_ref[j, 0:POINTS, :] = near[:POINTS]
        out_ref[j, 16:24, :] = jnp.where(left, own[0:8], own[8:16])
        out_ref[j, 24:26, :] = near[POINTS : POINTS + 2]
        out_ref[j, 26:27, :] = jnp.where(left_1, own[16:17], own[17:18])
        out_ref[j, 27:32, :] = jnp.zeros((5, 2 * CAP), F32)


def finish(*refs):
    solid, sea, refs = refs[:12], refs[12:16], refs[16:]
    state_out, out_ref, state_ref, sems, *scratch = refs
    back(*solid, state_ref, *scratch)
    copy = pltpu.make_async_copy(state_ref, state_out, sems.at[0])
    copy.start()
    basis = state_ref.shape[0] // FIELDS
    vertical = state_ref[vertical_field * basis : (vertical_field + 1) * basis, :]
    rates_out(vertical, *sea, out_ref)
    copy.wait()


def forced(place, got_ref, forcing_ref, s1_ref, s2_ref):
    tiles = got_ref.shape[0]
    tile_x = forcing_ref.shape[0]
    tile_y = forcing_ref.shape[1] - 128
    left8 = iota((8, 2 * CAP), 1) < CAP
    left1 = iota((1, 2 * CAP), 1) < CAP
    tops, bottoms, xs, ys = [], [], [], []
    for s in range(0, tiles, 2):
        one, two = got_ref[s, 16:24, :], got_ref[s + 1, 16:24, :]
        tops.append(jnp.where(left8, one, pltpu.roll(two, CAP, 1)))
        bottoms.append(jnp.where(left8, pltpu.roll(one, CAP, 1), two))
        one, two = got_ref[s, 24:32, :], got_ref[s + 1, 24:32, :]
        xs.append(jnp.where(left8, one, pltpu.roll(two, CAP, 1))[2:3])
        ys.append(jnp.where(left8, pltpu.roll(one, CAP, 1), two)[2:3])
    lower, upper = jnp.concatenate(tops, axis=1), jnp.concatenate(bottoms, axis=1)
    x0, y0 = jnp.concatenate(xs, axis=1), jnp.concatenate(ys, axis=1)
    arrived = x0.shape[1]
    hot = (iota((tile_x, arrived), 0).astype(F32) == x0).astype(F32).astype(BF16)
    from_y = iota((tile_y, arrived), 0).astype(F32) - y0
    stack = []
    for pr in range(patch_side):
        source = lower if pr < 2 else upper
        value = jnp.zeros((tile_y, arrived), F32)
        for pc in range(patch_side):
            at = (pr * patch_side + pc) % 8
            value = jnp.where(from_y == pc, source[at : at + 1], value)
        stack += parts(value)
    got = lax.dot_general(jnp.concatenate(stack, axis=0), hot, NT, preferred_element_type=F32)
    total = jnp.zeros((tile_y, tile_x), F32)
    for pr in range(patch_side):
        part = folded(got[2 * pr * tile_y : 2 * (pr + 1) * tile_y])
        total += part if pr == 0 else pltpu.roll(part, pr, 1)
    total = total.T
    forcing_ref[:, :tile_y] = total
    near = jnp.concatenate([got_ref[s, 0:POINTS, :] for s in range(tiles)], axis=1)
    x0 = jnp.concatenate([got_ref[s, 24:25, :] for s in range(tiles)], axis=1)
    y0 = jnp.concatenate([got_ref[s, 25:26, :] for s in range(tiles)], axis=1)
    arrived = x0.shape[1]
    hot = (iota((tile_x, arrived), 0).astype(F32) == x0).astype(F32).astype(BF16)
    rows = iota((8, arrived), 0)
    before = iota((8, arrived), 1) % (2 * CAP) < CAP
    high_y = jnp.where(before & (rows >= 6), (rows + (tile_y - 8)).astype(F32) - y0, -1.0)
    low_y = jnp.where(before | (rows >= 2), -1.0, rows.astype(F32) - y0)
    chunks = [None] * 16
    for pr in range(patch_side):
        high, low = jnp.zeros((8, arrived), F32), jnp.zeros((8, arrived), F32)
        for pc in range(patch_side):
            at = pr * patch_side + pc
            high = jnp.where(high_y == pc, near[at : at + 1], high)
            low = jnp.where(low_y == pc, near[at : at + 1], low)
        chunks[(4 * pr - 1) % 16], chunks[4 * pr] = high, low
    blank = jnp.zeros((8, arrived), F32)
    value = jnp.concatenate([blank if c is None else c for c in chunks], axis=0)
    got = folded(lax.dot_general(both_parts(value), hot, NT, preferred_element_type=F32))
    row = iota((128, tile_x), 0)
    used = (row < 2) | (row >= 126)
    total = jnp.where(used, got, 0.0)
    for pr in range(1, patch_side):
        moved_back = pltpu.roll(pltpu.roll(got, 128 - 32 * pr, 0), pr, 1)
        total += jnp.where(used, moved_back, 0.0)
    total = total.T
    forcing_ref[:, tile_y:] = total
    a1, _ = unequal(place)
    head, tail = forcing_ref[0:8, :], forcing_ref[tile_x - 8 : tile_x, :]
    tail = pltpu.roll(tail, 2, 0)
    s1_ref[...] = jnp.where(a1 > 0, tail, head)
    s2_ref[...] = jnp.where(a1 > 0, head, tail)


def edge_rows(place, heads, tails, p1_ref, p2_ref):
    a1, _ = unequal(place)
    for i in range(4):
        head, tail = heads[i, 0:2, :], tails[i, 6:8, :]
        one = jnp.where(a1 > 0, tail, head)
        two = jnp.where(a1 > 0, head, tail)
        for h in range(2):
            at = slice(3 * HALF + 4 * i + 2 * h, 3 * HALF + 4 * i + 2 * h + 2)
            lanes = slice(128 * h, 128 * (h + 1))
            p1_ref[at, :] = one[:, lanes]
            p2_ref[at, :] = two[:, lanes]


def edge_columns(place, depth_ref, momentum_ref, bottom_ref, one_ref, two_ref):
    arrays = [depth_ref[...], momentum_ref[0], momentum_ref[1], bottom_ref[...]]
    _, c1 = unequal(place)
    tile_y = depth_ref.shape[1]
    row = iota((8, tile_y), 0)
    up = jnp.where(row < 2, row + (tile_y - 2), row - 2)
    down = jnp.where(row < 2, row, row + (tile_y - 4))
    wanted = jnp.where(c1 > 0, up, down)
    hot = ((row < 4) & (wanted == iota((8, tile_y), 1))).astype(F32)
    for i, array in enumerate(arrays):
        columns = lax.dot_general(
            hot, array, NT, preferred_element_type=F32, precision=lax.Precision.HIGHEST
        )
        for h in range(2):
            at = slice(4 * i + 2 * h, 4 * i + 2 * h + 2)
            lanes = slice(128 * h, 128 * (h + 1))
            one_ref[at, :] = columns[0:2, lanes]
            two_ref[at, :] = columns[2:4, lanes]


def widened(place, depth_ref, momentum_ref, bottom_ref, p1_ref, p2_ref, q1_ref, q2_ref, out_ref):
    tile_x, tile_y = depth_ref.shape
    a1, c1 = unequal(place)
    arrays = [depth_ref[...], momentum_ref[0], momentum_ref[1], bottom_ref[...]]
    p1, p2 = p1_ref[3 * HALF :, :], p2_ref[3 * HALF :, :]
    q1, q2 = q1_ref[3 * HALF :, :], q2_ref[3 * HALF :, :]
    is_below, is_above = place[0] > 0, place[0] < place[2] - 1
    below = jnp.where(is_below, jnp.where(a1 > 0, p2, p1), 0.0)
    above = jnp.where(is_above, jnp.where(a1 > 0, p1, p2), 0.0)
    before = jnp.where(place[1] > 0, jnp.where(c1 > 0, q2, q1), 0.0)
    after = jnp.where(place[1] < place[3] - 1, jnp.where(c1 > 0, q1, q2), 0.0)
    n = OCEAN_ROWS

    def ends(rows):
        one, two = rows[n : n + 8], rows[n + 8 :]
        return (
            jnp.where(is_below, jnp.where(a1 > 0, two, one), 0.0),
            jnp.where(is_above, jnp.where(a1 > 0, one, two), 0.0),
        )

    before_below, before_above = ends(before)
    after_below, after_above = ends(after)
    lane = iota((2, 128), 1)
    low, high = lane < 2, lane >= 126
    for i, array in enumerate(arrays):
        first, second = slice(4 * i, 4 * i + 2), slice(4 * i + 2, 4 * i + 4)
        out_ref[i, 0:MARGIN, :] = jnp.zeros((MARGIN, tile_y + 128), F32)
        out_ref[i, MARGIN + tile_x :, :] = jnp.zeros((MARGIN, tile_y + 128), F32)
        out_ref[i, MARGIN : MARGIN + tile_x, :tile_y] = array
        for at, rows, left, right in (
            (MARGIN - 2, below, before_below, after_below),
            (MARGIN + tile_x, above, before_above, after_above),
        ):
            out_ref[i, at : at + 2, 0:128] = rows[first]
            out_ref[i, at : at + 2, 128:256] = rows[second]
            end = slice(2 * i, 2 * i + 2)
            corner = jnp.where(low, right[end], jnp.where(high, left[end], 0.0))
            out_ref[i, at : at + 2, 256:384] = corner
        start = jnp.concatenate([after[first], after[second]], axis=1)
        finish = jnp.concatenate([before[first], before[second]], axis=1)
        columns = jnp.concatenate([start, jnp.zeros((124, tile_x), F32), finish], axis=0)
        out_ref[i, MARGIN : MARGIN + tile_x, tile_y:] = columns.T


STRIP = 16


def next_of(x):
    return pltpu.roll(x, x.shape[1] - 1, 1)


def previous_of(x):
    return pltpu.roll(x, 1, 1)


def cells(state, cell, low, high):
    for at in range(low, high, 8):
        here = slice(at, at + 8)
        h, mx, my = state[0, here, :], state[1, here, :], state[2, here, :]
        safe = jnp.maximum(h, depth_floor)
        root = lax.rsqrt(safe)
        inverse = root * root
        c = safe * root
        u, v = mx * inverse, my * inverse
        half = 0.5 * h * h
        cell[0, here, :] = mx * u + half
        cell[1, here, :] = my * u
        cell[2, here, :] = my * v + half
        cell[3, here, :] = 0.5 * (jnp.abs(u) + c)
        cell[4, here, :] = 0.5 * (jnp.abs(v) + c)


def moved(state, cell, face, at, rows):
    here, up = slice(at, at + rows), slice(at + 1, at + rows + 1)
    below = slice(at - 1, at + rows - 1)
    now = [state[k, here, :] for k in range(3)]
    cross = cell[1, here, :]
    next_now = [state[k, up, :] for k in range(3)]
    wave = jnp.maximum(cell[3, here, :], cell[3, up, :])
    pairs = ((now[1], next_now[1]), (cell[0, here, :], cell[0, up, :]), (cross, cell[1, up, :]))
    upper = [
        0.5 * (pairs[k][0] + pairs[k][1]) - wave * (next_now[k] - now[k]) for k in range(3)
    ]
    for k in range(3):
        face[k, here, :] = upper[k]
    flux = (now[2], cross, cell[2, here, :])
    speed = cell[4, here, :]
    wave = jnp.maximum(speed, next_of(speed))
    next_now = [next_of(x) for x in now]
    next_flux = (next_now[2], next_of(flux[1]), next_of(flux[2]))
    y_face = [
        0.5 * (flux[k] + next_flux[k]) - wave * (next_now[k] - now[k]) for k in range(3)
    ]
    return [
        now[k] - step_ocean * (upper[k] - face[k, below, :] + y_face[k] - previous_of(y_face[k]))
        for k in range(3)
    ]


def sloped(height, bed, at, rows):
    b = bed[at : at + rows, :]
    slope_x = 0.5 * (bed[at + 1 : at + rows + 1, :] - bed[at - 1 : at + rows - 1, :])
    slope_y = 0.5 * (next_of(b) - previous_of(b))
    scale = step_ocean * height
    return scale * slope_x, scale * slope_y


def ocean_cells(
    place, depth_ref, momentum_ref, bottom_ref, p1_ref, p2_ref, q1_ref, q2_ref, wide, cell
):
    widened(place, depth_ref, momentum_ref, bottom_ref, p1_ref, p2_ref, q1_ref, q2_ref, wide)
    height, span = wide.shape[1:]
    cell[:, 0:8, :] = jnp.zeros((5, 8, span), F32)
    cell[:, height - 8 :, :] = jnp.zeros((5, 8, span), F32)
    cells(wide, cell, 8, height - 8)


def ocean_first(place, wide, cell, state, face):
    tile_x, tile_y = wide.shape[1] - 2 * MARGIN, wide.shape[2] - 128
    height, span = wide.shape[1:]
    lane = iota((STRIP, span), 1)
    outside = ((lane == span - 1) & (place[1] == 0)) | (
        (lane == tile_y) & (place[1] == place[3] - 1)
    )
    state[:, 0:8, :] = jnp.zeros((3, 8, span), F32)
    state[:, height - 8 :, :] = jnp.zeros((3, 8, span), F32)
    face[:, 0:8, :] = jnp.zeros((3, 8, span), F32)
    for at in range(8, height - 8, STRIP):
        new = moved(wide, cell, face, at, STRIP)
        row = iota((STRIP, span), 0) + at
        out = outside | ((row < MARGIN) & (place[0] == 0))
        out = out | ((row >= MARGIN + tile_x) & (place[0] == place[2] - 1))
        for k in range(3):
            state[k, at : at + STRIP, :] = jnp.where(out, 0.0, new[k])


def second_step(wide, first, bed, state, cell, face, rows, put, raise_bed):
    low, high = rows.start - 8, rows.stop + 8
    raise_bed(wide.at[3])
    for at in range(low, high, STRIP):
        here = slice(at, at + STRIP)
        change_x, change_y = sloped(wide[0, here, :], bed, at, STRIP)
        state[0, here, :] = first[0, here, :]
        state[1, here, :] = first[1, here, :] - change_x
        state[2, here, :] = first[2, here, :] - change_y
    cells(state, cell, low, high)
    raise_bed(bed)
    moved(state, cell, face, low, 8)
    for at in range(rows.start, rows.stop, STRIP):
        new = moved(state, cell, face, at, STRIP)
        change_x, change_y = sloped(state[0, at : at + STRIP, :], bed, at, STRIP)
        new[1] -= change_x
        new[2] -= change_y
        put(at, new)


def ocean_inner(wide, first, forcing_ref, out_ref, bed_ref, state, bed, cell, face):
    tile_x, tile_y = bed_ref.shape
    inner = slice(MARGIN, MARGIN + tile_x)
    bed[...] = wide[3]

    def raise_bed(source):
        bed[inner, :] = source[inner, :] + step_ocean * forcing_ref[...]

    def put(at, new):
        for k in range(3):
            out_ref[k, at - MARGIN : at - MARGIN + STRIP, :] = new[k][:, :tile_y]

    rows = slice(MARGIN + STRIP, MARGIN + tile_x - STRIP)
    second_step(wide, first, bed, state, cell, face, rows, put, raise_bed)
    bed_ref[...] = bed[inner, :tile_y]


def ocean_ends(
    place, wide, first, forcing_ref, s1_ref, s2_ref, inner_ref, raised_ref, out_hbm, bed_hbm,
    out_ref, bed_ref, sems, state, bed, cell, face,
):
    tile_x, tile_y = raised_ref.shape
    last = tile_x - STRIP
    middle = pl.ds(STRIP, tile_x - 2 * STRIP)
    copies = [
        pltpu.make_async_copy(raised_ref, bed_hbm, sems.at[0]),
        pltpu.make_async_copy(inner_ref.at[:, middle], out_hbm.at[:, middle], sems.at[1]),
    ]
    for copy in copies:
        copy.start()
    a1, _ = unequal(place)
    force_lo = step_ocean * jnp.where(a1 > 0, s2_ref[...], s1_ref[...])[0:2]
    force_lo = jnp.where(place[0] > 0, force_lo, 0.0)
    force_hi = step_ocean * jnp.where(a1 > 0, s1_ref[...], s2_ref[...])[0:2]
    force_hi = jnp.where(place[0] < place[2] - 1, force_hi, 0.0)

    def put(at, new):
        for k in range(3):
            out_ref[k, at - MARGIN : at - MARGIN + STRIP, :] = new[k][:, :tile_y]

    for n, start in enumerate((MARGIN, MARGIN + last)):
        outer = slice(start - 16, start) if n == 0 else slice(start + STRIP, start + STRIP + 16)
        edge = slice(MARGIN - 2, MARGIN) if n == 0 else slice(MARGIN + tile_x, MARGIN + tile_x + 2)
        force = force_lo if n == 0 else force_hi
        own = slice(start, start + 32) if n == 0 else slice(start - 16, start + 16)
        forcing = forcing_ref[own.start - MARGIN : own.stop - MARGIN, :]
        bed[outer, :] = wide[3, outer, :]

        def raise_bed(source):
            bed[own, :] = source[own, :] + step_ocean * forcing
            bed[edge, :] = source[edge, :] + force

        second_step(
            wide, first, bed, state, cell, face, slice(start, start + STRIP), put, raise_bed
        )
        at = pl.ds(start - MARGIN, STRIP)
        copies.append(pltpu.make_async_copy(out_ref.at[:, at], out_hbm.at[:, at], sems.at[2 + n]))
        copies[-1].start()
    for copy in copies:
        copy.wait()


def call(
    body, out_shape, *args, place=None, scratch=(), held=0, sent=0, copies=0, limit=VMEM_LIMIT
):
    out_space = [pltpu.HBM if i < sent else pltpu.VMEM for i in range(len(out_shape))]
    specs = [pl.BlockSpec(memory_space=pltpu.HBM if held else pltpu.VMEM) for _ in args]
    shapes = [
        s if isinstance(s, jax.ShapeDtypeStruct) else jax.ShapeDtypeStruct(s, F32) for s in out_shape
    ]
    scratch = [pltpu.VMEM(s, F32) for s in scratch]
    if copies:
        scratch = [pltpu.SemaphoreType.DMA((copies,))] + scratch
    scratch = [pltpu.VMEM(x.shape, x.dtype) for x in [*args[:held], *shapes[:sent]]] + scratch
    if place is not None:
        sizes, inner = place, body

        def body(*refs):
            here = (lax.axis_index("gx"), lax.axis_index("gy"))
            inner(here + sizes, *refs)

    return pl.pallas_call(
        body,
        out_shape=shapes,
        in_specs=specs,
        out_specs=[pl.BlockSpec(memory_space=space) for space in out_space],
        scratch_shapes=scratch,
        compiler_params=pltpu.CompilerParams(vmem_limit_bytes=limit),
    )(*args)


def swap(block, axis, parity, wrap=False):
    count = lax.axis_size(axis)
    last = count + parity - 1 if wrap else count - 1
    pairs = []
    for i in range(parity, last, 2):
        pairs += [(i, (i + 1) % count), ((i + 1) % count, i)]
    taken = {source for source, _ in pairs}
    pairs += [(i, i) for i in range(count) if i not in taken]
    return lax.ppermute(block, axis, pairs)


def per_device(
    coefficients,
    jacobian,
    face_normals,
    wave_speed,
    star_mats,
    deriv_mats,
    stiff_mats,
    source_mat,
    trace_mats,
    lift_mats,
    face_partner,
    send_faces,
    sea_face,
    sea_row,
    sea_base,
    interp_mat,
    water_depth,
    momentum,
    bottom,
):
    basis, elements = coefficients.shape[1:]
    rows = FIELDS * basis
    tile_x, tile_y = water_depth.shape
    tiles = lax.axis_size("gy")
    place = (lax.axis_size("gx"), tiles)
    speed = wave_speed.reshape(1, elements)
    traces = trace_mats.transpose(1, 0, 2)
    normals = face_normals.transpose(1, 0, 2)
    lifts = lift_mats.transpose(2, 0, 1)
    spread = (FIELDS, 3 * basis, elements)
    faces = (TABLE, 4 * elements)
    solid = (rows, elements)
    wide_shape = (tile_x + 2 * MARGIN, tile_y + 128)
    state = coefficients.reshape(solid)
    packed = (2 * HALF, 8 * CAP)
    flux_shape = (FIELDS, 4 * FACE_PAD, elements)
    for section in range(2):
        scratch = [spread, solid, solid, solid, (2 * HALF, 4 * CAP)]
        if section == 0:
            fixed = (state, jacobian, star_mats, source_mat, deriv_mats, traces, send_faces)
            buffers = [(3 * HALF + OCEAN_ROWS, 128)] * 2 + [(HALF, 128)] * 2
            integral, table, p1, p2, own1, own2 = call(
                start, [solid, faces] + buffers, *fixed, water_depth, momentum, bottom,
                place=place, scratch=[(4, 8, tile_y)] * 2 + scratch,
                held=len(fixed), sent=6, copies=len(fixed) + 14, limit=START_LIMIT,
            )
        else:
            buffers = [(3 * HALF, 128)] * 2 + [(HALF, 128)] * 2
            integral, table, p1, p2, own1, own2 = call(
                front_again, [solid, faces] + buffers,
                state, jacobian, star4, *derivs, *traced, send_faces, place=place, scratch=scratch,
            )
        p2, p1 = swap(p2, "gx", 1), swap(p1, "gx", 0)
        inside = (state, jacobian, star_mats, stiff_mats, integral)
        (base,) = call(volume, [solid], *inside, scratch=[spread])
        if section == 0:
            columns = call(
                edge_columns, [(OCEAN_ROWS, 128)] * 2, water_depth, momentum, bottom, place=place
            )
            size = 3 * HALF + 2 * OCEAN_ROWS
        else:
            columns, size = [], 3 * HALF
            wide, cell = call(
                ocean_cells,
                [(4,) + wide_shape, (5,) + wide_shape],
                water_depth, momentum, bottom, *halos,
                place=place,
            )
            base, wide, cell = lax.optimization_barrier((base, wide, cell))
        p1, p2, base = lax.optimization_barrier((p1, p2, base))
        q1, q2 = call(forward, [(size, 128)] * 2, p1, p2, own1, own2, *columns, place=place)
        q2, q1 = swap(q2, "gy", 1), swap(q1, "gy", 0)
        if section == 1:
            (flux,) = call(
                local_flux, [flux_shape], table, face_partner, normals, speed, star3,
                scratch=[faces],
            )
            (first,) = call(
                ocean_first,
                [(3,) + wide_shape],
                wide, cell,
                place=place, scratch=[(3,) + wide_shape],
            )
            q1, q2, flux, first = lax.optimization_barrier((q1, q2, flux, first))
        else:
            half = lambda *shape: jax.ShapeDtypeStruct(shape, BF16)
            size, sea = FIELDS * 8, sea_face.shape[0]
            star4, star3, *ready = call(
                prepared,
                [half(16 * (FIELDS + FIELDS % 2), 12 * (FIELDS + FIELDS % 2)), half(6 * size, 2 * size)]
                + [half(2 * basis, 3 * basis), half(basis, 3 * basis)]
                + [half(4 * FACE_PAD, 3 * basis)]
                + [half(2 * basis, 4 * FACE_PAD), half(basis, 4 * FACE_PAD)]
                + [half(8 * CAP, 4 * elements), half(4 * elements, sea), half(tiles, 4 * CAP, sea), (8, 8 * CAP)]
                + [half(4 * POINTS, 3 * basis)],
                star_mats, source_mat, deriv_mats, traces, lifts, face_partner,
                sea_face.reshape(1, -1), sea_row.T, normals, speed, interp_mat,
                place=place,
            )
            (flux,) = call(
                local_flux, [flux_shape], table, face_partner, normals, speed, star3,
                scratch=[faces],
            )
            q1, q2, flux, *ready = lax.optimization_barrier((q1, q2, flux, *ready))
            derivs, traced, lifting, (hot, sea_hot, slot_hot, scales, uplift) = (
                ready[0:2], ready[2:3], ready[3:5], ready[5:],
            )
        fixed = (star3, *lifting, hot, scales)
        arrived = (p1, p2, q1, q2)
        remote = (TABLE, 8 * CAP)
        if section == 0:
            (state,) = call(
                back, [solid], base, flux, *fixed, *arrived,
                place=place, scratch=[flux_shape, packed, remote],
            )
            halos = (p1, p2, q1, q2)
        else:
            state, outgoing = call(
                finish,
                [solid, (tiles, 32, 128)],
                base, flux, *fixed, *arrived,
                uplift, sea_base.T, sea_hot, slot_hot,
                place=place, scratch=[flux_shape, packed, remote], sent=1, copies=1,
            )
    incoming = lax.all_to_all(outgoing, "gy", split_axis=0, concat_axis=0, tiled=True)
    forcing, s1, s2 = call(
        forced,
        [(tile_x, tile_y + 128), (8, tile_y + 128), (8, tile_y + 128)],
        incoming,
        place=place,
    )
    s2, s1 = swap(s2, "gx", 1, wrap=True), swap(s1, "gx", 0)
    scratch = [(3,) + wide_shape, wide_shape, (5,) + wide_shape, (3,) + wide_shape]
    water = [(3, tile_x, tile_y), (tile_x, tile_y)]
    inner, raised = call(ocean_inner, water, wide, first, forcing, scratch=scratch)
    ocean_final, bed_final = call(
        ocean_ends, water, wide, first, forcing, s1, s2, inner, raised,
        place=place, scratch=scratch, sent=2, copies=4,
    )
    return (state.reshape(coefficients.shape), ocean_final, bed_final)


def solution(mesh):
    in_specs = (
        P(None, None, ("gx", "gy")),
        P(None, None, ("gx", "gy")),
        P(None, None, ("gx", "gy")),
        P(("gx", "gy")),
        P(),
        P(),
        P(),
        P(),
        P(),
        P(),
        P(None, ("gx", "gy")),
        P(None, ("gx", "gy")),
        P(("gx", "gy")),
        P(("gx", "gy"), None),
        P(("gx", "gy"), None),
        P(),
        P("gx", "gy"),
        P(None, "gx", "gy"),
        P("gx", "gy"),
    )
    out_specs = (P(None, None, ("gx", "gy")), P(None, "gx", "gy"), P("gx", "gy"))
    return jax.shard_map(
        per_device, mesh=mesh, in_specs=in_specs, out_specs=out_specs, check_vma=False
    )
```
